32 devices in a mesh: chan: 8 (over y, x, core), freq: 4 (over z).
Axes of the slice: x: 2, y: 2, z: 4, core: 2. Of those that a mesh axis runs over, the one named last changes fastest.
Arguments:
- spectra: bfloat16 [2, 30, 1024, 1024], P(None, None, 'freq', 'chan'), may hold values from -6 to 6
- src_ids: int32 [2, 32], replicated, may hold values from 0 to 1023
- pair_bin: int32 [2, 32, 1024], P(None, None, 'chan'), may hold values from 0 to 255, as said below
- slot_of_bin: int32 [256], replicated, may hold values from 0 to 255, each once
Outputs:
- offset_gather: float32 [256, 256], P('chan')
The draws below stay inside these ranges and needn't reach their ends.
Inputs may be any that keep to these rules, and one draw needn't show every extreme that they name: slot_of_bin names every row of offset_gather once. `pair_bin`: some offset bins are named by no pair.
All inputs are finite; a program needn't handle non-finite values.
Results may differ from the reference program's by a relative error of at most 0.0003.
Values may be sent and summed in bfloat16 or wider, within the bound.
No kernel may reach another device: no remote copies, remote signals or barrier semaphores. Data moves between devices by JAX's collectives and lax.ppermute only.
A program may use at most 64 MiB of HBM per device.

```python
import math
import jax
import jax.numpy as jnp
from jax import lax

F = 1024
NLAG = 256
W = 30
NSRC = 32
STEPS = 2
CH = 1024
NBIN = 256


def draw_pair_bin(key, part):
    empty_count = NBIN // 8
    used_count = NBIN - empty_count
    key_perm = jax.random.fold_in(key, 11)
    key_order = jax.random.fold_in(key, 12)
    key_coin = jax.random.fold_in(key, 13)
    key_outer = jax.random.fold_in(key, 14)
    key_inner = jax.random.fold_in(key, 15)
    key_flat = jax.random.fold_in(key, 16)
    inner_ids = (jax.random.permutation(key_perm, NBIN - 2) + 1).astype(jnp.int32)
    ends = jnp.array([0, NBIN - 1], jnp.int32)
    used_set = jnp.concatenate([ends, inner_ids[empty_count:]])
    used_ids = jax.random.permutation(key_order, used_set).astype(jnp.int32)
    shape = (STEPS, NSRC, CH)
    coin = jax.random.randint(key_coin, shape, 0, 2).astype(jnp.int32)
    outer = jax.random.randint(key_outer, shape, 1, used_count + 1).astype(jnp.int32)
    nested = jax.random.randint(key_inner, shape, 0, outer).astype(jnp.int32)
    flat_rank = jax.random.randint(key_flat, shape, 0, used_count).astype(jnp.int32)
    rank = jnp.where(coin == 0, nested, flat_rank)
    chosen = used_ids[rank].reshape(-1)
    chosen = chosen.at[0].set(NBIN - 1).at[1].set(0)
    return chosen.reshape(shape).astype(jnp.int32)


def set_ends(values, own_key, low, largest):
    shape = values.shape
    index_at = [jax.random.randint(jax.random.fold_in(own_key, axis), (), 0, shape[axis]) for axis in range(len(shape))]
    values = values.at[tuple(index_at)].set(low)
    longest = shape.index(max(shape))
    index_at[longest] = (index_at[longest] + 1) % shape[longest]
    return values.at[tuple(index_at)].set(largest)


def steps_of(stream_key, extent, cuts, low, top_value):
    factor_of, own = 1.0, jax.random.fold_in(stream_key, 6)
    for axis_at, parts in cuts:
        heights = jnp.exp(jax.random.uniform(jax.random.fold_in(own, axis_at), (parts,), jnp.float32, low / len(cuts), top_value / len(cuts)))
        factor_of = factor_of * jnp.repeat(heights, extent[axis_at] // parts).reshape([-1 if axis == axis_at else 1 for axis in range(len(extent))])
    return factor_of


def bell_draw(stream_key, extent, scale, limit, shards=(), kind=jnp.bfloat16):
    drawn = scale * jax.random.normal(stream_key, extent, jnp.float32)
    if shards:
        drawn = drawn * steps_of(stream_key, extent, shards, -0.22, 0.18)
    return jnp.clip(drawn, -limit, limit).astype(kind)


def setup_inputs(seed: int = 0) -> dict:
    arg_keys = jax.random.split(jax.random.key(seed), 5)
    spectra = bell_draw(arg_keys[0], (2, W, F, CH), 1.0, 6.0, ((2, 4), (3, 8)))
    src_ids = set_ends(jax.random.randint(arg_keys[1], (STEPS, NSRC), 0, CH), jax.random.fold_in(arg_keys[1], 1), 0, CH - 1).astype(jnp.int32)
    pair_bin = draw_pair_bin(jax.random.fold_in(arg_keys[4], 71), 0)
    slot_of_bin = jax.random.permutation(arg_keys[3], NBIN).astype(jnp.int32)
    return {"spectra": spectra, "src_ids": src_ids, "pair_bin": pair_bin, "slot_of_bin": slot_of_bin}


def lag_basis(anchor, amount, totals, lag_count, windows):
    frequency = anchor + lax.iota(jnp.int32, amount)
    shifts = lax.iota(jnp.int32, lag_count) - lag_count // 2
    phases = frequency[:, None] * shifts[None, :] % (2 * totals)
    angles = phases.astype(jnp.float32) * (math.pi / totals)
    factor = 1.0 / math.sqrt(windows * totals)
    return jnp.concatenate([jnp.cos(angles), -jnp.sin(angles)], axis=0) * factor

def reference(spectra, src_ids, pair_bin, slot_of_bin):
    span_f = min(F, 64)
    blocks = F // span_f
    lag_table = lag_basis(0, F, F, NLAG, W)
    binned = jnp.zeros((NBIN, 2 * F), jnp.float32)
    counts = jnp.zeros((NBIN,), jnp.float32)
    for step_no in range(STEPS):
        bin_ids = pair_bin[step_no].reshape(-1).astype(jnp.int32)
        source = spectra[:, :, :, src_ids[step_no]]

        def one_block(block_no):
            anchor = (block_no * span_f).astype(jnp.int32)
            receiver = lax.dynamic_slice_in_dim(spectra, anchor, span_f, 2).astype(jnp.float32)
            source_blk = lax.dynamic_slice_in_dim(source, anchor, span_f, 2).astype(jnp.float32)
            flipped = jnp.stack([-source_blk[1], source_blk[0]])
            stacked = jnp.stack([source_blk, flipped])
            crossed = jnp.einsum('jkwfs,kwfc->scjf', stacked, receiver)
            return jax.ops.segment_sum(crossed.reshape(NSRC * CH, 2 * span_f), bin_ids, num_segments=NBIN)
        pieces = lax.map(one_block, jnp.arange(blocks, dtype=jnp.int32))
        pieces = pieces.reshape(blocks, NBIN, 2, span_f).transpose(1, 2, 0, 3).reshape(NBIN, 2 * F)
        binned = binned + pieces
        counts = counts + jax.ops.segment_sum(jnp.ones((NSRC * CH,), jnp.float32), bin_ids, num_segments=NBIN)
    stacks = jnp.dot(binned, lag_table, precision=lax.Precision.HIGHEST)
    scaled = stacks / jnp.sqrt(jnp.maximum(counts, 1.0))[:, None]
    return jnp.zeros((NBIN, NLAG), jnp.float32).at[slot_of_bin].set(scaled)
```

```python
import functools
import math

import jax
import jax.numpy as jnp
from jax import lax
from jax.experimental import pallas as pl
from jax.experimental.pallas import tpu as pltpu
from jax.sharding import PartitionSpec as P

F = 1024
NLAG = 256
BF = jnp.bfloat16
F32 = jnp.float32
FBLK = 16
SBLK = 8
WPAD = 32
LIMIT = 56 * 1024 * 1024


def lag_basis(anchor, amount, totals, lag_count, windows):
    frequency = anchor + lax.iota(jnp.int32, amount)
    shifts = lax.iota(jnp.int32, lag_count) - lag_count // 2
    phases = frequency[:, None] * shifts[None, :] % (2 * totals)
    angles = phases.astype(F32) * (math.pi / totals)
    factor = 1.0 / math.sqrt(windows * totals)
    return jnp.concatenate([jnp.cos(angles), -jnp.sin(angles)], axis=0) * factor


def pick_kernel(core_ref, rel_ref, spec_ref, keep_ref, send_ref, spec_send_ref):
    wins, half = keep_ref.shape[0], keep_ref.shape[1]
    chans = spec_ref.shape[3]
    lanes = rel_ref.shape[1]
    core = core_ref[0]
    row = lax.broadcasted_iota(jnp.int32, (2 * chans, lanes), 0)
    col = lax.broadcasted_iota(jnp.int32, (2 * chans, lanes), 1)
    wanted = rel_ref[...] + jnp.where(col >= lanes // 2, chans, 0)
    inside = (rel_ref[...] >= 0) & (rel_ref[...] < chans)
    picker = jnp.where((row == wanted) & inside, 1.0, 0.0).astype(BF)
    mine = pl.ds(pl.multiple_of(core * half, half), half)
    other = pl.ds(pl.multiple_of((1 - core) * half, half), half)
    for w in range(wins):
        both = jnp.concatenate([spec_ref[0, w, mine, :], spec_ref[1, w, mine, :]], axis=1)
        keep_ref[w] = jnp.dot(both, picker, preferred_element_type=F32).astype(BF)
        real, imag = spec_ref[0, w, other, :], spec_ref[1, w, other, :]
        spec_send_ref[0, w] = real
        spec_send_ref[1, w] = imag
        both = jnp.concatenate([real, imag], axis=1)
        send_ref[w] = jnp.dot(both, picker, preferred_element_type=F32).astype(BF)


def pick(spectra, src_all, me, core):
    _, windows, freqs, chans = spectra.shape
    half = freqs // 2
    slots = src_all.shape[0]
    rel = src_all - me * chans
    rel = jnp.concatenate([rel, rel])[None, :]
    wb = 6 if windows % 6 == 0 else 1
    out = jax.ShapeDtypeStruct((windows, half, 2 * slots), BF)
    return pl.pallas_call(
        pick_kernel,
        grid_spec=pltpu.PrefetchScalarGridSpec(
            num_scalar_prefetch=1,
            grid=(windows // wb,),
            in_specs=[
                pl.BlockSpec((1, 2 * slots), lambda i, c: (0, 0)),
                pl.BlockSpec((2, wb, freqs, chans), lambda i, c: (0, i, 0, 0)),
            ],
            out_specs=[
                pl.BlockSpec((wb, half, 2 * slots), lambda i, c: (i, 0, 0)),
                pl.BlockSpec((wb, half, 2 * slots), lambda i, c: (i, 0, 0)),
                pl.BlockSpec((2, wb, half, chans), lambda i, c: (0, i, 0, 0)),
            ],
        ),
        out_shape=[out, out, jax.ShapeDtypeStruct((2, windows, half, chans), BF)],
        compiler_params=pltpu.CompilerParams(vmem_limit_bytes=LIMIT),
        name="pick_sources",
    )(core.reshape(1), rel, spectra)


def prep_kernel(core_ref, own_ref, got_ref, out_ref, scr):
    windows, fb, chans = own_ref.shape[1:]
    for k in range(2):
        base = k * WPAD * fb
        for half, ref in enumerate((own_ref, got_ref)):
            scr[half, pl.ds(base, windows * fb), :] = ref[k].astype(F32).reshape(windows * fb, chans)
            scr[half, pl.ds(base + windows * fb, (WPAD - windows) * fb), :] = jnp.zeros(((WPAD - windows) * fb, chans), F32)
    for f in range(fb):
        for half in range(2):
            rows = scr[half, pl.ds(f, 2 * WPAD, stride=fb), :]
            out_ref[f, :, pl.ds(half * chans, chans)] = rows.astype(BF)


def prep(spectra, got, core):
    _, windows, freqs, chans = spectra.shape
    half = freqs // 2
    steps = half // FBLK
    return pl.pallas_call(
        prep_kernel,
        grid_spec=pltpu.PrefetchScalarGridSpec(
            num_scalar_prefetch=1,
            grid=(steps,),
            in_specs=[
                pl.BlockSpec((2, windows, FBLK, chans), lambda i, c: (0, 0, c[0] * steps + i, 0)),
                pl.BlockSpec((2, windows, FBLK, chans), lambda i, c: (0, 0, i, 0)),
            ],
            out_specs=pl.BlockSpec((FBLK, 2 * WPAD, 2 * chans), lambda i, c: (i, 0, 0)),
            scratch_shapes=[pltpu.VMEM((2, 2 * WPAD * FBLK, chans), F32)],
        ),
        out_shape=jax.ShapeDtypeStruct((half, 2 * WPAD, 2 * chans), BF),
        compiler_params=pltpu.CompilerParams(vmem_limit_bytes=LIMIT),
        name="frequency_major",
    )(core.reshape(1), spectra, got)


def onehot_kernel(pairs_ref, row_bin_ref, out_ref, count_ref):
    chans2 = out_ref.shape[1]

    @pl.when(pl.program_id(0) == 0)
    def _():
        count_ref[...] = jnp.zeros_like(count_ref)

    total = jnp.zeros(count_ref.shape, F32)
    for s in range(out_ref.shape[0]):
        hit = jnp.where(pairs_ref[0, :, s : s + 1] == row_bin_ref[...], 1.0, 0.0)
        out_ref[s] = hit.astype(BF)
        total = total + jnp.sum(hit[: chans2 // 2], axis=0, keepdims=True)
    count_ref[...] += total


def onehot(pairs, row_bin):
    slots, chans2 = pairs.shape
    bins = row_bin.shape[0]
    grouped = pairs.reshape(slots // SBLK, SBLK, chans2).transpose(0, 2, 1)
    return pl.pallas_call(
        onehot_kernel,
        grid=(slots // SBLK,),
        in_specs=[
            pl.BlockSpec((1, chans2, SBLK), lambda i: (i, 0, 0)),
            pl.BlockSpec((1, bins), lambda i: (0, 0)),
        ],
        out_specs=[
            pl.BlockSpec((SBLK, chans2, bins), lambda i: (i, 0, 0)),
            pl.BlockSpec((1, bins), lambda i: (0, 0)),
        ],
        out_shape=[
            jax.ShapeDtypeStruct((slots, chans2, bins), BF),
            jax.ShapeDtypeStruct((1, bins), F32),
        ],
        compiler_params=pltpu.CompilerParams(vmem_limit_bytes=LIMIT),
        name="bin_onehot",
    )(grouped, row_bin[None, :])


def stack_kernel(nf, ns, xa_ref, xb_ref, ya_ref, yb_ref, recv_ref, hot_ref, table_ref, out_ref, xs, cross, acc):
    step = pl.program_id(0)
    windows, fb, lanes = xa_ref.shape
    slots = lanes // 2
    half = cross.shape[1] // lanes
    chans = cross.shape[2]
    tails = (WPAD - windows) * fb

    def crossing(a_ref, b_ref):
        both = a_ref[...].astype(F32) + b_ref[...].astype(F32)
        xs[pl.ds(0, windows * fb), :] = both.reshape(windows * fb, lanes)
        xs[pl.ds(windows * fb, tails), :] = jnp.zeros((tails, lanes), F32)
        imag = lax.broadcasted_iota(jnp.int32, (WPAD, lanes), 1) >= slots
        for f in range(fb):
            x = xs[pl.ds(f, WPAD, stride=fb), :]
            left = jnp.concatenate([jnp.where(imag, -x, x), pltpu.roll(x, slots, 1)], axis=0).astype(BF)
            got = lax.dot_general(left, recv_ref[f], (((0,), (0,)), ((), ())), preferred_element_type=F32)
            at = pl.ds(pl.multiple_of((step * fb + f) * lanes, lanes), lanes)
            cross[0, at, :] = got[:, :chans]
            cross[1, at, :] = got[:, chans:]

    @pl.when(step < nf // 2)
    def _():
        crossing(xa_ref, xb_ref)

    @pl.when((step >= nf // 2) & (step < nf))
    def _():
        crossing(ya_ref, yb_ref)

    @pl.when(step == nf)
    def _():
        acc[...] = jnp.zeros_like(acc)

    @pl.when(step >= nf)
    def _():
        total = acc[...]
        for s in range(SBLK):
            slot = (step - nf) * SBLK + s
            parts = []
            for turn in range(2):
                at = pl.ds(slot + turn * slots, half, stride=lanes)
                parts.append(jnp.concatenate([cross[0, at, :], cross[1, at, :]], axis=1))
            x = jnp.concatenate(parts, axis=0)
            high = x.astype(BF)
            low = (x - high.astype(F32)).astype(BF)
            total = total + jnp.dot(high, hot_ref[s], preferred_element_type=F32)
            total = total + jnp.dot(low, hot_ref[s], preferred_element_type=F32)
        acc[...] = total

    @pl.when(step == nf + ns - 1)
    def _():
        out_ref[...] = lax.dot_general(
            acc[...], table_ref[...], (((0,), (0,)), ((), ())), precision=lax.Precision.HIGHEST, preferred_element_type=F32
        )


def stack(routes, recv, hot, table):
    (xa, xb), (ya, yb) = routes
    windows, quarter, lanes = xa.shape
    half, _, chans2 = recv.shape
    slots, _, bins = hot.shape
    lags = table.shape[1]
    nf, ns = half // FBLK, slots // SBLK
    first = pl.BlockSpec((windows, FBLK, lanes), lambda i: (0, jnp.minimum(i, nf // 2 - 1), 0))
    second = pl.BlockSpec((windows, FBLK, lanes), lambda i: (0, jnp.clip(i - nf // 2, 0, nf // 2 - 1), 0))
    return pl.pallas_call(
        functools.partial(stack_kernel, nf, ns),
        grid=(nf + ns,),
        in_specs=[
            first,
            first,
            second,
            second,
            pl.BlockSpec((FBLK, 2 * WPAD, chans2), lambda i: (jnp.minimum(i, nf - 1), 0, 0)),
            pl.BlockSpec((SBLK, chans2, bins), lambda i: (jnp.maximum(i - nf, 0), 0, 0)),
            pl.BlockSpec((2 * half, lags), lambda i: (0, 0)),
        ],
        out_specs=pl.BlockSpec((bins, lags), lambda i: (0, 0)),
        out_shape=jax.ShapeDtypeStruct((bins, lags), F32),
        scratch_shapes=[
            pltpu.VMEM((WPAD * FBLK, lanes), F32),
            pltpu.VMEM((2, half * lanes, chans2 // 2), F32),
            pltpu.VMEM((2 * half, bins), F32),
        ],
        compiler_params=pltpu.CompilerParams(vmem_limit_bytes=LIMIT),
        name="cross_and_bin",
    )(xa, xb, ya, yb, recv, hot, table)


def swap(x, size, bit):
    return lax.ppermute(x, "chan", [(i, i ^ bit) for i in range(size)])


def body(nchan, nfreq, spectra, src_ids, pair_bin, slot_of_bin):
    _, windows, freqs, chans = spectra.shape
    half = freqs // 2
    bins = slot_of_bin.shape[0]
    slots = src_ids.shape[0] * src_ids.shape[1]
    me = lax.axis_index("chan")
    core = me & 1
    rest = [1 << k for k in range(1, nchan.bit_length() - 1)]

    keep, send, spec_send = pick(spectra, src_ids.reshape(-1), me, core)
    pairs_own = pair_bin.reshape(slots, chans)
    chip = keep + swap(send, nchan, 1)
    quarter = half // 2
    routes = []
    pieces = [chip[:, :quarter], chip[:, quarter:]]
    orders = [rest, rest[::-1]]
    for hop in range(len(rest)):
        gots = [swap(pieces[r], nchan, orders[r][hop]) for r in range(2)]
        if hop == len(rest) - 1:
            routes = [(pieces[r], gots[r]) for r in range(2)]
        else:
            pieces = [pieces[r] + gots[r] for r in range(2)]

    got_spec = swap(spec_send, nchan, 1)
    got_pairs = swap(pairs_own, nchan, 1)
    recv = prep(spectra, got_spec, core)

    per = bins // nchan
    order = jnp.arange(bins, dtype=jnp.int32).reshape(nchan // 2, 2, per).transpose(1, 0, 2).reshape(-1)
    named = slot_of_bin[None, :] == order[:, None]
    row_bin = jnp.sum(jnp.where(named, lax.iota(jnp.int32, bins)[None, :], 0), axis=1)
    hot, counts = onehot(jnp.concatenate([pairs_own, got_pairs], axis=1), row_bin)

    anchor = lax.axis_index("freq") * freqs + core * half
    table = lag_basis(anchor, half, F, NLAG, windows)
    lagged = stack(routes, recv, hot, table)

    blocks = lagged.reshape(nchan, per, NLAG)
    counted = jnp.zeros((nchan, 8, NLAG), F32).at[:, 0, :per].set(counts.reshape(nchan, per))
    payload = jnp.concatenate([blocks, counted], axis=1).reshape(2, nchan // 2, per + 8, NLAG)
    mine = jnp.where(core == 0, payload[0], payload[1])
    other = jnp.where(core == 0, payload[1], payload[0])
    mine = mine + swap(other, nchan, 1)
    at = me // 2
    if nchan // 2 <= 4:
        total = lax.dynamic_index_in_dim(mine, at, 0, keepdims=False)
        for move in range(1, nchan // 2):
            total = total + swap(lax.dynamic_index_in_dim(mine, at ^ move, 0, keepdims=False), nchan, 2 * move)
    else:
        for bit in rest[::-1]:
            size = mine.shape[0] // 2
            up = (me & bit) != 0
            low, high = mine[:size], mine[size:]
            mine = jnp.where(up, high, low) + swap(jnp.where(up, low, high), nchan, bit)
        total = mine[0]
    if nfreq <= 4:
        parts = [lax.ppermute(total, "freq", [(i, (i + k) % nfreq) for i in range(nfreq)]) for k in range(1, nfreq)]
        for part in parts:
            total = total + part
    else:
        for k in range(nfreq.bit_length() - 1):
            total = total + lax.ppermute(total, "freq", [(i, i ^ (1 << k)) for i in range(nfreq)])
    count = total[per, :per] * (1.0 / nfreq)
    return total[:per] / jnp.sqrt(jnp.maximum(count, 1.0))[:, None]


def solution(mesh):
    return jax.shard_map(
        functools.partial(body, mesh.shape["chan"], mesh.shape["freq"]),
        mesh=mesh,
        in_specs=(P(None, None, "freq", "chan"), P(), P(None, None, "chan"), P()),
        out_specs=P("chan", None),
        check_vma=False,
    )
```

```python
import functools
import math

import jax
import jax.numpy as jnp
from jax import lax
from jax.experimental import pallas as pl
from jax.experimental.pallas import tpu as pltpu
from jax.sharding import PartitionSpec as P

F = 1024
NLAG = 256
BF = jnp.bfloat16
F32 = jnp.float32
I32 = jnp.int32
FB = 16
WROWS = 16
LANES = 128
LIMIT = 60 * 1024 * 1024
PITCH = LANES + 9
PARAMS = pltpu.CompilerParams(vmem_limit_bytes=LIMIT)
ANY = pl.BlockSpec(memory_space=pl.ANY)
VMEM = pl.BlockSpec(memory_space=pltpu.VMEM)


def lag_basis(anchor, amount, totals, lag_count, windows):
    frequency = anchor + lax.iota(I32, amount)
    shifts = lax.iota(I32, lag_count) - lag_count // 2
    phases = frequency[:, None] * shifts[None, :] % (2 * totals)
    angles = phases.astype(F32) * (math.pi / totals)
    factor = 1.0 / math.sqrt(windows * totals)
    return jnp.cos(angles) * factor, -jnp.sin(angles) * factor


def iota(shape, dim):
    return lax.broadcasted_iota(I32, shape, dim)


def shift(values, size):
    return lax.shift_right_logical(values, jnp.int32(size.bit_length() - 1))


def as_column(row):
    size = row.shape[1]
    eye = iota((size, size), 0) == iota((size, size), 1)
    return jnp.sum(jnp.where(eye, row, 0), axis=1, keepdims=True)


def source_row(src_ref):
    return jnp.concatenate([src_ref[t : t + 1, :] for t in range(src_ref.shape[0])], axis=1)


def chip_ranks(row, per_chip):
    size = row.shape[1]
    own_row = shift(row, per_chip)
    col = as_column(row)
    own_col = shift(col, per_chip)
    same = own_col == own_row
    q0, q1 = iota((size, size), 0), iota((size, size), 1)
    rank_col = jnp.sum(jnp.where(same & (q1 < q0), 1, 0), axis=1, keepdims=True)
    rank_row = jnp.sum(jnp.where(same & (q0 < q1), 1, 0), axis=0, keepdims=True)
    return col, own_col, rank_col, own_row, rank_row


def frequency_first(rows):
    shape = (FB * WROWS, rows * FB)
    r, c = iota(shape, 0), iota(shape, 1)
    hit = (shift(r, WROWS) == (c & (FB - 1))) & ((r & (WROWS - 1)) == shift(c, FB))
    return jnp.where(hit, 1.0, 0.0).astype(BF)


def pick_kernel(cap, pieces, src_ref, spec_ref, keep_ref, send_ref, spec_send_ref, buf, keep_buf, send_buf, in_sem, out_sem):
    _, windows, freqs, chans = spec_ref.shape
    wp = windows // 2
    half = freqs // 2
    part = half // pieces
    me = lax.axis_index("chan")
    core = me & 1
    chunks = 5 if wp % 5 == 0 else 1
    wc = wp // chunks
    ins = []
    for j in range(chunks):
        for k in range(2):
            for w2 in range(2):
                at = pl.ds(w2 * wp + j * wc, wc)
                ins.append(pltpu.make_async_copy(spec_ref.at[k, at], buf.at[k, at], in_sem.at[j, 2 * k + w2]))
    for copy in ins:
        copy.start()

    row = source_row(src_ref)
    col, own_col, rank_col, _, _ = chip_ranks(row, 2 * chans)
    slots = row.shape[1]
    lane_r = iota((slots, LANES), 1) & (cap - 1)
    match = (own_col == shift(me, 2)) & (rank_col == lane_r)
    local = col - me * chans
    found = jnp.sum(jnp.where(match, local + 1, 0), axis=0, keepdims=True) - 1
    groups = LANES // cap
    shape = (groups * chans, LANES)
    r, c = iota(shape, 0), iota(shape, 1)
    hit = (shift(r, chans) == shift(c, cap)) & ((r & (chans - 1)) == found)
    picker = jnp.where(hit, 1.0, 0.0).astype(BF)

    mine = pl.multiple_of(core * half, half)
    other = pl.multiple_of((1 - core) * half, half)
    outs = []
    for j in range(chunks):
        for copy in ins[4 * j : 4 * j + 4]:
            copy.wait()
        for k in range(2):
            for w2 in range(2):
                at = pl.ds(w2 * wp + j * wc, wc)
                outs.append(
                    pltpu.make_async_copy(buf.at[k, at, pl.ds(other, half)], spec_send_ref.at[k, at], out_sem.at[j, 2 * k + w2])
                )
                outs[-1].start()
        for i in range(wc):
            w = j * wc + i
            for start, dest in ((other, send_buf), (mine, keep_buf)):
                at = pl.ds(start, half)
                if groups == 4:
                    turns = [[(w, 0), (w, 1), (wp + w, 0), (wp + w, 1)]]
                    places = [w]
                else:
                    turns = [[(w, 0), (w, 1)], [(wp + w, 0), (wp + w, 1)]]
                    places = [w, wp + w]
                for turn, place in zip(turns, places):
                    left = jnp.concatenate([buf[k, ww, at, :] for ww, k in turn], axis=1)
                    got = jnp.dot(left, picker, preferred_element_type=F32).astype(BF)
                    for p in range(pieces):
                        dest[p, place] = got[p * part : (p + 1) * part]
    last = [
        pltpu.make_async_copy(send_buf, send_ref, out_sem.at[chunks, 0]),
        pltpu.make_async_copy(keep_buf, keep_ref, out_sem.at[chunks, 1]),
    ]
    for copy in last:
        copy.start()
    for copy in outs + last:
        copy.wait()


def pick(spectra, src_ids, cap, pieces):
    _, windows, freqs, chans = spectra.shape
    half = freqs // 2
    rows = windows * cap * 2 // LANES
    chunks = 5 if (windows // 2) % 5 == 0 else 1
    shape = (pieces, rows, half // pieces, LANES)
    out = jax.ShapeDtypeStruct(shape, BF)
    return pl.pallas_call(
        functools.partial(pick_kernel, cap, pieces),
        in_specs=[VMEM, ANY],
        out_specs=[ANY, ANY, ANY],
        out_shape=[out, out, jax.ShapeDtypeStruct((2, windows, half, chans), BF)],
        scratch_shapes=[
            pltpu.VMEM(spectra.shape, BF),
            pltpu.VMEM(shape, BF),
            pltpu.VMEM(shape, BF),
            pltpu.SemaphoreType.DMA((chunks, 4)),
            pltpu.SemaphoreType.DMA((chunks + 1, 4)),
        ],
        compiler_params=PARAMS,
        name="pick_sources",
    )(src_ids, spectra)


def prep_kernel(own_ref, got_ref, out_ref, own, got, res, in_sem, out_sem):
    _, windows, half, chans = got.shape
    wp = windows // 2
    core = lax.axis_index("chan") & 1
    mine = pl.ds(pl.multiple_of(core * half, half), half)
    ins = []
    for k in range(2):
        ins.append(pltpu.make_async_copy(own_ref.at[k, :, mine], own.at[k], in_sem.at[k, 0]))
        ins.append(pltpu.make_async_copy(got_ref.at[k], got.at[k], in_sem.at[k, 1]))
    for copy in ins:
        copy.start()
    turn = frequency_first(wp)
    for copy in ins:
        copy.wait()
    outs = []
    for b in range(half // FB):
        at = pl.ds(b * FB, FB)
        for k in range(2):
            for w2 in range(2):
                ws = pl.ds(w2 * wp, wp)
                both = jnp.concatenate([own[k, ws, at, :], got[k, ws, at, :]], axis=2).reshape(wp * FB, 2 * chans)
                moved = jnp.dot(turn, both, preferred_element_type=F32).astype(BF)
                res[at, pl.ds((2 * k + w2) * WROWS, WROWS), :] = moved.reshape(FB, WROWS, 2 * chans)
        outs.append(pltpu.make_async_copy(res.at[at], out_ref.at[at], out_sem.at[b]))
        outs[-1].start()
    for copy in outs:
        copy.wait()


def prep(spectra, got):
    _, windows, freqs, chans = spectra.shape
    half = freqs // 2
    shape = (half, 4 * WROWS, 2 * chans)
    return pl.pallas_call(
        prep_kernel,
        in_specs=[ANY, ANY],
        out_specs=ANY,
        out_shape=jax.ShapeDtypeStruct(shape, BF),
        scratch_shapes=[
            pltpu.VMEM(got.shape, BF),
            pltpu.VMEM(got.shape, BF),
            pltpu.VMEM(shape, BF),
            pltpu.SemaphoreType.DMA((2, 2)),
            pltpu.SemaphoreType.DMA((half // FB,)),
        ],
        compiler_params=PARAMS,
        name="frequency_major",
    )(spectra, got)


def onehot_kernel(nchan, own_ref, got_ref, slot_ref, out_ref, count_ref, pairs, row_bin):
    chans = own_ref.shape[1]
    bins = slot_ref.shape[1]
    per = bins // nchan
    group = out_ref.shape[0]
    step = pl.program_id(0)

    @pl.when(step == 0)
    def _():
        pairs[:, pl.ds(0, chans)] = own_ref[...]
        pairs[:, pl.ds(chans, chans)] = got_ref[...]
        slot_col = as_column(slot_ref[...])
        r = iota((1, bins), 1)
        block, rest = shift(r, per), r & (per - 1)
        core, chip = shift(block, nchan // 2), block & (nchan // 2 - 1)
        order = (chip * 2 + core) * per + rest
        row_bin[...] = jnp.sum(jnp.where(slot_col == order, iota((bins, 1), 0), 0), axis=0, keepdims=True)
        count_ref[...] = jnp.zeros_like(count_ref)

    named = row_bin[...]
    total = jnp.zeros(count_ref.shape, F32)
    block = jnp.transpose(pairs[pl.ds(pl.multiple_of(step * group, group), group), :])
    for s in range(group):
        hit = jnp.where(block[:, s : s + 1] == named, 1.0, 0.0)
        out_ref[s] = hit.astype(BF)
        total = total + jnp.sum(hit[:chans], axis=0, keepdims=True)
    count_ref[...] += total


def onehot(own, got, slot_of_bin, nchan):
    slots, chans = own.shape
    bins = slot_of_bin.shape[0]
    group = 8
    return pl.pallas_call(
        functools.partial(onehot_kernel, nchan),
        grid=(slots // group,),
        in_specs=[
            pl.BlockSpec((slots, chans), lambda i: (0, 0)),
            pl.BlockSpec((slots, chans), lambda i: (0, 0)),
            pl.BlockSpec((1, bins), lambda i: (0, 0)),
        ],
        out_specs=[
            pl.BlockSpec((group, 2 * chans, bins), lambda i: (i, 0, 0)),
            pl.BlockSpec((1, bins), lambda i: (0, 0)),
        ],
        out_shape=[
            jax.ShapeDtypeStruct((slots, 2 * chans, bins), BF),
            jax.ShapeDtypeStruct((1, bins), F32),
        ],
        scratch_shapes=[pltpu.VMEM((slots, 2 * chans), I32), pltpu.VMEM((1, bins), I32)],
        compiler_params=PARAMS,
        name="bin_onehot",
    )(own, got, slot_of_bin[None, :])


def cross_kernel(cap, chips, routes, first_f, final, *refs):
    pieces = len(routes)
    src_ref, recv_ref, hot_ref, cos_ref, sin_ref, count_ref, prior_ref = refs[:7]
    xrefs = refs[7 : 7 + pieces * chips]
    refs = refs[7 + pieces * chips :]
    outs, refs = (refs[:2], refs[2:]) if final else (refs[:1], refs[1:])
    xbuf, recv, hot, xs, cross, whole, in_sem, hot_sem, recv_sem = refs
    _, _, rows, part, _ = xbuf.shape
    count, chans2 = recv.shape[0], recv.shape[2]
    slots, _, bins = hot.shape
    wp = rows * LANES // (2 * cap) // 2
    groups = LANES // cap

    xin = []
    for p in range(pieces):
        for d in range(chips):
            xin.append(pltpu.make_async_copy(xrefs[p * chips + d], xbuf.at[p, d], in_sem.at[p, d]))
    rin = pltpu.make_async_copy(recv_ref.at[pl.ds(first_f, count)], recv, recv_sem)
    hgroup = slots // hot_sem.shape[0]
    hin = [
        pltpu.make_async_copy(hot_ref.at[pl.ds(g * hgroup, hgroup)], hot.at[pl.ds(g * hgroup, hgroup)], hot_sem.at[g])
        for g in range(hot_sem.shape[0])
    ]
    for copy in xin + [rin] + hin:
        copy.start()

    me = lax.axis_index("chan")
    row = source_row(src_ref)
    _, _, _, own_row, rank_row = chip_ranks(row, chans2)
    own_row = jnp.concatenate([own_row] * groups, axis=1)
    rank_row = jnp.concatenate([rank_row] * groups, axis=1)
    shape = (LANES, groups * slots)
    r, c = iota(shape, 0), iota(shape, 1)
    aligned = (shift(r, cap) == shift(c, slots)) & ((r & (cap - 1)) == rank_row)
    turn = frequency_first(wp)
    for copy in xin:
        copy.wait()
    for p in range(pieces):
        place = jnp.concatenate(
            [jnp.where(aligned & (own_row == (shift(me, 2) ^ (routes[p][d] >> 1))), 1.0, 0.0).astype(BF) for d in range(chips)],
            axis=0,
        )
        for b in range(part // FB):
            at = pl.ds(b * FB, FB)
            sides = []
            for h in range(rows // wp):
                ws = pl.ds(h * wp, wp)
                got = jnp.concatenate([xbuf[p, d, ws, at, :] for d in range(chips)], axis=2)
                got = got.reshape(wp * FB, chips * LANES)
                sides.append(jnp.dot(got, place, preferred_element_type=F32).astype(BF))
            moved = jnp.concatenate(sides, axis=1) if len(sides) > 1 else sides[0]
            xs[pl.ds((p * part + b * FB) * WROWS, FB * WROWS), :] = jnp.dot(turn, moved, preferred_element_type=F32)

    rin.wait()
    imag = iota((2 * WROWS, LANES), 1) >= slots

    def one_group(g, carry):
        for j in range(8):
            f = g * 8 + j
            x = xs[pl.ds(pl.multiple_of(f * WROWS, WROWS), WROWS), :]
            x = jnp.concatenate([x[:, :LANES], x[:, LANES:]], axis=0)
            upper = jnp.where(imag, -x, x)
            if j:
                upper = pltpu.roll(upper, j, 1)
            left = jnp.concatenate([upper, pltpu.roll(x, slots + j, 1)], axis=0).astype(BF)
            got = lax.dot_general(left, recv[f], (((0,), (0,)), ((), ())), preferred_element_type=F32)
            base = pl.multiple_of(g * (8 * PITCH) + j * (PITCH - 1), 8)
            for h in range(2):
                side = got[:, h * LANES : (h + 1) * LANES]
                cross[h, pl.ds(base, LANES), :] = side
                if j:
                    cross[h, pl.ds(pl.multiple_of(base + LANES, 8), 8), :] = side[:8]
        return carry

    lax.fori_loop(0, count // 8, one_group, 0)

    total = jnp.zeros((2 * count, bins), F32)
    for copy in hin:
        copy.wait()

    def one_slot(s2, total):
        for s in (2 * s2, 2 * s2 + 1):
            parts = []
            for turn in range(2):
                at = pl.ds(s + turn * slots, count, stride=PITCH)
                parts.append(jnp.concatenate([cross[0, at, :], cross[1, at, :]], axis=1))
            x = jnp.concatenate(parts, axis=0)
            high = x.astype(BF)
            low = (x - high.astype(F32)).astype(BF)
            weights = hot[s]
            total = total + jnp.dot(high, weights, preferred_element_type=F32)
            total = total + jnp.dot(low, weights, preferred_element_type=F32)
        return total

    total = lax.fori_loop(0, slots // 2, one_slot, total)
    at = pl.ds(first_f, count)
    table = jnp.concatenate([cos_ref[at, :], sin_ref[at, :]], axis=0)
    lagged = lax.dot_general(total, table, (((0,), (0,)), ((), ())), precision=lax.Precision.HIGHEST, preferred_element_type=F32)
    if not final:
        outs[0][...] = lagged
        return
    if first_f:
        lagged = lagged + prior_ref[...]
    whole[...] = lagged
    core = me & 1
    blocks, padded, lags = outs[0].shape
    per = bins // (2 * blocks)
    crows = count_ref.shape[0]
    for which, dest in ((core, outs[0]), (1 - core, outs[1])):
        for d in range(blocks):
            start = pl.multiple_of((which * blocks + d) * per, per)
            dest[d, pl.ds(0, per), :] = whole[pl.ds(start, per), :]
            dest[d, pl.ds(per, crows), :] = count_ref[...]


def cross_and_bin(arrays, routes, src_ids, recv, hot, counts, cos, sin, prior, first_f, cap, nchan, final):
    pieces, chips = len(arrays), len(arrays[0])
    rows, part, _ = arrays[0][0].shape
    slots, chans2, bins = hot.shape
    lags = cos.shape[1]
    count = pieces * part
    per = bins // nchan
    if final:
        out = jax.ShapeDtypeStruct((nchan // 2, per + 8, lags), F32)
        out_shape, out_specs = [out, out], [VMEM, VMEM]
    else:
        out_shape, out_specs = [jax.ShapeDtypeStruct((bins, lags), F32)], [VMEM]
    return pl.pallas_call(
        functools.partial(cross_kernel, cap, chips, routes, first_f, final),
        in_specs=[VMEM, ANY, ANY, VMEM, VMEM, VMEM, VMEM] + [ANY] * (pieces * chips),
        out_specs=out_specs,
        out_shape=out_shape,
        scratch_shapes=[
            pltpu.VMEM((pieces, chips, rows, part, LANES), BF),
            pltpu.VMEM((count,) + recv.shape[1:], BF),
            pltpu.VMEM(hot.shape, BF),
            pltpu.VMEM((count * WROWS, 2 * LANES), F32),
            pltpu.VMEM((2, count * PITCH + 8, chans2 // 2), F32),
            pltpu.VMEM((bins, lags), F32),
            pltpu.SemaphoreType.DMA((pieces, chips)),
            pltpu.SemaphoreType.DMA((8,)),
            pltpu.SemaphoreType.DMA,
        ],
        compiler_params=PARAMS,
        name="cross_and_bin",
    )(src_ids, recv, hot, cos, sin, counts, prior, *[x for held in arrays for x in held])


def swap(x, size, bit):
    return lax.ppermute(x, "chan", [(i, i ^ bit) for i in range(size)])


def sums(nchan, nfreq, cap, spectra, src_ids, pair_bin, slot_of_bin):
    _, windows, freqs, chans = spectra.shape
    half = freqs // 2
    bins = slot_of_bin.shape[0]
    slots = src_ids.shape[0] * src_ids.shape[1]
    me = lax.axis_index("chan")
    core = me & 1
    rest = [1 << k for k in range(1, nchan.bit_length() - 1)]
    pieces = min(4, half // FB)

    keep, send, spec_send = pick(spectra, src_ids, cap, pieces)
    got = swap(send, nchan, 1)
    chip = [keep[p] + got[p] for p in range(pieces)]
    arrays, routes = [], []
    for p in range(pieces):
        held, names = [chip[p]], [0]
        for bit in rest if p % 2 == 0 else rest[::-1]:
            held = held + [swap(x, nchan, bit) for x in held]
            names = names + [name ^ bit for name in names]
        arrays.append(held)
        routes.append(names)

    pairs_own = pair_bin.reshape(slots, chans)
    got_pairs = swap(pairs_own, nchan, 1)
    got_spec = swap(spec_send, nchan, 1)
    hot, counts = onehot(pairs_own, got_pairs, slot_of_bin, nchan)
    recv = prep(spectra, got_spec)
    cos, sin = lag_basis(lax.axis_index("freq") * freqs + core * half, half, F, NLAG, windows)
    counts = counts.reshape(bins // NLAG, NLAG)
    chunk = 2
    prior = jnp.zeros((bins, NLAG), F32)
    for p in range(0, pieces, chunk):
        final = p + chunk >= pieces
        out = cross_and_bin(
            arrays[p : p + chunk], routes[p : p + chunk], src_ids, recv, hot, counts, cos, sin, prior, p * (half // pieces), cap, nchan, final
        )
        if not final:
            prior = out[0]
    mine, other = out

    per = bins // nchan
    mine = mine + swap(other, nchan, 1)
    at = me // 2
    if nchan // 2 <= 4:
        total = lax.dynamic_index_in_dim(mine, at, 0, keepdims=False)
        for move in range(1, nchan // 2):
            total = total + swap(lax.dynamic_index_in_dim(mine, at ^ move, 0, keepdims=False), nchan, 2 * move)
    else:
        for bit in rest[::-1]:
            size = mine.shape[0] // 2
            up = (me & bit) != 0
            low, high = mine[:size], mine[size:]
            mine = jnp.where(up, high, low) + swap(jnp.where(up, low, high), nchan, bit)
        total = mine[0]
    owned = total[:per]
    parts = [owned]
    if nfreq <= 4:
        parts += [lax.ppermute(owned, "freq", [(i, i ^ k) for i in range(nfreq)]) for k in range(1, nfreq)]
    else:
        for k in range(nfreq.bit_length() - 1):
            owned = parts[0]
            parts = [owned + lax.ppermute(owned, "freq", [(i, i ^ (1 << k)) for i in range(nfreq)])]
    counted = total[per : per + bins // NLAG].reshape(bins)
    count = lax.dynamic_slice(counted, ((core * (nchan // 2) + at) * per,), (per,))
    return parts, count


def scaled(parts, count):
    total = parts[0]
    for part in parts[1:]:
        total = total + part
    return total / jnp.sqrt(jnp.maximum(count, 1.0))[:, None]


def body(nchan, nfreq, spectra, src_ids, pair_bin, slot_of_bin):
    args = (spectra, src_ids, pair_bin, slot_of_bin)
    slots = src_ids.shape[0] * src_ids.shape[1]
    cap = slots // 2
    owner = src_ids.reshape(-1) // (2 * spectra.shape[3])
    loads = jnp.sum((owner[None, :] == lax.iota(I32, nchan // 2)[:, None]).astype(I32), axis=1)
    fits = jnp.max(loads) <= cap
    parts, count = sums(nchan, nfreq, cap, *args)
    return lax.cond(
        fits,
        lambda parts, count, *args: scaled(parts, count),
        lambda parts, count, *args: scaled(*sums(nchan, nfreq, slots, *args)),
        parts,
        count,
        *args,
    )


def solution(mesh):
    return jax.shard_map(
        functools.partial(body, mesh.shape["chan"], mesh.shape["freq"]),
        mesh=mesh,
        in_specs=(P(None, None, "freq", "chan"), P(), P(None, None, "chan"), P()),
        out_specs=P("chan", None),
        check_vma=False,
    )
```

```python
import functools
import math

import jax
import jax.numpy as jnp
from jax import lax
from jax.experimental import pallas as pl
from jax.experimental.pallas import tpu as pltpu
from jax.sharding import PartitionSpec as P

F = 1024
NLAG = 256
BF = jnp.bfloat16
F32 = jnp.float32
I32 = jnp.int32
FB = 16
WROWS = 16
LANES = 128
SLACK = 6 * 1024 * 1024
PITCH = LANES + 9
TURN = 8
GROUPS = 4
ANY = pl.BlockSpec(memory_space=pl.ANY)
VMEM = pl.BlockSpec(memory_space=pltpu.VMEM)


def lag_basis(anchor, amount, totals, lag_count, windows):
    frequency = anchor + lax.iota(I32, amount)
    shifts = lax.iota(I32, lag_count) - lag_count // 2
    phases = frequency[:, None] * shifts[None, :] % (2 * totals)
    angles = phases.astype(F32) * (math.pi / totals)
    factor = 1.0 / math.sqrt(windows * totals)
    return jnp.cos(angles) * factor, -jnp.sin(angles) * factor


def params(*buffers):
    used = sum(math.prod(shape) * jnp.dtype(kind).itemsize for shape, kind in buffers)
    return pltpu.CompilerParams(vmem_limit_bytes=used + SLACK)


def iota(shape, dim):
    return lax.broadcasted_iota(I32, shape, dim)


def shift(values, size):
    return lax.shift_right_logical(values, jnp.int32(size.bit_length() - 1))


def as_column(row):
    size = row.shape[1]
    eye = iota((size, size), 0) == iota((size, size), 1)
    return jnp.sum(jnp.where(eye, row, 0), axis=1, keepdims=True)


def source_row(src_ref):
    return jnp.concatenate([src_ref[t : t + 1, :] for t in range(src_ref.shape[0])], axis=1)


def chip_ranks(row, per_chip):
    size = row.shape[1]
    own_row = shift(row, per_chip)
    col = as_column(row)
    own_col = shift(col, per_chip)
    same = own_col == own_row
    q0, q1 = iota((size, size), 0), iota((size, size), 1)
    rank_col = jnp.sum(jnp.where(same & (q1 < q0), 1, 0), axis=1, keepdims=True)
    rank_row = jnp.sum(jnp.where(same & (q0 < q1), 1, 0), axis=0, keepdims=True)
    return col, own_col, rank_col, own_row, rank_row


def frequency_first(rows):
    shape = (FB * WROWS, rows * FB)
    r, c = iota(shape, 0), iota(shape, 1)
    hit = (shift(r, WROWS) == (c & (FB - 1))) & ((r & (WROWS - 1)) == shift(c, FB))
    return jnp.where(hit, 1.0, 0.0).astype(BF)


def pick_kernel(cap, pieces, src_ref, spec_ref, keep_ref, send_ref, buf, keep_buf, send_buf, in_sem, out_sem):
    _, windows, freqs, chans = spec_ref.shape
    wp = windows // 2
    half = freqs // 2
    part = half // pieces
    groups = LANES // cap
    me = lax.axis_index("chan")
    core = me & 1
    chunks = in_sem.shape[0]
    wc = wp // chunks
    ins = []
    for j in range(chunks):
        for k in range(2):
            for w2 in range(2):
                at = pl.ds(w2 * wp + j * wc, wc)
                ins.append(pltpu.make_async_copy(spec_ref.at[k, at], buf.at[k, at], in_sem.at[j, 2 * k + w2]))
    for copy in ins:
        copy.start()

    row = source_row(src_ref)
    col, own_col, rank_col, _, _ = chip_ranks(row, 2 * chans)
    slots = row.shape[1]
    lane_r = iota((slots, LANES), 1) & (cap - 1)
    match = (own_col == shift(me, 2)) & (rank_col == lane_r)
    local = col - me * chans
    found = jnp.sum(jnp.where(match, local + 1, 0), axis=0, keepdims=True) - 1
    shape = (groups * chans, LANES)
    r, c = iota(shape, 0), iota(shape, 1)
    hit = (shift(r, chans) == shift(c, cap)) & ((r & (chans - 1)) == found)
    picker = jnp.where(hit, 1.0, 0.0).astype(BF)

    mine = pl.multiple_of(core * half, half)
    other = pl.multiple_of((1 - core) * half, half)
    outs = []
    for j in range(chunks):
        for copy in ins[4 * j : 4 * j + 4]:
            copy.wait()
        for i in range(wc):
            w = j * wc + i
            if groups == 4:
                turns, places = [[(w, 0), (w, 1), (wp + w, 0), (wp + w, 1)]], [w]
            else:
                turns, places = [[(w, 0), (w, 1)], [(wp + w, 0), (wp + w, 1)]], [w, wp + w]
            for start, dest in ((other, send_buf), (mine, keep_buf)):
                for turn, place in zip(turns, places):
                    left = jnp.concatenate([buf[k, ww, pl.ds(start, half), :] for ww, k in turn], axis=1)
                    got = jnp.dot(left, picker, preferred_element_type=F32).astype(BF)
                    for p in range(pieces):
                        dest[p, place] = got[p * part : (p + 1) * part]
        for h in range(4 // groups if groups < 4 else 1):
            at = pl.ds(h * wp + j * wc, wc)
            for n, (dest, ref) in enumerate(((send_buf, send_ref), (keep_buf, keep_ref))):
                outs.append(pltpu.make_async_copy(dest.at[:, at], ref.at[:, at], out_sem.at[j, 2 * h + n]))
                outs[-1].start()
    for copy in outs:
        copy.wait()


def pick(spectra, src_ids, cap, pieces):
    _, windows, freqs, chans = spectra.shape
    half = freqs // 2
    rows = windows * cap * 2 // LANES
    chunks = 5 if (windows // 2) % 5 == 0 else 1
    shape = (pieces, rows, half // pieces, LANES)
    out = jax.ShapeDtypeStruct(shape, BF)
    return pl.pallas_call(
        functools.partial(pick_kernel, cap, pieces),
        in_specs=[VMEM, ANY],
        out_specs=[ANY, ANY],
        out_shape=[out, out],
        scratch_shapes=[
            pltpu.VMEM(spectra.shape, BF),
            pltpu.VMEM(shape, BF),
            pltpu.VMEM(shape, BF),
            pltpu.SemaphoreType.DMA((chunks, 4)),
            pltpu.SemaphoreType.DMA((chunks, 4)),
        ],
        compiler_params=params((spectra.shape, BF), (shape, BF), (shape, BF)),
        name="pick_sources",
    )(src_ids, spectra)


def prep_kernel(own_ref, got_ref, out_ref, own, got, in_sem):
    _, windows, half, chans = got.shape
    wp = windows // 2
    core = lax.axis_index("chan") & 1
    mine = pl.ds(pl.multiple_of(core * half, half), half)
    ins = []
    for k in range(2):
        ins.append(pltpu.make_async_copy(own_ref.at[k, :, mine], own.at[k], in_sem.at[k, 0]))
        ins.append(pltpu.make_async_copy(got_ref.at[k, :, mine], got.at[k], in_sem.at[k, 1]))
    for copy in ins:
        copy.start()
    turn = frequency_first(wp)
    for copy in ins:
        copy.wait()
    for b in range(half // FB):
        at = pl.ds(b * FB, FB)
        for k in range(2):
            for w2 in range(2):
                ws = pl.ds(w2 * wp, wp)
                both = jnp.concatenate([own[k, ws, at, :], got[k, ws, at, :]], axis=2).reshape(wp * FB, 2 * chans)
                moved = jnp.dot(turn, both, preferred_element_type=F32).astype(BF)
                out_ref[at, pl.ds((2 * k + w2) * WROWS, WROWS), :] = moved.reshape(FB, WROWS, 2 * chans)


def prep(spectra, got):
    _, windows, freqs, chans = spectra.shape
    half = freqs // 2
    shape = (half, 4 * WROWS, 2 * chans)
    side = (2, windows, half, chans)
    return pl.pallas_call(
        prep_kernel,
        in_specs=[ANY, ANY],
        out_specs=VMEM,
        out_shape=jax.ShapeDtypeStruct(shape, BF),
        scratch_shapes=[pltpu.VMEM(side, BF), pltpu.VMEM(side, BF), pltpu.SemaphoreType.DMA((2, 2))],
        compiler_params=params((side, BF), (side, BF)),
        name="frequency_major",
    )(spectra, got)


def onehot_kernel(nchan, own_ref, got_ref, slot_ref, out_ref, count_ref, pairs):
    slots, chans = own_ref.shape
    bins = slot_ref.shape[1]
    per = bins // nchan
    group = 8
    pairs[:, pl.ds(0, chans)] = own_ref[...]
    pairs[:, pl.ds(chans, chans)] = got_ref[...]
    slot_col = as_column(slot_ref[...])
    r = iota((1, bins), 1)
    block, rest = shift(r, per), r & (per - 1)
    core, chip = shift(block, nchan // 2), block & (nchan // 2 - 1)
    order = (chip * 2 + core) * per + rest
    named = jnp.sum(jnp.where(slot_col == order, iota((bins, 1), 0), 0), axis=0, keepdims=True)
    ones = jnp.ones((8, chans), BF)
    count_ref[...] = jnp.zeros_like(count_ref)

    def one_step(step, carry):
        block = jnp.transpose(pairs[pl.ds(pl.multiple_of(step * group, group), group), :])
        total = jnp.zeros((8, bins), F32)
        for s in range(group):
            hit = jnp.where(block[:, s : s + 1] == named, 1.0, 0.0).astype(BF)
            out_ref[step * group + s] = hit
            total = total + jnp.dot(ones, hit[:chans], preferred_element_type=F32)
        count_ref[...] += total
        return carry

    lax.fori_loop(0, slots // group, one_step, 0)


def onehot(own, got, slot_of_bin, nchan):
    slots, chans = own.shape
    bins = slot_of_bin.shape[0]
    shape = (slots, 2 * chans, bins)
    return pl.pallas_call(
        functools.partial(onehot_kernel, nchan),
        in_specs=[VMEM, VMEM, VMEM],
        out_specs=[VMEM, VMEM],
        out_shape=[jax.ShapeDtypeStruct(shape, BF), jax.ShapeDtypeStruct((8, bins), F32)],
        scratch_shapes=[pltpu.VMEM((slots, 2 * chans), I32)],
        compiler_params=params(((bins, bins), I32)),
        name="bin_onehot",
    )(own, got, slot_of_bin[None, :])


def cross_kernel(cap, chips, routes, *refs):
    pieces = len(routes)
    src_ref, recv, hot, cos_ref, sin_ref, count_ref = refs[:6]
    xrefs = refs[6 : 6 + pieces * chips]
    refs = refs[6 + pieces * chips :]
    outs, refs = refs[:2], refs[2:]
    xs, cross, sums, whole = refs
    rows, part, _ = xrefs[0].shape
    count, _, chans2 = recv.shape
    slots, _, bins = hot.shape
    wp = rows * LANES // (2 * cap) // 2
    groups = LANES // cap
    me = lax.axis_index("chan")
    row = source_row(src_ref)
    _, _, _, own_row, rank_row = chip_ranks(row, chans2)
    own_row = jnp.concatenate([own_row] * groups, axis=1)
    rank_row = jnp.concatenate([rank_row] * groups, axis=1)
    shape = (LANES, groups * slots)
    r, c = iota(shape, 0), iota(shape, 1)
    aligned = (shift(r, cap) == shift(c, slots)) & ((r & (cap - 1)) == rank_row)
    turn = frequency_first(wp)
    for p in range(pieces):
        place = jnp.concatenate(
            [jnp.where(aligned & (own_row == (shift(me, 2) ^ (routes[p][d] >> 1))), 1.0, 0.0).astype(BF) for d in range(chips)],
            axis=0,
        )
        for b in range(part // FB):
            at = pl.ds(b * FB, FB)
            sides = []
            for h in range(rows // wp):
                ws = pl.ds(h * wp, wp)
                got = jnp.concatenate([xrefs[p * chips + d][ws, at, :] for d in range(chips)], axis=2)
                got = got.reshape(wp * FB, chips * LANES)
                sides.append(jnp.dot(got, place, preferred_element_type=F32).astype(BF))
            moved = jnp.concatenate(sides, axis=1) if len(sides) > 1 else sides[0]
            xs[pl.ds((p * part + b * FB) * WROWS, FB * WROWS), :] = jnp.dot(turn, moved, preferred_element_type=F32)

    imag = iota((2 * WROWS, LANES), 1) >= slots
    quarter = shift(iota((1, 4 * 4 * WROWS), 1), 4 * WROWS)
    masks = [jnp.where(quarter == i, 1.0, 0.0).astype(BF) for i in range(4)]

    def one_group(step, carry):
        for sub in range(2 * min(GROUPS, count // 8)):
            g, q = step * min(GROUPS, count // 8) + sub // 2, sub % 2
            lefts = []
            for j in range(4 * q, 4 * q + 4):
                at = pl.ds(pl.multiple_of((g * 8 + j) * WROWS, WROWS), WROWS)
                x = xs[at, :]
                x = jnp.concatenate([x[:, :LANES], x[:, LANES:]], axis=0)
                upper = jnp.where(imag, -x, x)
                if j:
                    upper = pltpu.roll(upper, j, 1)
                lefts += [upper, pltpu.roll(x, slots + j, 1)]
            left = jnp.transpose(jnp.concatenate(lefts, axis=0)).astype(BF)
            left = jnp.concatenate([left * mask for mask in masks], axis=0)
            right = recv[pl.ds(g * 8 + 4 * q, 4)].reshape(4 * 4 * WROWS, chans2)
            got = jnp.dot(left, right, preferred_element_type=F32)
            for i in range(4):
                j = 4 * q + i
                base = pl.multiple_of(g * (8 * PITCH) + j * (PITCH - 1), 8)
                for h in range(2):
                    side = got[i * LANES : (i + 1) * LANES, h * LANES : (h + 1) * LANES]
                    cross[h, pl.ds(base, LANES), :] = side
                    if j:
                        cross[h, pl.ds(pl.multiple_of(base + LANES, 8), 8), :] = side[:8]
        return carry

    lax.fori_loop(0, count // (8 * min(GROUPS, count // 8)), one_group, 0)

    sums[...] = jnp.zeros_like(sums)

    def one_turn(step, carry):
        lefts = []
        for u in range(TURN):
            s = step * TURN + u
            parts = []
            for turn in range(2):
                at = pl.ds(s + turn * slots, count, stride=PITCH)
                parts.append(jnp.concatenate([cross[0, at, :], cross[1, at, :]], axis=1))
            x = jnp.concatenate(parts, axis=0)
            high = x.astype(BF)
            low = (x - high.astype(F32)).astype(BF)
            lefts.append(jnp.concatenate([high, low], axis=0))
        left = jnp.concatenate(lefts, axis=1)
        right = hot[pl.ds(step * TURN, TURN)].reshape(TURN * chans2, bins)
        sums[...] += jnp.dot(left, right, preferred_element_type=F32)
        return carry

    lax.fori_loop(0, slots // TURN, one_turn, 0)
    total = sums[pl.ds(0, 2 * count), :] + sums[pl.ds(2 * count, 2 * count), :]
    table = jnp.concatenate([cos_ref[...], sin_ref[...]], axis=0)
    whole[...] = lax.dot_general(total, table, (((0,), (0,)), ((), ())), precision=lax.Precision.HIGHEST, preferred_element_type=F32)
    core = me & 1
    blocks, padded, lags = outs[0].shape
    per = bins // (2 * blocks)
    crows = count_ref.shape[0]
    for which, dest in ((core, outs[0]), (1 - core, outs[1])):
        for d in range(blocks):
            start = pl.multiple_of((which * blocks + d) * per, per)
            dest[d, pl.ds(0, per), :] = whole[pl.ds(start, per), :]
            dest[d, pl.ds(per, crows), :] = count_ref[...]


def cross_and_bin(arrays, routes, src_ids, recv, hot, counts, cos, sin, cap, nchan):
    pieces, chips = len(arrays), len(arrays[0])
    rows, part, _ = arrays[0][0].shape
    _, chans2, bins = hot.shape
    lags = cos.shape[1]
    count = pieces * part
    per = bins // nchan
    out = jax.ShapeDtypeStruct((nchan // 2, per + 8, lags), F32)
    operands = [((pieces, chips, rows, part, LANES), BF), (recv.shape, BF), (hot.shape, BF)]
    buffers = [
        ((count * WROWS, 2 * LANES), F32),
        ((2, count * PITCH + 8, chans2 // 2), F32),
        ((4 * count, bins), F32),
        ((bins, lags), F32),
    ]
    return pl.pallas_call(
        functools.partial(cross_kernel, cap, chips, routes),
        in_specs=[VMEM] * (6 + pieces * chips),
        out_specs=[VMEM, VMEM],
        out_shape=[out, out],
        scratch_shapes=[pltpu.VMEM(shape, kind) for shape, kind in buffers],
        compiler_params=params(*buffers),
        name="cross_and_bin",
    )(src_ids, recv, hot, cos, sin, counts, *[x for held in arrays for x in held])


def swap(x, size, bit):
    return lax.ppermute(x, "chan", [(i, i ^ bit) for i in range(size)])


def sums(nchan, nfreq, cap, spectra, src_ids, pair_bin, slot_of_bin):
    _, windows, freqs, chans = spectra.shape
    half = freqs // 2
    bins = slot_of_bin.shape[0]
    slots = src_ids.shape[0] * src_ids.shape[1]
    me = lax.axis_index("chan")
    core = me & 1
    rest = [1 << k for k in range(1, nchan.bit_length() - 1)]
    pieces = 2

    pairs_own = pair_bin.reshape(slots, chans)
    got_pairs = swap(pairs_own, nchan, 1)
    keep, send = pick(spectra, src_ids, cap, pieces)
    got = swap(send, nchan, 1)
    chip = [keep[p] + got[p] for p in range(pieces)]
    orders = [rest if p % 2 == 0 else rest[::-1] for p in range(pieces)]
    arrays, routes = [[x] for x in chip], [[0] for _ in chip]
    early = [[] for _ in chip]
    for hop in range(len(rest)):
        if hop == len(rest) - 1:
            early = [[swap(chip[p], nchan, orders[p][hop])] for p in range(pieces)]
            hot, counts = onehot(pairs_own, got_pairs, slot_of_bin, nchan)
            later, early, counts = lax.optimization_barrier(([held[1:] for held in arrays], early, counts))
            arrays = [[held[0]] + rest_of for held, rest_of in zip(arrays, later)]
        for p in range(pieces):
            bit = orders[p][hop]
            arrays[p] = arrays[p] + early[p] + [swap(x, nchan, bit) for x in arrays[p][len(early[p]) :]]
            routes[p] = routes[p] + [name ^ bit for name in routes[p]]

    spectra_sent, got = lax.optimization_barrier((spectra, got))
    got_spec, counts = lax.optimization_barrier((swap(spectra_sent, nchan, 1), counts))
    recv = prep(spectra, got_spec)
    cos, sin = lag_basis(lax.axis_index("freq") * freqs + core * half, half, F, NLAG, windows)
    counts = counts[0].reshape(bins // NLAG, NLAG)
    out = cross_and_bin(arrays, routes, src_ids, recv, hot, counts, cos, sin, cap, nchan)
    mine, other = out

    per = bins // nchan
    mine = mine + swap(other, nchan, 1)
    at = me // 2
    if nchan // 2 <= 4:
        total = lax.dynamic_index_in_dim(mine, at, 0, keepdims=False)
        for move in range(1, nchan // 2):
            total = total + swap(lax.dynamic_index_in_dim(mine, at ^ move, 0, keepdims=False), nchan, 2 * move)
    else:
        for bit in rest[::-1]:
            size = mine.shape[0] // 2
            up = (me & bit) != 0
            low, high = mine[:size], mine[size:]
            mine = jnp.where(up, high, low) + swap(jnp.where(up, low, high), nchan, bit)
        total = mine[0]
    owned = total[:per]
    parts = [owned]
    if nfreq <= 4:
        parts += [lax.ppermute(owned, "freq", [(i, i ^ k) for i in range(nfreq)]) for k in range(nfreq - 1, 0, -1)]
    else:
        for k in range(nfreq.bit_length() - 1):
            owned = parts[0]
            parts = [owned + lax.ppermute(owned, "freq", [(i, i ^ (1 << k)) for i in range(nfreq)])]
    counted = total[per : per + bins // NLAG].reshape(bins)
    count = lax.dynamic_slice(counted, ((core * (nchan // 2) + at) * per,), (per,))
    return parts, count


def scaled(parts, count):
    total = parts[0]
    for part in parts[1:]:
        total = total + part
    return total / jnp.sqrt(jnp.maximum(count, 1.0))[:, None]


def body(nchan, nfreq, spectra, src_ids, pair_bin, slot_of_bin):
    args = (spectra, src_ids, pair_bin, slot_of_bin)
    slots = src_ids.shape[0] * src_ids.shape[1]
    cap = slots // 2
    owner = src_ids.reshape(-1) // (2 * spectra.shape[3])
    loads = jnp.sum((owner[None, :] == lax.iota(I32, nchan // 2)[:, None]).astype(I32), axis=1)
    fits = jnp.max(loads) <= cap
    parts, count = sums(nchan, nfreq, cap, *args)
    return lax.cond(
        fits,
        lambda parts, count, *args: scaled(parts, count),
        lambda parts, count, *args: scaled(*sums(nchan, nfreq, slots, *args)),
        parts,
        count,
        *args,
    )


def solution(mesh):
    return jax.shard_map(
        functools.partial(body, mesh.shape["chan"], mesh.shape["freq"]),
        mesh=mesh,
        in_specs=(P(None, None, "freq", "chan"), P(), P(None, None, "chan"), P()),
        out_specs=P("chan", None),
        check_vma=False,
    )
```

```python
import functools
import math

import jax
import jax.numpy as jnp
from jax import lax
from jax.experimental import pallas as pl
from jax.experimental.pallas import tpu as pltpu
from jax.sharding import PartitionSpec as P

F = 1024
NLAG = 256
BF = jnp.bfloat16
F32 = jnp.float32
I32 = jnp.int32
FB = 16
WROWS = 16
LANES = 128
SLACK = 6 * 1024 * 1024
PITCH = LANES + 9
TURN = 16
GROUPS = 16
GROUP = 8
ANY = pl.BlockSpec(memory_space=pl.ANY)
VMEM = pl.BlockSpec(memory_space=pltpu.VMEM)


def lag_basis(anchor, amount, totals, lag_count, windows):
    frequency = anchor + lax.iota(I32, amount)
    shifts = lax.iota(I32, lag_count) - lag_count // 2
    phases = frequency[:, None] * shifts[None, :] % (2 * totals)
    angles = phases.astype(F32) * (math.pi / totals)
    factor = 1.0 / math.sqrt(windows * totals)
    return jnp.cos(angles) * factor, -jnp.sin(angles) * factor


def params(*buffers):
    used = sum(math.prod(shape) * jnp.dtype(kind).itemsize for shape, kind in buffers)
    return pltpu.CompilerParams(vmem_limit_bytes=used + SLACK)


def iota(shape, dim):
    return lax.broadcasted_iota(I32, shape, dim)


def shift(values, size):
    return lax.shift_right_logical(values, jnp.int32(size.bit_length() - 1))


def as_column(row):
    size = row.shape[1]
    eye = iota((size, size), 0) == iota((size, size), 1)
    return jnp.sum(jnp.where(eye, row, 0), axis=1, keepdims=True)


def source_row(src_ref):
    return jnp.concatenate([src_ref[t : t + 1, :] for t in range(src_ref.shape[0])], axis=1)


def chip_ranks(row, per_chip):
    size = row.shape[1]
    own_row = shift(row, per_chip)
    col = as_column(row)
    own_col = shift(col, per_chip)
    same = own_col == own_row
    q0, q1 = iota((size, size), 0), iota((size, size), 1)
    rank_col = jnp.sum(jnp.where(same & (q1 < q0), 1, 0), axis=1, keepdims=True)
    rank_row = jnp.sum(jnp.where(same & (q0 < q1), 1, 0), axis=0, keepdims=True)
    return col, own_col, rank_col, own_row, rank_row


def frequency_first(rows):
    shape = (FB * WROWS, rows * FB)
    r, c = iota(shape, 0), iota(shape, 1)
    hit = (shift(r, WROWS) == (c & (FB - 1))) & ((r & (WROWS - 1)) == shift(c, FB))
    return jnp.where(hit, 1.0, 0.0).astype(BF)


def pick_kernel(cap, pieces, src_ref, spec_ref, keep_ref, send_ref, buf, keep_buf, send_buf, in_sem, out_sem):
    _, windows, freqs, chans = spec_ref.shape
    wp = windows // 2
    half = freqs // 2
    part = half // pieces
    groups = LANES // cap
    me = lax.axis_index("chan")
    core = me & 1
    chunks = in_sem.shape[0]
    wc = wp // chunks
    ins = []
    for j in range(chunks):
        for k in range(2):
            for w2 in range(2):
                at = pl.ds(w2 * wp + j * wc, wc)
                ins.append(pltpu.make_async_copy(spec_ref.at[k, at], buf.at[k, at], in_sem.at[j, 2 * k + w2]))
    for copy in ins:
        copy.start()

    row = source_row(src_ref)
    col, own_col, rank_col, _, _ = chip_ranks(row, 2 * chans)
    slots = row.shape[1]
    lane_r = iota((slots, LANES), 1) & (cap - 1)
    match = (own_col == shift(me, 2)) & (rank_col == lane_r)
    local = col - me * chans
    found = jnp.sum(jnp.where(match, local + 1, 0), axis=0, keepdims=True) - 1
    shape = (groups * chans, LANES)
    r, c = iota(shape, 0), iota(shape, 1)
    hit = (shift(r, chans) == shift(c, cap)) & ((r & (chans - 1)) == found)
    picker = jnp.where(hit, 1.0, 0.0).astype(BF)

    mine = pl.multiple_of(core * half, half)
    other = pl.multiple_of((1 - core) * half, half)
    outs = []
    for j in range(chunks):
        for copy in ins[4 * j : 4 * j + 4]:
            copy.wait()
        for i in range(wc):
            w = j * wc + i
            if groups == 4:
                turns, places = [[(w, 0), (w, 1), (wp + w, 0), (wp + w, 1)]], [w]
            else:
                turns, places = [[(w, 0), (w, 1)], [(wp + w, 0), (wp + w, 1)]], [w, wp + w]
            for start, dest in ((other, send_buf), (mine, keep_buf)):
                for turn, place in zip(turns, places):
                    left = jnp.concatenate([buf[k, ww, pl.ds(start, half), :] for ww, k in turn], axis=1)
                    got = jnp.dot(left, picker, preferred_element_type=F32).astype(BF)
                    for p in range(pieces):
                        dest[p, place] = got[p * part : (p + 1) * part]
        for h in range(4 // groups if groups < 4 else 1):
            at = pl.ds(h * wp + j * wc, wc)
            for n, (dest, ref) in enumerate(((send_buf, send_ref), (keep_buf, keep_ref))):
                outs.append(pltpu.make_async_copy(dest.at[:, at], ref.at[:, at], out_sem.at[j, 2 * h + n]))
                outs[-1].start()
    for copy in outs:
        copy.wait()


def pick(spectra, src_ids, cap, pieces):
    _, windows, freqs, chans = spectra.shape
    half = freqs // 2
    rows = windows * cap * 2 // LANES
    chunks = 5 if (windows // 2) % 5 == 0 else 1
    shape = (pieces, rows, half // pieces, LANES)
    out = jax.ShapeDtypeStruct(shape, BF)
    return pl.pallas_call(
        functools.partial(pick_kernel, cap, pieces),
        in_specs=[VMEM, ANY],
        out_specs=[ANY, ANY],
        out_shape=[out, out],
        scratch_shapes=[
            pltpu.VMEM(spectra.shape, BF),
            pltpu.VMEM(shape, BF),
            pltpu.VMEM(shape, BF),
            pltpu.SemaphoreType.DMA((chunks, 4)),
            pltpu.SemaphoreType.DMA((chunks, 4)),
        ],
        compiler_params=params((spectra.shape, BF), (shape, BF), (shape, BF)),
        name="pick_sources",
    )(src_ids, spectra)


def tables_kernel(
    nchan, spec_ref, got_ref, own_pairs, got_pairs, slot_ref, recv_ref, hot_ref, count_ref, own, got, named, tally, in_sem
):
    _, windows, half, chans = got.shape
    slots = own_pairs.shape[0]
    bins = slot_ref.shape[1]
    per = bins // nchan
    wp = windows // 2
    core = lax.axis_index("chan") & 1
    mine = pl.ds(pl.multiple_of(core * half, half), half)
    ins = []
    for k in range(2):
        ins.append(pltpu.make_async_copy(spec_ref.at[k, :, mine], own.at[k], in_sem.at[k, 0]))
        ins.append(pltpu.make_async_copy(got_ref.at[k, :, mine], got.at[k], in_sem.at[k, 1]))
    for copy in ins:
        copy.start()

    r = iota((bins, 1), 0)
    block, rest = shift(r, per), r & (per - 1)
    side, chip = shift(block, nchan // 2), block & (nchan // 2 - 1)
    order = (chip * 2 + side) * per + rest
    row_bin = jnp.sum(jnp.where(slot_ref[...] == order, iota((1, bins), 1), 0), axis=1, keepdims=True)
    named[...] = jnp.broadcast_to(row_bin, named.shape)
    tally[...] = jnp.zeros_like(tally)

    def one_step(step, carry):
        total = tally[...]
        for u in range(GROUP):
            s = step * GROUP + u
            bin_of = named[...]
            mine_hit = jnp.where(own_pairs[pl.ds(s, 1), :] == bin_of, 1.0, 0.0)
            hot_ref[s, :, pl.ds(0, chans)] = mine_hit.astype(BF)
            hot_ref[s, :, pl.ds(chans, chans)] = jnp.where(got_pairs[pl.ds(s, 1), :] == bin_of, 1.0, 0.0).astype(BF)
            total = total + mine_hit
        tally[...] = total
        return carry

    lax.fori_loop(0, slots // GROUP, one_step, 0)
    count_ref[...] = lax.dot_general(
        jnp.ones((8, chans), BF), tally[...].astype(BF), (((1,), (1,)), ((), ())), preferred_element_type=F32
    )

    turn = frequency_first(wp)
    for copy in ins:
        copy.wait()
    for b in range(half // FB):
        at = pl.ds(b * FB, FB)
        for k in range(2):
            for w2 in range(2):
                ws = pl.ds(w2 * wp, wp)
                both = jnp.concatenate([own[k, ws, at, :], got[k, ws, at, :]], axis=2).reshape(wp * FB, 2 * chans)
                moved = jnp.dot(turn, both, preferred_element_type=F32).astype(BF)
                recv_ref[at, pl.ds((2 * k + w2) * WROWS, WROWS), :] = moved.reshape(FB, WROWS, 2 * chans)


def tables(spectra, got, own_pairs, got_pairs, slot_of_bin, nchan):
    _, windows, freqs, chans = spectra.shape
    half = freqs // 2
    slots = own_pairs.shape[0]
    bins = slot_of_bin.shape[0]
    side = ((2, windows, half, chans), BF)
    square = ((bins, chans), I32)
    return pl.pallas_call(
        functools.partial(tables_kernel, nchan),
        in_specs=[ANY, ANY, VMEM, VMEM, VMEM],
        out_specs=[VMEM, VMEM, VMEM],
        out_shape=[
            jax.ShapeDtypeStruct((half, 4 * WROWS, 2 * chans), BF),
            jax.ShapeDtypeStruct((slots, bins, 2 * chans), BF),
            jax.ShapeDtypeStruct((8, bins), F32),
        ],
        scratch_shapes=[
            pltpu.VMEM(*side),
            pltpu.VMEM(*side),
            pltpu.VMEM(*square),
            pltpu.VMEM((bins, chans), F32),
            pltpu.SemaphoreType.DMA((2, 2)),
        ],
        compiler_params=params(side, side, square, square, ((bins, bins), I32)),
        name="tables",
    )(spectra, got, own_pairs, got_pairs, slot_of_bin[None, :])


def cross_kernel(cap, chips, pieces, *refs):
    src_ref, recv, hot, cos_ref, sin_ref, count_ref = refs[:6]
    xrefs = refs[6 : 6 + pieces * chips]
    refs = refs[6 + pieces * chips :]
    outs, refs = refs[:2], refs[2:]
    xs, cross, sums, whole = refs
    rows, part, _ = xrefs[0].shape
    count, _, chans2 = recv.shape
    slots, bins, _ = hot.shape
    wp = rows * LANES // (2 * cap) // 2
    groups = LANES // cap
    me = lax.axis_index("chan")
    row = source_row(src_ref)
    _, _, _, own_row, rank_row = chip_ranks(row, chans2)
    own_row = jnp.concatenate([own_row] * groups, axis=1)
    rank_row = jnp.concatenate([rank_row] * groups, axis=1)
    shape = (LANES, groups * slots)
    r, c = iota(shape, 0), iota(shape, 1)
    aligned = (shift(r, cap) == shift(c, slots)) & ((r & (cap - 1)) == rank_row)
    turn = frequency_first(wp)
    place = jnp.concatenate(
        [jnp.where(aligned & (own_row == (shift(me, 2) ^ d)), 1.0, 0.0).astype(BF) for d in range(chips)], axis=0
    )
    for p in range(pieces):
        for b in range(part // FB):
            at = pl.ds(b * FB, FB)
            sides = []
            for h in range(rows // wp):
                ws = pl.ds(h * wp, wp)
                got = jnp.concatenate([xrefs[p * chips + d][ws, at, :] for d in range(chips)], axis=2)
                got = got.reshape(wp * FB, chips * LANES)
                sides.append(jnp.dot(got, place, preferred_element_type=F32).astype(BF))
            moved = jnp.concatenate(sides, axis=1) if len(sides) > 1 else sides[0]
            xs[pl.ds((p * part + b * FB) * WROWS, FB * WROWS), :] = jnp.dot(turn, moved, preferred_element_type=F32)

    imag = iota((2 * WROWS, LANES), 1) >= slots
    quarter = shift(iota((1, 4 * 4 * WROWS), 1), 4 * WROWS)
    masks = [jnp.where(quarter == i, 1.0, 0.0).astype(BF) for i in range(4)]

    def one_group(step, carry):
        for sub in range(2 * min(GROUPS, count // 8)):
            g, q = step * min(GROUPS, count // 8) + sub // 2, sub % 2
            lefts = []
            for j in range(4 * q, 4 * q + 4):
                at = pl.ds(pl.multiple_of((g * 8 + j) * WROWS, WROWS), WROWS)
                x = xs[at, :]
                x = jnp.concatenate([x[:, :LANES], x[:, LANES:]], axis=0)
                upper = jnp.where(imag, -x, x)
                if j:
                    upper = pltpu.roll(upper, j, 1)
                lefts += [upper, pltpu.roll(x, slots + j, 1)]
            left = jnp.transpose(jnp.concatenate(lefts, axis=0)).astype(BF)
            left = jnp.concatenate([left * mask for mask in masks], axis=0)
            right = recv[pl.ds(g * 8 + 4 * q, 4)].reshape(4 * 4 * WROWS, chans2)
            got = jnp.dot(left, right, preferred_element_type=F32)
            for i in range(4):
                j = 4 * q + i
                base = pl.multiple_of(g * (8 * PITCH) + j * (PITCH - 1), 8)
                for h in range(2):
                    side = got[i * LANES : (i + 1) * LANES, h * LANES : (h + 1) * LANES]
                    cross[h, pl.ds(base, LANES), :] = side
                    if j:
                        cross[h, pl.ds(pl.multiple_of(base + LANES, 8), 8), :] = side[:8]
        return carry

    lax.fori_loop(0, count // (8 * min(GROUPS, count // 8)), one_group, 0)

    sums[...] = jnp.zeros_like(sums)

    def one_turn(step, carry):
        lefts = []
        for u in range(TURN):
            s = step * TURN + u
            parts = []
            for turn in range(2):
                at = pl.ds(s + turn * slots, count, stride=PITCH)
                parts.append(jnp.concatenate([cross[0, at, :], cross[1, at, :]], axis=1))
            x = jnp.concatenate(parts, axis=0)
            high = x.astype(BF)
            low = (x - high.astype(F32)).astype(BF)
            lefts.append(jnp.concatenate([high, low], axis=0))
        left = jnp.concatenate(lefts, axis=1)
        right = jnp.concatenate([hot[step * TURN + u] for u in range(TURN)], axis=1)
        sums[...] += lax.dot_general(left, right, (((1,), (1,)), ((), ())), preferred_element_type=F32)
        return carry

    lax.fori_loop(0, slots // TURN, one_turn, 0)
    total = sums[pl.ds(0, 2 * count), :] + sums[pl.ds(2 * count, 2 * count), :]
    table = jnp.concatenate([cos_ref[...], sin_ref[...]], axis=0)
    whole[...] = lax.dot_general(total, table, (((0,), (0,)), ((), ())), precision=lax.Precision.HIGHEST, preferred_element_type=F32)
    core = me & 1
    blocks, padded, lags = outs[0].shape
    per = bins // (2 * blocks)
    crows = count_ref.shape[0]
    for which, dest in ((core, outs[0]), (1 - core, outs[1])):
        for d in range(blocks):
            start = pl.multiple_of((which * blocks + d) * per, per)
            dest[d, pl.ds(0, per), :] = whole[pl.ds(start, per), :]
            dest[d, pl.ds(per, crows), :] = count_ref[...]


def cross_and_bin(arrays, src_ids, recv, hot, counts, cos, sin, cap, nchan):
    pieces, chips = len(arrays), len(arrays[0])
    rows, part, _ = arrays[0][0].shape
    _, bins, chans2 = hot.shape
    lags = cos.shape[1]
    count = pieces * part
    per = bins // nchan
    out = jax.ShapeDtypeStruct((nchan // 2, per + 8, lags), F32)
    operands = [((pieces, chips, rows, part, LANES), BF), (recv.shape, BF), (hot.shape, BF)]
    buffers = [
        ((count * WROWS, 2 * LANES), F32),
        ((2, count * PITCH + 8, chans2 // 2), F32),
        ((4 * count, bins), F32),
        ((bins, lags), F32),
    ]
    return pl.pallas_call(
        functools.partial(cross_kernel, cap, chips, pieces),
        in_specs=[VMEM] * (6 + pieces * chips),
        out_specs=[VMEM, VMEM],
        out_shape=[out, out],
        scratch_shapes=[pltpu.VMEM(shape, kind) for shape, kind in buffers],
        compiler_params=params(*buffers),
        name="cross_and_bin",
    )(src_ids, recv, hot, cos, sin, counts, *[x for held in arrays for x in held])


def swap(x, size, bit):
    return lax.ppermute(x, "chan", [(i, i ^ bit) for i in range(size)])


def sums(nchan, nfreq, cap, spectra, src_ids, pair_bin, slot_of_bin):
    _, windows, freqs, chans = spectra.shape
    half = freqs // 2
    bins = slot_of_bin.shape[0]
    slots = src_ids.shape[0] * src_ids.shape[1]
    me = lax.axis_index("chan")
    core = me & 1
    rest = [1 << k for k in range(1, nchan.bit_length() - 1)]
    pieces = 2

    pairs_own = pair_bin.reshape(slots, chans)
    got_pairs = swap(pairs_own, nchan, 1)
    keep, send = pick(spectra, src_ids, cap, pieces)
    got = swap(send, nchan, 1)
    spectra_sent, got, got_pairs = lax.optimization_barrier((spectra, got, got_pairs))
    got_spec = swap(spectra_sent, nchan, 1)
    chip = [keep[p] + got[p] for p in range(pieces)]
    orders = [rest if p % 2 == 0 else rest[::-1] for p in range(pieces)]
    arrays, routes = [[x] for x in chip], [[0] for _ in chip]
    early = [[] for _ in chip]
    for hop in range(len(rest)):
        if hop == len(rest) - 1:
            early = [[swap(chip[p], nchan, orders[p][hop])] for p in range(pieces)]
        for p in range(pieces):
            bit = orders[p][hop]
            arrays[p] = arrays[p] + early[p] + [swap(x, nchan, bit) for x in arrays[p][len(early[p]) :]]
            routes[p] = routes[p] + [name ^ bit for name in routes[p]]

    recv, hot, counts = tables(spectra, got_spec, pairs_own, got_pairs, slot_of_bin, nchan)
    cos, sin = lag_basis(lax.axis_index("freq") * freqs + core * half, half, F, NLAG, windows)
    counts = counts[0].reshape(bins // NLAG, NLAG)
    arrays = [[held[names.index(2 * d)] for d in range(len(held))] for held, names in zip(arrays, routes)]
    out = cross_and_bin(arrays, src_ids, recv, hot, counts, cos, sin, cap, nchan)
    mine, other = out

    per = bins // nchan
    mine = mine + swap(other, nchan, 1)
    at = me // 2
    if nchan // 2 <= 4:
        total = lax.dynamic_index_in_dim(mine, at, 0, keepdims=False)
        for move in range(1, nchan // 2):
            total = total + swap(lax.dynamic_index_in_dim(mine, at ^ move, 0, keepdims=False), nchan, 2 * move)
    else:
        for bit in rest[::-1]:
            size = mine.shape[0] // 2
            up = (me & bit) != 0
            low, high = mine[:size], mine[size:]
            mine = jnp.where(up, high, low) + swap(jnp.where(up, low, high), nchan, bit)
        total = mine[0]
    owned = total[:per]
    parts = [owned]
    if nfreq <= 4:
        parts += [lax.ppermute(owned, "freq", [(i, i ^ k) for i in range(nfreq)]) for k in range(nfreq - 1, 0, -1)]
    else:
        for k in range(nfreq.bit_length() - 1):
            owned = parts[0]
            parts = [owned + lax.ppermute(owned, "freq", [(i, i ^ (1 << k)) for i in range(nfreq)])]
    counted = total[per : per + bins // NLAG].reshape(bins)
    count = lax.dynamic_slice(counted, ((core * (nchan // 2) + at) * per,), (per,))
    return parts, count


def scaled(parts, count):
    total = parts[0]
    for part in parts[1:]:
        total = total + part
    return total / jnp.sqrt(jnp.maximum(count, 1.0))[:, None]


def body(nchan, nfreq, spectra, src_ids, pair_bin, slot_of_bin):
    args = (spectra, src_ids, pair_bin, slot_of_bin)
    slots = src_ids.shape[0] * src_ids.shape[1]
    cap = slots // 2
    owner = src_ids.reshape(-1) // (2 * spectra.shape[3])
    loads = jnp.sum((owner[None, :] == lax.iota(I32, nchan // 2)[:, None]).astype(I32), axis=1)
    fits = jnp.max(loads) <= cap
    parts, count = sums(nchan, nfreq, cap, *args)
    return lax.cond(
        fits,
        lambda parts, count, *args: scaled(parts, count),
        lambda parts, count, *args: scaled(*sums(nchan, nfreq, slots, *args)),
        parts,
        count,
        *args,
    )


def solution(mesh):
    return jax.shard_map(
        functools.partial(body, mesh.shape["chan"], mesh.shape["freq"]),
        mesh=mesh,
        in_specs=(P(None, None, "freq", "chan"), P(), P(None, None, "chan"), P()),
        out_specs=P("chan", None),
        check_vma=False,
    )
```

```python
import functools
import math

import jax
import jax.numpy as jnp
from jax import lax
from jax.experimental import pallas as pl
from jax.experimental.pallas import tpu as pltpu
from jax.sharding import PartitionSpec as P

F = 1024
NLAG = 256
BF = jnp.bfloat16
F32 = jnp.float32
I32 = jnp.int32
FB = 16
WROWS = 16
LANES = 128
SLACK = 6 * 1024 * 1024
PITCH = LANES + 9
TURN = 16
BIG = 8 * 1024 * 1024
CAP = 25
PACK = 2 * LANES
XPITCH = 2 * WROWS + 1
GROUPS = 16
GROUP = 8
ANY = pl.BlockSpec(memory_space=pl.ANY)
VMEM = pl.BlockSpec(memory_space=pltpu.VMEM)


def lag_basis(anchor, amount, totals, lag_count, windows):
    frequency = anchor + lax.iota(I32, amount)
    shifts = lax.iota(I32, lag_count) - lag_count // 2
    phases = frequency[:, None] * shifts[None, :] % (2 * totals)
    angles = phases.astype(F32) * (math.pi / totals)
    factor = 1.0 / math.sqrt(windows * totals)
    return jnp.cos(angles) * factor, -jnp.sin(angles) * factor


def params(*buffers):
    used = sum(math.prod(shape) * jnp.dtype(kind).itemsize for shape, kind in buffers)
    return pltpu.CompilerParams(vmem_limit_bytes=used + SLACK)


def iota(shape, dim):
    return lax.broadcasted_iota(I32, shape, dim)


def shift(values, size):
    return lax.shift_right_logical(values, jnp.int32(size.bit_length() - 1))


def as_column(row):
    size = row.shape[1]
    eye = iota((size, size), 0) == iota((size, size), 1)
    return jnp.sum(jnp.where(eye, row, 0), axis=1, keepdims=True)


def source_row(src_ref):
    return jnp.concatenate([src_ref[t : t + 1, :] for t in range(src_ref.shape[0])], axis=1)


def chip_ranks(row, per_chip):
    size = row.shape[1]
    own_row = shift(row, per_chip)
    col = as_column(row)
    own_col = shift(col, per_chip)
    same = own_col == own_row
    q0, q1 = iota((size, size), 0), iota((size, size), 1)
    rank_col = jnp.sum(jnp.where(same & (q1 < q0), 1, 0), axis=1, keepdims=True)
    rank_row = jnp.sum(jnp.where(same & (q0 < q1), 1, 0), axis=0, keepdims=True)
    return col, own_col, rank_col, own_row, rank_row


def packed(cap, shape, dim):
    lane = iota(shape, dim)
    group = jnp.zeros(shape, I32)
    for j in range(1, PACK // cap + 1):
        group = group + jnp.where(lane >= j * cap, 1, 0)
    return group, lane - group * cap


def frequency_first(rows):
    shape = (FB * WROWS, rows * FB)
    r, c = iota(shape, 0), iota(shape, 1)
    hit = (shift(r, WROWS) == (c & (FB - 1))) & ((r & (WROWS - 1)) == shift(c, FB))
    return jnp.where(hit, 1.0, 0.0).astype(BF)


def pick_kernel(cap, src_ref, spec_ref, keep_ref, send_ref, buf, res, in_sem, out_sem):
    _, _, freqs, chans = spec_ref.shape
    half = freqs // 2
    wg = PACK // (2 * cap)
    groups = in_sem.shape[0]
    me = lax.axis_index("chan")
    core = me & 1
    ins = []
    for b in range(groups):
        for k in range(2):
            at = pl.ds(b * wg, wg)
            ins.append(pltpu.make_async_copy(spec_ref.at[k, at], buf.at[k, at], in_sem.at[b, k]))
    for copy in ins:
        copy.start()

    row = source_row(src_ref)
    col, own_col, rank_col, _, _ = chip_ranks(row, 2 * chans)
    slots = row.shape[1]
    _, lane_r = packed(cap, (slots, PACK), 1)
    match = (own_col == shift(me, 2)) & (rank_col == lane_r)
    local = col - me * chans
    found = jnp.sum(jnp.where(match, local + 1, 0), axis=0, keepdims=True) - 1
    shape = (2 * wg * chans, PACK)
    lane_g, _ = packed(cap, (1, PACK), 1)
    r = iota(shape, 0)
    picker = jnp.where((shift(r, chans) == lane_g) & ((r & (chans - 1)) == found), 1.0, 0.0).astype(BF)

    mine = pl.multiple_of(core * half, half)
    other = pl.multiple_of((1 - core) * half, half)
    outs = []
    turn = 2 if groups % 2 == 0 else 1
    for b0 in range(0, groups, turn):
        lefts = []
        for b in range(b0, b0 + turn):
            for copy in ins[2 * b : 2 * b + 2]:
                copy.wait()
            lefts.append(jnp.concatenate([buf[k, b * wg + i] for i in range(wg) for k in range(2)], axis=1))
        left = jnp.concatenate(lefts, axis=0)
        got = jnp.dot(left, picker, preferred_element_type=F32).astype(BF)
        for b in range(b0, b0 + turn):
            res[b] = got[(b - b0) * freqs : (b - b0 + 1) * freqs]
        for n, (start, ref) in enumerate(((other, send_ref), (mine, keep_ref))):
            at = pl.ds(b0, turn)
            outs.append(pltpu.make_async_copy(res.at[at, pl.ds(start, half)], ref.at[at], out_sem.at[b0, n]))
            outs[-1].start()
    for copy in outs:
        copy.wait()


def pick(spectra, src_ids, cap):
    _, windows, freqs, chans = spectra.shape
    half = freqs // 2
    groups = windows // (PACK // (2 * cap))
    shape = (groups, half, PACK)
    out = jax.ShapeDtypeStruct(shape, BF)
    return pl.pallas_call(
        functools.partial(pick_kernel, cap),
        in_specs=[VMEM, ANY],
        out_specs=[ANY, ANY],
        out_shape=[out, out],
        scratch_shapes=[
            pltpu.VMEM(spectra.shape, BF),
            pltpu.VMEM((groups, freqs, PACK), BF),
            pltpu.SemaphoreType.DMA((groups, 2)),
            pltpu.SemaphoreType.DMA((groups, 2)),
        ],
        compiler_params=params((spectra.shape, BF), (shape, BF), (shape, BF)),
        name="pick_sources",
    )(src_ids, spectra)


def tables_kernel(
    nchan, spec_ref, got_ref, own_pairs, got_pairs, slot_ref, recv_ref, hot_ref, count_ref, own, got, named, tally, in_sem
):
    _, windows, half, chans = got.shape
    slots = own_pairs.shape[0]
    bins = slot_ref.shape[1]
    per = bins // nchan
    wp = windows // 2
    core = lax.axis_index("chan") & 1
    mine = pl.ds(pl.multiple_of(core * half, half), half)
    ins = []
    for k in range(2):
        ins.append(pltpu.make_async_copy(spec_ref.at[k, :, mine], own.at[k], in_sem.at[k, 0]))
        ins.append(pltpu.make_async_copy(got_ref.at[k, :, mine], got.at[k], in_sem.at[k, 1]))
    for copy in ins:
        copy.start()

    r = iota((bins, 1), 0)
    block, rest = shift(r, per), r & (per - 1)
    side, chip = shift(block, nchan // 2), block & (nchan // 2 - 1)
    order = (chip * 2 + side) * per + rest
    row_bin = jnp.sum(jnp.where(slot_ref[...] == order, iota((1, bins), 1), 0), axis=1, keepdims=True)
    named[...] = jnp.broadcast_to(row_bin, named.shape)
    tally[...] = jnp.zeros_like(tally)

    def one_step(step, carry):
        total = tally[...]
        for u in range(GROUP):
            s = step * GROUP + u
            bin_of = named[...]
            mine_hit = jnp.where(own_pairs[pl.ds(s, 1), :] == bin_of, 1.0, 0.0)
            hot_ref[s, :, pl.ds(0, chans)] = mine_hit.astype(BF)
            hot_ref[s, :, pl.ds(chans, chans)] = jnp.where(got_pairs[pl.ds(s, 1), :] == bin_of, 1.0, 0.0).astype(BF)
            total = total + mine_hit
        tally[...] = total
        return carry

    lax.fori_loop(0, slots // GROUP, one_step, 0)
    count_ref[...] = lax.dot_general(
        jnp.ones((8, chans), BF), tally[...].astype(BF), (((1,), (1,)), ((), ())), preferred_element_type=F32
    )

    turn = frequency_first(wp)
    for copy in ins:
        copy.wait()
    for b in range(half // FB):
        at = pl.ds(b * FB, FB)
        for k in range(2):
            for w2 in range(2):
                ws = pl.ds(w2 * wp, wp)
                both = jnp.concatenate([own[k, ws, at, :], got[k, ws, at, :]], axis=2).reshape(wp * FB, 2 * chans)
                moved = jnp.dot(turn, both, preferred_element_type=F32).astype(BF)
                recv_ref[at, pl.ds((2 * k + w2) * WROWS, WROWS), :] = moved.reshape(FB, WROWS, 2 * chans)


def tables(spectra, got, own_pairs, got_pairs, slot_of_bin, nchan):
    _, windows, freqs, chans = spectra.shape
    half = freqs // 2
    slots = own_pairs.shape[0]
    bins = slot_of_bin.shape[0]
    side = ((2, windows, half, chans), BF)
    square = ((bins, chans), I32)
    return pl.pallas_call(
        functools.partial(tables_kernel, nchan),
        in_specs=[ANY, ANY, VMEM, VMEM, VMEM],
        out_specs=[VMEM, VMEM, VMEM],
        out_shape=[
            jax.ShapeDtypeStruct((half, 4 * WROWS, 2 * chans), BF),
            jax.ShapeDtypeStruct((slots, bins, 2 * chans), BF),
            jax.ShapeDtypeStruct((8, bins), F32),
        ],
        scratch_shapes=[
            pltpu.VMEM(*side),
            pltpu.VMEM(*side),
            pltpu.VMEM(*square),
            pltpu.VMEM((bins, chans), F32),
            pltpu.SemaphoreType.DMA((2, 2)),
        ],
        compiler_params=params(side, side, square, square, ((bins, bins), I32)),
        name="tables",
    )(spectra, got, own_pairs, got_pairs, slot_of_bin[None, :])


def cross_kernel(cap, chips, pieces, *refs):
    src_ref, recv, hot, cos_ref, sin_ref, count_ref = refs[:6]
    xrefs = refs[6 : 6 + pieces * chips]
    refs = refs[6 + pieces * chips :]
    outs, refs = refs[:2], refs[2:]
    xs, cross, sums, whole = refs
    groups, part, _ = xrefs[0].shape
    count, _, chans2 = recv.shape
    slots, bins, _ = hot.shape
    wg = PACK // (2 * cap)
    wp = groups * wg // 2

    me = lax.axis_index("chan")
    row = source_row(src_ref)
    _, _, _, own_row, rank_row = chip_ranks(row, chans2)
    own_row = jnp.concatenate([own_row] * (2 * wg), axis=1)
    rank_row = jnp.concatenate([rank_row] * (2 * wg), axis=1)
    lane_g, lane_r = packed(cap, (PACK, 1), 0)
    wide = 2 * wg * slots
    aligned = (lane_g == shift(iota((1, wide), 1), slots)) & (lane_r == rank_row)
    place = jnp.concatenate(
        [jnp.where(aligned & (own_row == (shift(me, 2) ^ d)), 1.0, 0.0).astype(BF) for d in range(chips)], axis=0
    )
    for p in range(pieces):
        got = jnp.concatenate([xrefs[p * chips + d][...] for d in range(chips)], axis=2)
        got = jnp.dot(got.reshape(groups * part, chips * PACK), place, preferred_element_type=F32)
        for w in range(2 * wp):
            b, i = w // wg, w % wg
            at = pl.ds(p * part * XPITCH + (w // wp) * WROWS + w % wp, part, stride=XPITCH)
            xs[at, :] = got[b * part : (b + 1) * part, i * LANES : (i + 1) * LANES]
        for w2 in range(2):
            for w in range(wp, WROWS):
                at = pl.ds(p * part * XPITCH + w2 * WROWS + w, part, stride=XPITCH)
                xs[at, :] = jnp.zeros((part, LANES), F32)

    imag = iota((2 * WROWS, LANES), 1) >= slots
    quarter = shift(iota((1, 4 * 4 * WROWS), 1), 4 * WROWS)
    masks = [jnp.where(quarter == i, 1.0, 0.0).astype(BF) for i in range(4)]

    def one_group(step, carry):
        for sub in range(2 * min(GROUPS, count // 8)):
            g, q = step * min(GROUPS, count // 8) + sub // 2, sub % 2
            lefts = []
            for j in range(4 * q, 4 * q + 4):
                x = xs[pl.ds((g * 8 + j) * XPITCH, 2 * WROWS), :]
                upper = jnp.where(imag, -x, x)
                if j:
                    upper = pltpu.roll(upper, j, 1)
                lefts += [upper, pltpu.roll(x, slots + j, 1)]
            left = jnp.transpose(jnp.concatenate(lefts, axis=0)).astype(BF)
            left = jnp.concatenate([left * mask for mask in masks], axis=0)
            right = recv[pl.ds(g * 8 + 4 * q, 4)].reshape(4 * 4 * WROWS, chans2)
            got = jnp.dot(left, right, preferred_element_type=F32)
            for i in range(4):
                j = 4 * q + i
                base = pl.multiple_of(g * (8 * PITCH) + j * (PITCH - 1), 8)
                for h in range(2):
                    side = got[i * LANES : (i + 1) * LANES, h * LANES : (h + 1) * LANES]
                    cross[h, pl.ds(base, LANES), :] = side
                    if j:
                        cross[h, pl.ds(pl.multiple_of(base + LANES, 8), 8), :] = side[:8]
        return carry

    lax.fori_loop(0, count // (8 * min(GROUPS, count // 8)), one_group, 0)

    sums[...] = jnp.zeros_like(sums)

    def one_turn(step, carry):
        lefts = []
        for u in range(TURN):
            s = step * TURN + u
            parts = []
            for turn in range(2):
                at = pl.ds(s + turn * slots, count, stride=PITCH)
                parts.append(jnp.concatenate([cross[0, at, :], cross[1, at, :]], axis=1))
            x = jnp.concatenate(parts, axis=0)
            high = x.astype(BF)
            low = (x - high.astype(F32)).astype(BF)
            lefts.append(jnp.concatenate([high, low], axis=0))
        left = jnp.concatenate(lefts, axis=1)
        right = jnp.concatenate([hot[step * TURN + u] for u in range(TURN)], axis=1)
        sums[...] += lax.dot_general(left, right, (((1,), (1,)), ((), ())), preferred_element_type=F32)
        return carry

    lax.fori_loop(0, slots // TURN, one_turn, 0)
    total = sums[pl.ds(0, 2 * count), :] + sums[pl.ds(2 * count, 2 * count), :]
    table = jnp.concatenate([cos_ref[...], sin_ref[...]], axis=0)
    whole[...] = lax.dot_general(total, table, (((0,), (0,)), ((), ())), precision=lax.Precision.HIGHEST, preferred_element_type=F32)
    core = me & 1
    blocks, padded, lags = outs[0].shape
    per = bins // (2 * blocks)
    crows = count_ref.shape[0]
    for which, dest in ((core, outs[0]), (1 - core, outs[1])):
        for d in range(blocks):
            start = pl.multiple_of((which * blocks + d) * per, per)
            dest[d, pl.ds(0, per), :] = whole[pl.ds(start, per), :]
            dest[d, pl.ds(per, crows), :] = count_ref[...]


def cross_and_bin(arrays, src_ids, recv, hot, counts, cos, sin, cap, nchan):
    pieces, chips = len(arrays), len(arrays[0])
    groups, part, _ = arrays[0][0].shape
    _, bins, chans2 = hot.shape
    lags = cos.shape[1]
    count = pieces * part
    per = bins // nchan
    out = jax.ShapeDtypeStruct((nchan // 2, per + 8, lags), F32)
    buffers = [
        ((count * XPITCH + 8, LANES), F32),
        ((groups * part, 4 * PACK), F32),
        ((chips * PACK, 4 * PACK), F32),
        ((2, count * PITCH + 8, chans2 // 2), F32),
        ((4 * count, bins), F32),
        ((bins, lags), F32),
    ]
    scratch = [buffers[0]] + buffers[3:]
    return pl.pallas_call(
        functools.partial(cross_kernel, cap, chips, pieces),
        in_specs=[VMEM] * (6 + pieces * chips),
        out_specs=[VMEM, VMEM],
        out_shape=[out, out],
        scratch_shapes=[pltpu.VMEM(shape, kind) for shape, kind in scratch],
        compiler_params=params(*buffers, *([(hot.shape, BF)] if hot.size > BIG else [])),
        name="cross_and_bin",
    )(src_ids, recv, hot, cos, sin, counts, *[x for held in arrays for x in held])


def swap(x, size, bit):
    return lax.ppermute(x, "chan", [(i, i ^ bit) for i in range(size)])


def gathered(nchan, pieces, chip):
    rest = [1 << k for k in range(1, nchan.bit_length() - 1)]
    result = []
    held = [[x] for x in chip]
    names = [[0] for _ in chip]
    for hop in range(len(rest)):
        bits = [rest[hop] if p % 2 == 0 else rest[-1 - hop] for p in range(pieces)]
        early = [swap(chip[p], nchan, bits[p]) for p in range(pieces)]
        for p, bit in enumerate(bits):
            held[p] = held[p] + [early[p]] + [swap(x, nchan, bit) for x in held[p][1:]]
            names[p] = names[p] + [name ^ bit for name in names[p]]
    for p in range(pieces):
        result.append([held[p][names[p].index(2 * d)] for d in range(len(held[p]))])
    return result


def chip_sources(nchan, cap, pieces, spectra, src_ids):
    keep, send = pick(spectra, src_ids, cap)
    got = swap(send, nchan, 1)
    part = keep.shape[1] // pieces
    return [keep[:, p * part : (p + 1) * part] + got[:, p * part : (p + 1) * part] for p in range(pieces)]


def finish(nchan, nfreq, cap, chip, spectra, src_ids, pairs_own, got_pairs, slot_of_bin):
    _, windows, freqs, chans = spectra.shape
    half = freqs // 2
    bins = slot_of_bin.shape[0]
    me = lax.axis_index("chan")
    core = me & 1
    rest = [1 << k for k in range(1, nchan.bit_length() - 1)]
    arrays = gathered(nchan, len(chip), chip)
    spectra_sent, chip = lax.optimization_barrier((spectra, chip))
    got_spec = swap(spectra_sent, nchan, 1)
    recv, hot, counts = tables(spectra, got_spec, pairs_own, got_pairs, slot_of_bin, nchan)
    cos, sin = lag_basis(lax.axis_index("freq") * freqs + core * half, half, F, NLAG, windows)
    counts = counts[0].reshape(bins // NLAG, NLAG)
    out = cross_and_bin(arrays, src_ids, recv, hot, counts, cos, sin, cap, nchan)
    mine, other = out

    per = bins // nchan
    mine = mine + swap(other, nchan, 1)
    at = me // 2
    if nchan // 2 <= 4:
        total = lax.dynamic_index_in_dim(mine, at, 0, keepdims=False)
        for move in range(1, nchan // 2):
            total = total + swap(lax.dynamic_index_in_dim(mine, at ^ move, 0, keepdims=False), nchan, 2 * move)
    else:
        for bit in rest[::-1]:
            size = mine.shape[0] // 2
            up = (me & bit) != 0
            low, high = mine[:size], mine[size:]
            mine = jnp.where(up, high, low) + swap(jnp.where(up, low, high), nchan, bit)
        total = mine[0]
    owned = total[:per]
    parts = [owned]
    if nfreq <= 4:
        parts += [lax.ppermute(owned, "freq", [(i, i ^ k) for i in range(nfreq)]) for k in range(nfreq - 1, 0, -1)]
    else:
        for k in range(nfreq.bit_length() - 1):
            owned = parts[0]
            parts = [owned + lax.ppermute(owned, "freq", [(i, i ^ (1 << k)) for i in range(nfreq)])]
    counted = total[per : per + bins // NLAG].reshape(bins)
    count = lax.dynamic_slice(counted, ((core * (nchan // 2) + at) * per,), (per,))
    return parts, count


def scaled(parts, count):
    total = parts[0]
    for part in parts[1:]:
        total = total + part
    return total / jnp.sqrt(jnp.maximum(count, 1.0))[:, None]


def body(nchan, nfreq, spectra, src_ids, pair_bin, slot_of_bin):
    chans = spectra.shape[3]
    slots = src_ids.shape[0] * src_ids.shape[1]
    pieces = 2
    pairs_own = pair_bin.reshape(slots, chans)
    got_pairs = swap(pairs_own, nchan, 1)
    chip = lax.optimization_barrier(chip_sources(nchan, CAP, pieces, spectra, src_ids))
    owner = src_ids // (2 * chans)
    loads = jnp.sum((owner[None] == lax.iota(I32, nchan // 2)[:, None, None]).astype(I32), axis=(1, 2))
    fits = jnp.max(loads) <= CAP

    def small(parts, count, *args):
        return scaled(parts, count)

    def large(parts, count, *args):
        chip = chip_sources(nchan, slots, pieces, *args[:2])
        return scaled(*finish(nchan, nfreq, slots, chip, *args))

    args = (spectra, src_ids, pairs_own, got_pairs, slot_of_bin)
    parts, count = finish(nchan, nfreq, CAP, chip, *args)
    return lax.cond(fits, small, large, parts, count, *args)


def solution(mesh):
    return jax.shard_map(
        functools.partial(body, mesh.shape["chan"], mesh.shape["freq"]),
        mesh=mesh,
        in_specs=(P(None, None, "freq", "chan"), P(), P(None, None, "chan"), P()),
        out_specs=P("chan", None),
        check_vma=False,
    )
```

```python
import functools
import math

import jax
import jax.numpy as jnp
from jax import lax
from jax.experimental import pallas as pl
from jax.experimental.pallas import tpu as pltpu
from jax.sharding import PartitionSpec as P

F = 1024
NLAG = 256
BF = jnp.bfloat16
F32 = jnp.float32
I32 = jnp.int32
FB = 16
WROWS = 16
LANES = 128
SLACK = 6 * 1024 * 1024
PITCH = LANES + 9
TURN = 16
BIG = 8 * 1024 * 1024
CAP = 25
PACK = 2 * LANES
XPITCH = 2 * WROWS + 1
GROUPS = 16
GROUP = 8
ANY = pl.BlockSpec(memory_space=pl.ANY)
VMEM = pl.BlockSpec(memory_space=pltpu.VMEM)


def lag_basis(anchor, amount, totals, lag_count, windows):
    frequency = anchor + lax.iota(I32, amount)
    shifts = lax.iota(I32, lag_count) - lag_count // 2
    phases = frequency[:, None] * shifts[None, :] % (2 * totals)
    angles = phases.astype(F32) * (math.pi / totals)
    factor = 1.0 / math.sqrt(windows * totals)
    return jnp.cos(angles) * factor, -jnp.sin(angles) * factor


def params(*buffers):
    used = sum(math.prod(shape) * jnp.dtype(kind).itemsize for shape, kind in buffers)
    return pltpu.CompilerParams(vmem_limit_bytes=used + SLACK)


def iota(shape, dim):
    return lax.broadcasted_iota(I32, shape, dim)


def shift(values, size):
    return lax.shift_right_logical(values, jnp.int32(size.bit_length() - 1))


def as_column(row):
    size = row.shape[1]
    eye = iota((size, size), 0) == iota((size, size), 1)
    return jnp.sum(jnp.where(eye, row, 0), axis=1, keepdims=True)


def source_row(src_ref):
    return jnp.concatenate([src_ref[t : t + 1, :] for t in range(src_ref.shape[0])], axis=1)


def chip_ranks(row, per_chip):
    size = row.shape[1]
    own_row = shift(row, per_chip)
    col = as_column(row)
    own_col = shift(col, per_chip)
    same = own_col == own_row
    q0, q1 = iota((size, size), 0), iota((size, size), 1)
    rank_col = jnp.sum(jnp.where(same & (q1 < q0), 1, 0), axis=1, keepdims=True)
    rank_row = jnp.sum(jnp.where(same & (q0 < q1), 1, 0), axis=0, keepdims=True)
    return col, own_col, rank_col, own_row, rank_row


def packed(cap, shape, dim):
    lane = iota(shape, dim)
    group = jnp.zeros(shape, I32)
    for j in range(1, PACK // cap + 1):
        group = group + jnp.where(lane >= j * cap, 1, 0)
    return group, lane - group * cap


def frequency_first(rows):
    shape = (FB * WROWS, rows * FB)
    r, c = iota(shape, 0), iota(shape, 1)
    hit = (shift(r, WROWS) == (c & (FB - 1))) & ((r & (WROWS - 1)) == shift(c, FB))
    return jnp.where(hit, 1.0, 0.0).astype(BF)


def pick_kernel(cap, src_ref, spec_ref, keep_ref, send_ref, buf, res, in_sem, out_sem):
    _, _, freqs, chans = spec_ref.shape
    half = freqs // 2
    wg = PACK // (2 * cap)
    groups = in_sem.shape[0]
    me = lax.axis_index("chan")
    core = me & 1
    ins = []
    for b in range(groups):
        for k in range(2):
            at = pl.ds(b * wg, wg)
            ins.append(pltpu.make_async_copy(spec_ref.at[k, at], buf.at[k, at], in_sem.at[b, k]))
    for copy in ins:
        copy.start()

    row = source_row(src_ref)
    col, own_col, rank_col, _, _ = chip_ranks(row, 2 * chans)
    slots = row.shape[1]
    _, lane_r = packed(cap, (slots, PACK), 1)
    match = (own_col == shift(me, 2)) & (rank_col == lane_r)
    local = col - me * chans
    found = jnp.sum(jnp.where(match, local + 1, 0), axis=0, keepdims=True) - 1
    shape = (2 * wg * chans, PACK)
    lane_g, _ = packed(cap, (1, PACK), 1)
    r = iota(shape, 0)
    picker = jnp.where((shift(r, chans) == lane_g) & ((r & (chans - 1)) == found), 1.0, 0.0).astype(BF)

    mine = pl.multiple_of(core * half, half)
    other = pl.multiple_of((1 - core) * half, half)
    outs = []
    turn = 2 if groups % 2 == 0 else 1
    for b0 in range(0, groups, turn):
        lefts = []
        for b in range(b0, b0 + turn):
            for copy in ins[2 * b : 2 * b + 2]:
                copy.wait()
            lefts.append(jnp.concatenate([buf[k, b * wg + i] for i in range(wg) for k in range(2)], axis=1))
        left = jnp.concatenate(lefts, axis=0)
        got = jnp.dot(left, picker, preferred_element_type=F32).astype(BF)
        for b in range(b0, b0 + turn):
            res[b] = got[(b - b0) * freqs : (b - b0 + 1) * freqs]
        for n, (start, ref) in enumerate(((other, send_ref), (mine, keep_ref))):
            at = pl.ds(b0, turn)
            outs.append(pltpu.make_async_copy(res.at[at, pl.ds(start, half)], ref.at[at], out_sem.at[b0, n]))
            outs[-1].start()
    for copy in outs:
        copy.wait()


def pick(spectra, src_ids, cap):
    _, windows, freqs, chans = spectra.shape
    half = freqs // 2
    groups = windows // (PACK // (2 * cap))
    shape = (groups, half, PACK)
    out = jax.ShapeDtypeStruct(shape, BF)
    return pl.pallas_call(
        functools.partial(pick_kernel, cap),
        in_specs=[VMEM, ANY],
        out_specs=[ANY, ANY],
        out_shape=[out, out],
        scratch_shapes=[
            pltpu.VMEM(spectra.shape, BF),
            pltpu.VMEM((groups, freqs, PACK), BF),
            pltpu.SemaphoreType.DMA((groups, 2)),
            pltpu.SemaphoreType.DMA((groups, 2)),
        ],
        compiler_params=params((spectra.shape, BF), (shape, BF), (shape, BF)),
        name="pick_sources",
    )(src_ids, spectra)


def place_sources(cap, names, src_ref, per_chip, xrefs, xs):
    chips = len(names)
    groups, part, _ = xrefs[0].shape
    wg = PACK // (2 * cap)
    wp = groups * wg // 2
    me = lax.axis_index("chan")
    row = source_row(src_ref)
    slots = row.shape[1]
    _, _, _, own_row, rank_row = chip_ranks(row, per_chip)
    own_row = jnp.concatenate([own_row] * (2 * wg), axis=1)
    rank_row = jnp.concatenate([rank_row] * (2 * wg), axis=1)
    lane_g, lane_r = packed(cap, (PACK, 1), 0)
    wide = 2 * wg * slots
    aligned = (lane_g == shift(iota((1, wide), 1), slots)) & (lane_r == rank_row)
    place = [jnp.where(aligned & (own_row == (shift(me, 2) ^ d)), 1.0, 0.0).astype(BF) for d in names]
    place = jnp.concatenate(place, axis=0)
    for p in range(len(xrefs) // chips):
        got = jnp.concatenate([xrefs[p * chips + n][...] for n in range(chips)], axis=2)
        got = jnp.dot(got.reshape(groups * part, chips * PACK), place, preferred_element_type=F32)
        for w in range(2 * wp):
            b, i = w // wg, w % wg
            at = pl.ds(p * part * XPITCH + (w // wp) * WROWS + w % wp, part, stride=XPITCH)
            xs[at, :] = got[b * part : (b + 1) * part, i * LANES : (i + 1) * LANES]
        for w2 in range(2):
            for w in range(wp, WROWS):
                at = pl.ds(p * part * XPITCH + w2 * WROWS + w, part, stride=XPITCH)
                xs[at, :] = jnp.zeros((part, LANES), F32)


def tables_kernel(
    nchan, spec_ref, got_ref, own_pairs, got_pairs, slot_ref, recv_ref, hot_ref, count_ref, own, got, named, tally, in_sem
):
    _, windows, half, chans = got.shape
    slots = own_pairs.shape[0]
    bins = slot_ref.shape[1]
    per = bins // nchan
    wp = windows // 2
    core = lax.axis_index("chan") & 1
    mine = pl.ds(pl.multiple_of(core * half, half), half)
    ins = []
    for k in range(2):
        ins.append(pltpu.make_async_copy(spec_ref.at[k, :, mine], own.at[k], in_sem.at[k, 0]))
        ins.append(pltpu.make_async_copy(got_ref.at[k, :, mine], got.at[k], in_sem.at[k, 1]))
    for copy in ins:
        copy.start()

    r = iota((bins, 1), 0)
    block, rest = shift(r, per), r & (per - 1)
    side, chip = shift(block, nchan // 2), block & (nchan // 2 - 1)
    order = (chip * 2 + side) * per + rest
    row_bin = jnp.sum(jnp.where(slot_ref[...] == order, iota((1, bins), 1), 0), axis=1, keepdims=True)
    named[...] = jnp.broadcast_to(row_bin, named.shape)
    tally[...] = jnp.zeros_like(tally)

    def one_step(step, carry):
        total = tally[...]
        for u in range(GROUP):
            s = step * GROUP + u
            bin_of = named[...]
            mine_hit = jnp.where(own_pairs[pl.ds(s, 1), :] == bin_of, 1.0, 0.0)
            hot_ref[s, :, pl.ds(0, chans)] = mine_hit.astype(BF)
            hot_ref[s, :, pl.ds(chans, chans)] = jnp.where(got_pairs[pl.ds(s, 1), :] == bin_of, 1.0, 0.0).astype(BF)
            total = total + mine_hit
        tally[...] = total
        return carry

    lax.fori_loop(0, slots // GROUP, one_step, 0)
    count_ref[...] = lax.dot_general(
        jnp.ones((8, chans), BF), tally[...].astype(BF), (((1,), (1,)), ((), ())), preferred_element_type=F32
    )

    turn = frequency_first(wp)
    for copy in ins:
        copy.wait()
    for b in range(half // FB):
        at = pl.ds(b * FB, FB)
        for k in range(2):
            for w2 in range(2):
                ws = pl.ds(w2 * wp, wp)
                both = jnp.concatenate([own[k, ws, at, :], got[k, ws, at, :]], axis=2).reshape(wp * FB, 2 * chans)
                moved = jnp.dot(turn, both, preferred_element_type=F32).astype(BF)
                recv_ref[at, pl.ds((2 * k + w2) * WROWS, WROWS), :] = moved.reshape(FB, WROWS, 2 * chans)


def tables(spectra, got, own_pairs, got_pairs, slot_of_bin, nchan):
    _, windows, freqs, chans = spectra.shape
    half = freqs // 2
    slots = own_pairs.shape[0]
    bins = slot_of_bin.shape[0]
    side = ((2, windows, half, chans), BF)
    square = ((bins, chans), I32)
    return pl.pallas_call(
        functools.partial(tables_kernel, nchan),
        in_specs=[ANY, ANY, VMEM, VMEM, VMEM],
        out_specs=[VMEM, VMEM, VMEM],
        out_shape=[
            jax.ShapeDtypeStruct((half, 4 * WROWS, 2 * chans), BF),
            jax.ShapeDtypeStruct((slots, bins, 2 * chans), BF),
            jax.ShapeDtypeStruct((8, bins), F32),
        ],
        scratch_shapes=[
            pltpu.VMEM(*side),
            pltpu.VMEM(*side),
            pltpu.VMEM(*square),
            pltpu.VMEM((bins, chans), F32),
            pltpu.SemaphoreType.DMA((2, 2)),
        ],
        compiler_params=params(side, side, square, square, ((bins, bins), I32)),
        name="tables",
    )(spectra, got, own_pairs, got_pairs, slot_of_bin[None, :])


def early_kernel(cap, names, per_chip, src_ref, *refs):
    place_sources(cap, names, src_ref, per_chip, refs[:-1], refs[-1])


def place_early(arrays, names, src_ids, cap, per_chip):
    groups, part, _ = arrays[0].shape
    count = len(arrays) // len(names) * part
    shape = (count * XPITCH + 8, LANES)
    return pl.pallas_call(
        functools.partial(early_kernel, cap, names, per_chip),
        in_specs=[VMEM] * (1 + len(arrays)),
        out_specs=VMEM,
        out_shape=jax.ShapeDtypeStruct(shape, F32),
        compiler_params=params(*staging(arrays, names)),
        name="place_early",
    )(src_ids, *arrays)


def cross_kernel(cap, names, pieces, *refs):
    src_ref, recv, hot, cos_ref, sin_ref, count_ref, xs_early = refs[:7]
    xrefs = refs[7 : 7 + pieces * len(names)]
    refs = refs[7 + pieces * len(names) :]
    outs, refs = refs[:2], refs[2:]
    xs, cross, sums, whole = refs
    count, _, chans2 = recv.shape
    slots, bins, _ = hot.shape
    place_sources(cap, names, src_ref, chans2, xrefs, xs)
    imag = iota((2 * WROWS, LANES), 1) >= slots
    quarter = shift(iota((1, 4 * 4 * WROWS), 1), 4 * WROWS)
    masks = [jnp.where(quarter == i, 1.0, 0.0).astype(BF) for i in range(4)]

    def one_group(step, carry):
        for sub in range(2 * min(GROUPS, count // 8)):
            g, q = step * min(GROUPS, count // 8) + sub // 2, sub % 2
            lefts = []
            for j in range(4 * q, 4 * q + 4):
                at = pl.ds((g * 8 + j) * XPITCH, 2 * WROWS)
                x = xs_early[at, :] + xs[at, :]
                upper = jnp.where(imag, -x, x)
                if j:
                    upper = pltpu.roll(upper, j, 1)
                lefts += [upper, pltpu.roll(x, slots + j, 1)]
            left = jnp.transpose(jnp.concatenate(lefts, axis=0)).astype(BF)
            left = jnp.concatenate([left * mask for mask in masks], axis=0)
            right = recv[pl.ds(g * 8 + 4 * q, 4)].reshape(4 * 4 * WROWS, chans2)
            got = jnp.dot(left, right, preferred_element_type=F32)
            for i in range(4):
                j = 4 * q + i
                base = pl.multiple_of(g * (8 * PITCH) + j * (PITCH - 1), 8)
                for h in range(2):
                    side = got[i * LANES : (i + 1) * LANES, h * LANES : (h + 1) * LANES]
                    cross[h, pl.ds(base, LANES), :] = side
                    if j:
                        cross[h, pl.ds(pl.multiple_of(base + LANES, 8), 8), :] = side[:8]
        return carry

    lax.fori_loop(0, count // (8 * min(GROUPS, count // 8)), one_group, 0)

    sums[...] = jnp.zeros_like(sums)

    def one_turn(step, carry):
        lefts = []
        for u in range(TURN):
            s = step * TURN + u
            parts = []
            for turn in range(2):
                at = pl.ds(s + turn * slots, count, stride=PITCH)
                parts.append(jnp.concatenate([cross[0, at, :], cross[1, at, :]], axis=1))
            x = jnp.concatenate(parts, axis=0)
            high = x.astype(BF)
            low = (x - high.astype(F32)).astype(BF)
            lefts.append(jnp.concatenate([high, low], axis=0))
        left = jnp.concatenate(lefts, axis=1)
        right = jnp.concatenate([hot[step * TURN + u] for u in range(TURN)], axis=1)
        sums[...] += lax.dot_general(left, right, (((1,), (1,)), ((), ())), preferred_element_type=F32)
        return carry

    lax.fori_loop(0, slots // TURN, one_turn, 0)
    total = sums[pl.ds(0, 2 * count), :] + sums[pl.ds(2 * count, 2 * count), :]
    table = jnp.concatenate([cos_ref[...], sin_ref[...]], axis=0)
    whole[...] = lax.dot_general(total, table, (((0,), (0,)), ((), ())), precision=lax.Precision.HIGHEST, preferred_element_type=F32)
    core = lax.axis_index("chan") & 1
    blocks = outs[0].shape[0]
    per = bins // (2 * blocks)
    crows = count_ref.shape[0]
    for which, dest in ((core, outs[0]), (1 - core, outs[1])):
        for d in range(blocks):
            start = pl.multiple_of((which * blocks + d) * per, per)
            dest[d, pl.ds(0, per), :] = whole[pl.ds(start, per), :]
            dest[d, pl.ds(per, crows), :] = count_ref[...]


def staging(arrays, names):
    groups, part, _ = arrays[0].shape
    chips = len(names)
    return [((groups * part, 4 * PACK), F32), ((groups * part, chips * PACK), BF), ((chips * PACK, 4 * PACK), F32)]


def cross_and_bin(arrays, names, xs_early, src_ids, recv, hot, counts, cos, sin, cap, nchan):
    _, bins, chans2 = hot.shape
    lags = cos.shape[1]
    count = recv.shape[0]
    per = bins // nchan
    out = jax.ShapeDtypeStruct((nchan // 2, per + 8, lags), F32)
    scratch = [
        (xs_early.shape, F32),
        ((2, count * PITCH + 8, chans2 // 2), F32),
        ((4 * count, bins), F32),
        ((bins, lags), F32),
    ]
    buffers = scratch + staging(arrays, names)
    return pl.pallas_call(
        functools.partial(cross_kernel, cap, names, len(arrays) // len(names)),
        in_specs=[VMEM] * (7 + len(arrays)),
        out_specs=[VMEM, VMEM],
        out_shape=[out, out],
        scratch_shapes=[pltpu.VMEM(shape, kind) for shape, kind in scratch],
        compiler_params=params(*buffers, *([(hot.shape, BF)] if hot.size > BIG else [])),
        name="cross_and_bin",
    )(src_ids, recv, hot, cos, sin, counts, xs_early, *arrays)


def swap(x, size, bit):
    return lax.ppermute(x, "chan", [(i, i ^ bit) for i in range(size)])


def gathered(nchan, pieces, chip):
    rest = [1 << k for k in range(1, nchan.bit_length() - 1)]
    result = []
    held = [[x] for x in chip]
    names = [[0] for _ in chip]
    for hop in range(len(rest)):
        bits = [rest[hop] if p % 2 == 0 else rest[-1 - hop] for p in range(pieces)]
        early = [swap(chip[p], nchan, bits[p]) for p in range(pieces)]
        for p, bit in enumerate(bits):
            held[p] = held[p] + [early[p]] + [swap(x, nchan, bit) for x in held[p][1:]]
            names[p] = names[p] + [name ^ bit for name in names[p]]
    for p in range(pieces):
        result.append([held[p][names[p].index(2 * d)] for d in range(len(held[p]))])
    return result


def chip_sources(nchan, cap, pieces, spectra, src_ids):
    keep, send = pick(spectra, src_ids, cap)
    got = swap(send, nchan, 1)
    part = keep.shape[1] // pieces
    return [keep[:, p * part : (p + 1) * part] + got[:, p * part : (p + 1) * part] for p in range(pieces)]


def finish(nchan, nfreq, cap, chip, spectra, src_ids, pairs_own, got_pairs, slot_of_bin):
    _, windows, freqs, chans = spectra.shape
    half = freqs // 2
    bins = slot_of_bin.shape[0]
    me = lax.axis_index("chan")
    core = me & 1
    rest = [1 << k for k in range(1, nchan.bit_length() - 1)]
    arrays = gathered(nchan, len(chip), chip)
    spectra_sent, chip = lax.optimization_barrier((spectra, chip))
    got_spec = swap(spectra_sent, nchan, 1)
    chips = len(arrays[0])
    early, late = list(range(chips - chips // 4)), list(range(chips - chips // 4, chips))
    first = [held[d] for held in arrays for d in early]
    recv, hot, counts = tables(spectra, got_spec, pairs_own, got_pairs, slot_of_bin, nchan)
    counts, first = lax.optimization_barrier((counts, first))
    xs_early = place_early(first, early, src_ids, cap, 2 * chans)
    cos, sin = lag_basis(lax.axis_index("freq") * freqs + core * half, half, F, NLAG, windows)
    counts = counts[0].reshape(bins // NLAG, NLAG)
    last = [held[d] for held in arrays for d in late]
    out = cross_and_bin(last, late, xs_early, src_ids, recv, hot, counts, cos, sin, cap, nchan)
    mine, other = out

    per = bins // nchan
    mine = mine + swap(other, nchan, 1)
    at = me // 2
    if nchan // 2 <= 4:
        total = lax.dynamic_index_in_dim(mine, at, 0, keepdims=False)
        for move in range(1, nchan // 2):
            total = total + swap(lax.dynamic_index_in_dim(mine, at ^ move, 0, keepdims=False), nchan, 2 * move)
    else:
        for bit in rest[::-1]:
            size = mine.shape[0] // 2
            up = (me & bit) != 0
            low, high = mine[:size], mine[size:]
            mine = jnp.where(up, high, low) + swap(jnp.where(up, low, high), nchan, bit)
        total = mine[0]
    owned = total[:per]
    parts = [owned]
    if nfreq <= 4:
        parts += [lax.ppermute(owned, "freq", [(i, i ^ k) for i in range(nfreq)]) for k in range(nfreq - 1, 0, -1)]
    else:
        for k in range(nfreq.bit_length() - 1):
            owned = parts[0]
            parts = [owned + lax.ppermute(owned, "freq", [(i, i ^ (1 << k)) for i in range(nfreq)])]
    counted = total[per : per + bins // NLAG].reshape(bins)
    count = lax.dynamic_slice(counted, ((core * (nchan // 2) + at) * per,), (per,))
    return parts, count


def scaled(parts, count):
    total = parts[0]
    for part in parts[1:]:
        total = total + part
    return total / jnp.sqrt(jnp.maximum(count, 1.0))[:, None]


def body(nchan, nfreq, spectra, src_ids, pair_bin, slot_of_bin):
    chans = spectra.shape[3]
    slots = src_ids.shape[0] * src_ids.shape[1]
    pieces = 2
    pairs_own = pair_bin.reshape(slots, chans)
    got_pairs = swap(pairs_own, nchan, 1)
    chip = lax.optimization_barrier(chip_sources(nchan, CAP, pieces, spectra, src_ids))
    owner = src_ids // (2 * chans)
    loads = jnp.sum((owner[None] == lax.iota(I32, nchan // 2)[:, None, None]).astype(I32), axis=(1, 2))
    fits = jnp.max(loads) <= CAP

    def small(parts, count, *args):
        return scaled(parts, count)

    def large(parts, count, *args):
        chip = chip_sources(nchan, slots, pieces, *args[:2])
        return scaled(*finish(nchan, nfreq, slots, chip, *args))

    args = (spectra, src_ids, pairs_own, got_pairs, slot_of_bin)
    parts, count = finish(nchan, nfreq, CAP, chip, *args)
    return lax.cond(fits, small, large, parts, count, *args)


def solution(mesh):
    return jax.shard_map(
        functools.partial(body, mesh.shape["chan"], mesh.shape["freq"]),
        mesh=mesh,
        in_specs=(P(None, None, "freq", "chan"), P(), P(None, None, "chan"), P()),
        out_specs=P("chan", None),
        check_vma=False,
    )
```

```python
import functools
import math

import jax
import jax.numpy as jnp
from jax import lax
from jax.experimental import pallas as pl
from jax.experimental.pallas import tpu as pltpu
from jax.sharding import PartitionSpec as P

F = 1024
NLAG = 256
BF = jnp.bfloat16
F32 = jnp.float32
I32 = jnp.int32
FB = 16
WROWS = 16
LANES = 128
SLACK = 6 * 1024 * 1024
PITCH = LANES + 9
TURN = 32
BIG = 8 * 1024 * 1024
CAP = 25
PACK = 2 * LANES
XPITCH = 2 * WROWS + 1
GROUPS = 16
GROUP = 8
ANY = pl.BlockSpec(memory_space=pl.ANY)
VMEM = pl.BlockSpec(memory_space=pltpu.VMEM)


def lag_basis(anchor, amount, totals, lag_count, windows):
    frequency = anchor + lax.iota(I32, amount)
    shifts = lax.iota(I32, lag_count) - lag_count // 2
    phases = frequency[:, None] * shifts[None, :] % (2 * totals)
    angles = phases.astype(F32) * (math.pi / totals)
    factor = 1.0 / math.sqrt(windows * totals)
    return jnp.cos(angles) * factor, -jnp.sin(angles) * factor


def params(*buffers):
    used = sum(math.prod(shape) * jnp.dtype(kind).itemsize for shape, kind in buffers)
    return pltpu.CompilerParams(vmem_limit_bytes=used + SLACK)


def iota(shape, dim):
    return lax.broadcasted_iota(I32, shape, dim)


def shift(values, size):
    return lax.shift_right_logical(values, jnp.int32(size.bit_length() - 1))


def as_column(row):
    size = row.shape[1]
    eye = iota((size, size), 0) == iota((size, size), 1)
    return jnp.sum(jnp.where(eye, row, 0), axis=1, keepdims=True)


def source_row(src_ref):
    return jnp.concatenate([src_ref[t : t + 1, :] for t in range(src_ref.shape[0])], axis=1)


def chip_ranks(row, per_chip):
    size = row.shape[1]
    own_row = shift(row, per_chip)
    col = as_column(row)
    own_col = shift(col, per_chip)
    same = own_col == own_row
    q0, q1 = iota((size, size), 0), iota((size, size), 1)
    rank_col = jnp.sum(jnp.where(same & (q1 < q0), 1, 0), axis=1, keepdims=True)
    rank_row = jnp.sum(jnp.where(same & (q0 < q1), 1, 0), axis=0, keepdims=True)
    return col, own_col, rank_col, own_row, rank_row


def packed(cap, shape, dim):
    lane = iota(shape, dim)
    group = jnp.zeros(shape, I32)
    for j in range(1, PACK // cap + 1):
        group = group + jnp.where(lane >= j * cap, 1, 0)
    return group, lane - group * cap


def frequency_first(rows):
    shape = (FB * WROWS, rows * FB)
    r, c = iota(shape, 0), iota(shape, 1)
    hit = (shift(r, WROWS) == (c & (FB - 1))) & ((r & (WROWS - 1)) == shift(c, FB))
    return jnp.where(hit, 1.0, 0.0).astype(BF)


def pick_kernel(cap, src_ref, spec_ref, keep_ref, send_ref, buf, res, in_sem, out_sem):
    _, _, freqs, chans = spec_ref.shape
    half = freqs // 2
    wg = PACK // (2 * cap)
    groups = in_sem.shape[0]
    me = lax.axis_index("chan")
    core = me & 1
    ins = []
    for b in range(groups):
        for k in range(2):
            at = pl.ds(b * wg, wg)
            ins.append(pltpu.make_async_copy(spec_ref.at[k, at], buf.at[k, at], in_sem.at[b, k]))
    for copy in ins:
        copy.start()

    row = source_row(src_ref)
    col, own_col, rank_col, _, _ = chip_ranks(row, 2 * chans)
    slots = row.shape[1]
    _, lane_r = packed(cap, (slots, PACK), 1)
    match = (own_col == shift(me, 2)) & (rank_col == lane_r)
    local = col - me * chans
    found = jnp.sum(jnp.where(match, local + 1, 0), axis=0, keepdims=True) - 1
    shape = (2 * wg * chans, PACK)
    lane_g, _ = packed(cap, (1, PACK), 1)
    r = iota(shape, 0)
    picker = jnp.where((shift(r, chans) == lane_g) & ((r & (chans - 1)) == found), 1.0, 0.0).astype(BF)

    mine = pl.multiple_of(core * half, half)
    other = pl.multiple_of((1 - core) * half, half)
    outs = []
    turn = 2 if groups % 2 == 0 else 1
    for b0 in range(0, groups, turn):
        lefts = []
        for b in range(b0, b0 + turn):
            for copy in ins[2 * b : 2 * b + 2]:
                copy.wait()
            lefts.append(jnp.concatenate([buf[k, b * wg + i] for i in range(wg) for k in range(2)], axis=1))
        left = jnp.concatenate(lefts, axis=0)
        got = []
        for h in range(PACK // LANES):
            first, last = h * LANES // cap * chans, min(-(-(h + 1) * LANES // cap), 2 * wg) * chans
            part = picker[first:last, h * LANES : (h + 1) * LANES]
            got.append(jnp.dot(left[:, first:last], part, preferred_element_type=F32))
        got = jnp.concatenate(got, axis=1).astype(BF)
        for b in range(b0, b0 + turn):
            res[b] = got[(b - b0) * freqs : (b - b0 + 1) * freqs]
        for n, (start, ref) in enumerate(((other, send_ref), (mine, keep_ref))):
            at = pl.ds(b0, turn)
            outs.append(pltpu.make_async_copy(res.at[at, pl.ds(start, half)], ref.at[at], out_sem.at[b0, n]))
            outs[-1].start()
    for copy in outs:
        copy.wait()


def pick(spectra, src_ids, cap):
    _, windows, freqs, chans = spectra.shape
    half = freqs // 2
    groups = windows // (PACK // (2 * cap))
    shape = (groups, half, PACK)
    out = jax.ShapeDtypeStruct(shape, BF)
    return pl.pallas_call(
        functools.partial(pick_kernel, cap),
        in_specs=[VMEM, ANY],
        out_specs=[ANY, ANY],
        out_shape=[out, out],
        scratch_shapes=[
            pltpu.VMEM(spectra.shape, BF),
            pltpu.VMEM((groups, freqs, PACK), BF),
            pltpu.SemaphoreType.DMA((groups, 2)),
            pltpu.SemaphoreType.DMA((groups, 2)),
        ],
        compiler_params=params((spectra.shape, BF), (shape, BF), (shape, BF)),
        name="pick_sources",
    )(src_ids, spectra)


def placement(cap, names, src_ref, per_chip):
    wg = PACK // (2 * cap)
    me = lax.axis_index("chan")
    row = source_row(src_ref)
    slots = row.shape[1]
    _, _, _, own_row, rank_row = chip_ranks(row, per_chip)
    own_row = jnp.concatenate([own_row] * (2 * wg), axis=1)
    rank_row = jnp.concatenate([rank_row] * (2 * wg), axis=1)
    lane_g, lane_r = packed(cap, (PACK, 1), 0)
    wide = 2 * wg * slots
    aligned = (lane_g == shift(iota((1, wide), 1), slots)) & (lane_r == rank_row)
    place = [jnp.where(aligned & (own_row == (shift(me, 2) ^ d)), 1.0, 0.0).astype(BF) for d in names]
    return jnp.concatenate(place, axis=0)


def place_sources(place, xrefs, xs):
    groups, part, _ = xrefs[0].shape
    chips = place.shape[0] // PACK
    wg = place.shape[1] // LANES
    wp = groups * wg // 2
    for p in range(len(xrefs) // chips):
        got = jnp.concatenate([xrefs[p * chips + n][...] for n in range(chips)], axis=2)
        got = jnp.dot(got.reshape(groups * part, chips * PACK), place, preferred_element_type=F32)
        for w in range(2 * wp):
            b, i = w // wg, w % wg
            at = pl.ds(p * part * XPITCH + (w // wp) * WROWS + w % wp, part, stride=XPITCH)
            xs[at, :] = got[b * part : (b + 1) * part, i * LANES : (i + 1) * LANES]
        for w2 in range(2):
            for w in range(wp, WROWS):
                at = pl.ds(p * part * XPITCH + w2 * WROWS + w, part, stride=XPITCH)
                xs[at, :] = jnp.zeros((part, LANES), F32)


def tables_kernel(
    nchan, spec_ref, got_ref, own_pairs, got_pairs, slot_ref, recv_ref, hot_ref, count_ref, own, got, named, tally, in_sem
):
    _, windows, half, chans = got.shape
    slots = own_pairs.shape[0]
    bins = slot_ref.shape[1]
    per = bins // nchan
    wp = windows // 2
    core = lax.axis_index("chan") & 1
    mine = pl.ds(pl.multiple_of(core * half, half), half)
    ins = []
    for k in range(2):
        ins.append(pltpu.make_async_copy(spec_ref.at[k, :, mine], own.at[k], in_sem.at[k, 0]))
        ins.append(pltpu.make_async_copy(got_ref.at[k, :, mine], got.at[k], in_sem.at[k, 1]))
    for copy in ins:
        copy.start()

    r = iota((bins, 1), 0)
    block, rest = shift(r, per), r & (per - 1)
    side, chip = shift(block, nchan // 2), block & (nchan // 2 - 1)
    order = (chip * 2 + side) * per + rest
    row_bin = jnp.sum(jnp.where(slot_ref[...] == order, iota((1, bins), 1), 0), axis=1, keepdims=True)
    named[...] = jnp.broadcast_to(row_bin, named.shape)
    tally[...] = jnp.zeros_like(tally)

    def one_step(step, carry):
        total = tally[...]
        for u in range(GROUP):
            s = step * GROUP + u
            bin_of = named[...]
            mine_hit = jnp.where(own_pairs[pl.ds(s, 1), :] == bin_of, 1.0, 0.0)
            hot_ref[s, :, pl.ds(0, chans)] = mine_hit.astype(BF)
            hot_ref[s, :, pl.ds(chans, chans)] = jnp.where(got_pairs[pl.ds(s, 1), :] == bin_of, 1.0, 0.0).astype(BF)
            total = total + mine_hit
        tally[...] = total
        return carry

    lax.fori_loop(0, slots // GROUP, one_step, 0)
    count_ref[...] = lax.dot_general(
        jnp.ones((8, chans), BF), tally[...].astype(BF), (((1,), (1,)), ((), ())), preferred_element_type=F32
    )

    turn = frequency_first(wp)
    for copy in ins:
        copy.wait()
    for b in range(half // FB):
        at = pl.ds(b * FB, FB)
        for k in range(2):
            for w2 in range(2):
                ws = pl.ds(w2 * wp, wp)
                both = jnp.concatenate([own[k, ws, at, :], got[k, ws, at, :]], axis=2).reshape(wp * FB, 2 * chans)
                moved = jnp.dot(turn, both, preferred_element_type=F32).astype(BF)
                recv_ref[at, pl.ds((2 * k + w2) * WROWS, WROWS), :] = moved.reshape(FB, WROWS, 2 * chans)


def tables(spectra, got, own_pairs, got_pairs, slot_of_bin, nchan):
    _, windows, freqs, chans = spectra.shape
    half = freqs // 2
    slots = own_pairs.shape[0]
    bins = slot_of_bin.shape[0]
    side = ((2, windows, half, chans), BF)
    square = ((bins, chans), I32)
    return pl.pallas_call(
        functools.partial(tables_kernel, nchan),
        in_specs=[ANY, ANY, VMEM, VMEM, VMEM],
        out_specs=[VMEM, VMEM, VMEM],
        out_shape=[
            jax.ShapeDtypeStruct((half, 4 * WROWS, 2 * chans), BF),
            jax.ShapeDtypeStruct((slots, bins, 2 * chans), BF),
            jax.ShapeDtypeStruct((8, bins), F32),
        ],
        scratch_shapes=[
            pltpu.VMEM(*side),
            pltpu.VMEM(*side),
            pltpu.VMEM(*square),
            pltpu.VMEM((bins, chans), F32),
            pltpu.SemaphoreType.DMA((2, 2)),
        ],
        compiler_params=params(side, side, square, square, ((bins, bins), I32)),
        name="tables",
    )(spectra, got, own_pairs, got_pairs, slot_of_bin[None, :])


def early_kernel(cap, names, late, per_chip, src_ref, *refs):
    *xrefs, xs_ref, late_ref = refs
    place_sources(placement(cap, names, src_ref, per_chip), xrefs, xs_ref)
    late_ref[...] = placement(cap, late, src_ref, per_chip)


def place_early(arrays, names, late, src_ids, cap, per_chip):
    groups, part, _ = arrays[0].shape
    count = len(arrays) // len(names) * part
    shape = (count * XPITCH + 8, LANES)
    return pl.pallas_call(
        functools.partial(early_kernel, cap, names, late, per_chip),
        in_specs=[VMEM] * (1 + len(arrays)),
        out_specs=[VMEM, VMEM],
        out_shape=[
            jax.ShapeDtypeStruct(shape, F32),
            jax.ShapeDtypeStruct((len(late) * PACK, PACK // (2 * cap) * LANES), BF),
        ],
        compiler_params=params(*staging(arrays, names)),
        name="place_early",
    )(src_ids, *arrays)


def cross_kernel(inputs, *refs):
    place_ref, recv, hot, cos_ref, sin_ref, count_ref, xs_early = refs[:7]
    xrefs, refs = refs[7 : 7 + inputs], refs[7 + inputs :]
    outs, refs = refs[:2], refs[2:]
    xs, cross, sums, whole = refs
    count, _, chans2 = recv.shape
    slots, bins, _ = hot.shape
    place_sources(place_ref[...], xrefs, xs)
    imag = iota((2 * WROWS, LANES), 1) >= slots
    quarter = shift(iota((1, 4 * 4 * WROWS), 1), 4 * WROWS)
    masks = [jnp.where(quarter == i, 1.0, 0.0).astype(BF) for i in range(4)]

    def one_group(step, carry):
        for sub in range(2 * min(GROUPS, count // 8)):
            g, q = step * min(GROUPS, count // 8) + sub // 2, sub % 2
            lefts = []
            for j in range(4 * q, 4 * q + 4):
                at = pl.ds((g * 8 + j) * XPITCH, 2 * WROWS)
                x = (xs_early[at, :] + xs[at, :]).astype(BF)
                upper = jnp.where(imag, -x, x)
                if j:
                    upper = pltpu.roll(upper, j, 1)
                lefts += [upper, pltpu.roll(x, slots + j, 1)]
            left = jnp.transpose(jnp.concatenate(lefts, axis=0))
            left = jnp.concatenate([left * mask for mask in masks], axis=0)
            right = recv[pl.ds(g * 8 + 4 * q, 4)].reshape(4 * 4 * WROWS, chans2)
            got = jnp.dot(left, right, preferred_element_type=F32)
            for i in range(4):
                j = 4 * q + i
                base = pl.multiple_of(g * (8 * PITCH) + j * (PITCH - 1), 8)
                for h in range(2):
                    side = got[i * LANES : (i + 1) * LANES, h * LANES : (h + 1) * LANES]
                    cross[h, pl.ds(base, LANES), :] = side
                    if j:
                        cross[h, pl.ds(pl.multiple_of(base + LANES, 8), 8), :] = side[:8]
        return carry

    lax.fori_loop(0, count // (8 * min(GROUPS, count // 8)), one_group, 0)

    sums[...] = jnp.zeros_like(sums)

    def one_turn(step, carry):
        lefts = []
        for u in range(TURN):
            s = step * TURN + u
            parts = []
            for turn in range(2):
                at = pl.ds(s + turn * slots, count, stride=PITCH)
                parts.append(jnp.concatenate([cross[0, at, :], cross[1, at, :]], axis=1))
            x = jnp.concatenate(parts, axis=0)
            high = x.astype(BF)
            low = (x - high.astype(F32)).astype(BF)
            lefts.append(jnp.concatenate([high, low], axis=0))
        left = jnp.concatenate(lefts, axis=1)
        right = jnp.concatenate([hot[step * TURN + u] for u in range(TURN)], axis=1)
        sums[...] += lax.dot_general(left, right, (((1,), (1,)), ((), ())), preferred_element_type=F32)
        return carry

    lax.fori_loop(0, slots // TURN, one_turn, 0)
    total = sums[pl.ds(0, 2 * count), :] + sums[pl.ds(2 * count, 2 * count), :]
    table = jnp.concatenate([cos_ref[...], sin_ref[...]], axis=0)
    whole[...] = lax.dot_general(total, table, (((0,), (0,)), ((), ())), precision=lax.Precision.HIGHEST, preferred_element_type=F32)
    core = lax.axis_index("chan") & 1
    blocks = outs[0].shape[0]
    per = bins // (2 * blocks)
    crows = count_ref.shape[0]
    for which, dest in ((core, outs[0]), (1 - core, outs[1])):
        for d in range(blocks):
            start = pl.multiple_of((which * blocks + d) * per, per)
            dest[d, pl.ds(0, per), :] = whole[pl.ds(start, per), :]
            dest[d, pl.ds(per, crows), :] = count_ref[...]


def staging(arrays, names):
    groups, part, _ = arrays[0].shape
    chips = len(names)
    return [((groups * part, 4 * PACK), F32), ((groups * part, chips * PACK), BF), ((chips * PACK, 4 * PACK), F32)]


def cross_and_bin(arrays, names, xs_early, place, recv, hot, counts, cos, sin, nchan):
    _, bins, chans2 = hot.shape
    lags = cos.shape[1]
    count = recv.shape[0]
    per = bins // nchan
    out = jax.ShapeDtypeStruct((nchan // 2, per + 8, lags), F32)
    scratch = [
        (xs_early.shape, F32),
        ((2, count * PITCH + 8, chans2 // 2), F32),
        ((4 * count, bins), F32),
        ((bins, lags), F32),
    ]
    buffers = scratch + staging(arrays, names)
    return pl.pallas_call(
        functools.partial(cross_kernel, len(arrays)),
        in_specs=[VMEM] * (7 + len(arrays)),
        out_specs=[VMEM, VMEM],
        out_shape=[out, out],
        scratch_shapes=[pltpu.VMEM(shape, kind) for shape, kind in scratch],
        compiler_params=params(*buffers, *([(hot.shape, BF)] if hot.size > BIG else [])),
        name="cross_and_bin",
    )(place, recv, hot, cos, sin, counts, xs_early, *arrays)


def swap(x, size, bit):
    return lax.ppermute(x, "chan", [(i, i ^ bit) for i in range(size)])


def gathered(nchan, pieces, chip):
    rest = [1 << k for k in range(1, nchan.bit_length() - 1)]
    result = []
    held = [[x] for x in chip]
    names = [[0] for _ in chip]
    for hop in range(len(rest)):
        bits = [rest[hop] if p % 2 == 0 else rest[-1 - hop] for p in range(pieces)]
        early = [swap(chip[p], nchan, bits[p]) for p in range(pieces)]
        for p, bit in enumerate(bits):
            held[p] = held[p] + [early[p]] + [swap(x, nchan, bit) for x in held[p][1:]]
            names[p] = names[p] + [name ^ bit for name in names[p]]
    for p in range(pieces):
        result.append([held[p][names[p].index(2 * d)] for d in range(len(held[p]))])
    return result


def chip_sources(nchan, cap, pieces, spectra, src_ids):
    keep, send = pick(spectra, src_ids, cap)
    got = swap(send, nchan, 1)
    part = keep.shape[1] // pieces
    return [keep[:, p * part : (p + 1) * part] + got[:, p * part : (p + 1) * part] for p in range(pieces)]


def finish(nchan, nfreq, cap, chip, spectra, src_ids, pairs_own, got_pairs, slot_of_bin):
    _, windows, freqs, chans = spectra.shape
    half = freqs // 2
    bins = slot_of_bin.shape[0]
    me = lax.axis_index("chan")
    core = me & 1
    rest = [1 << k for k in range(1, nchan.bit_length() - 1)]
    arrays = gathered(nchan, len(chip), chip)
    spectra_sent, chip = lax.optimization_barrier((spectra, chip))
    got_spec = swap(spectra_sent, nchan, 1)
    chips = len(arrays[0])
    early, late = list(range(chips - chips // 4)), list(range(chips - chips // 4, chips))
    first = [held[d] for held in arrays for d in early]
    recv, hot, counts = tables(spectra, got_spec, pairs_own, got_pairs, slot_of_bin, nchan)
    counts, first = lax.optimization_barrier((counts, first))
    xs_early, place = place_early(first, early, late, src_ids, cap, 2 * chans)
    cos, sin = lag_basis(lax.axis_index("freq") * freqs + core * half, half, F, NLAG, windows)
    counts = counts[0].reshape(bins // NLAG, NLAG)
    last = [held[d] for held in arrays for d in late]
    out = cross_and_bin(last, late, xs_early, place, recv, hot, counts, cos, sin, nchan)
    mine, other = out

    per = bins // nchan
    mine = mine + swap(other, nchan, 1)
    at = me // 2
    if nchan // 2 <= 4:
        total = lax.dynamic_index_in_dim(mine, at, 0, keepdims=False)
        for move in range(nchan // 2 - 1, 0, -1):
            total = total + swap(lax.dynamic_index_in_dim(mine, at ^ move, 0, keepdims=False), nchan, 2 * move)
    else:
        for bit in rest[::-1]:
            size = mine.shape[0] // 2
            up = (me & bit) != 0
            low, high = mine[:size], mine[size:]
            mine = jnp.where(up, high, low) + swap(jnp.where(up, low, high), nchan, bit)
        total = mine[0]
    owned = total[:per]
    parts = [owned]
    if nfreq <= 4:
        parts += [lax.ppermute(owned, "freq", [(i, i ^ k) for i in range(nfreq)]) for k in range(nfreq - 1, 0, -1)]
    else:
        for k in range(nfreq.bit_length() - 1):
            owned = parts[0]
            parts = [owned + lax.ppermute(owned, "freq", [(i, i ^ (1 << k)) for i in range(nfreq)])]
    counted = total[per : per + bins // NLAG].reshape(bins)
    count = lax.dynamic_slice(counted, ((core * (nchan // 2) + at) * per,), (per,))
    return parts, count


def scaled(parts, count):
    total = parts[0]
    for part in parts[1:]:
        total = total + part
    return total / jnp.sqrt(jnp.maximum(count, 1.0))[:, None]


def body(nchan, nfreq, spectra, src_ids, pair_bin, slot_of_bin):
    chans = spectra.shape[3]
    slots = src_ids.shape[0] * src_ids.shape[1]
    pieces = 2
    pairs_own = pair_bin.reshape(slots, chans)
    got_pairs = swap(pairs_own, nchan, 1)
    chip = lax.optimization_barrier(chip_sources(nchan, CAP, pieces, spectra, src_ids))
    owner = src_ids // (2 * chans)
    loads = jnp.sum((owner[None] == lax.iota(I32, nchan // 2)[:, None, None]).astype(I32), axis=(1, 2))
    fits = jnp.max(loads) <= CAP

    def small(parts, count, *args):
        return scaled(parts, count)

    def large(parts, count, *args):
        chip = chip_sources(nchan, slots, pieces, *args[:2])
        return scaled(*finish(nchan, nfreq, slots, chip, *args))

    args = (spectra, src_ids, pairs_own, got_pairs, slot_of_bin)
    parts, count = finish(nchan, nfreq, CAP, chip, *args)
    return lax.cond(fits, small, large, parts, count, *args)


def solution(mesh):
    return jax.shard_map(
        functools.partial(body, mesh.shape["chan"], mesh.shape["freq"]),
        mesh=mesh,
        in_specs=(P(None, None, "freq", "chan"), P(), P(None, None, "chan"), P()),
        out_specs=P("chan", None),
        check_vma=False,
    )
```

```python
import functools
import math

import jax
import jax.numpy as jnp
from jax import lax
from jax.experimental import pallas as pl
from jax.experimental.pallas import tpu as pltpu
from jax.sharding import PartitionSpec as P

F = 1024
NLAG = 256
BF = jnp.bfloat16
F32 = jnp.float32
I32 = jnp.int32
FB = 16
WROWS = 16
LANES = 128
SLACK = 6 * 1024 * 1024
PITCH = LANES + 9
TURN = 32
BIG = 8 * 1024 * 1024
CAP = 25
PACK = 2 * LANES
XPITCH = 2 * WROWS + 1
GROUPS = 16
GROUP = 8
ANY = pl.BlockSpec(memory_space=pl.ANY)
VMEM = pl.BlockSpec(memory_space=pltpu.VMEM)


def lag_basis(anchor, amount, totals, lag_count, windows):
    frequency = anchor + lax.iota(I32, amount)
    shifts = lax.iota(I32, lag_count) - lag_count // 2
    phases = frequency[:, None] * shifts[None, :] % (2 * totals)
    angles = phases.astype(F32) * (math.pi / totals)
    factor = 1.0 / math.sqrt(windows * totals)
    return jnp.cos(angles) * factor, -jnp.sin(angles) * factor


def params(*buffers):
    used = sum(math.prod(shape) * jnp.dtype(kind).itemsize for shape, kind in buffers)
    return pltpu.CompilerParams(vmem_limit_bytes=used + SLACK)


def iota(shape, dim):
    return lax.broadcasted_iota(I32, shape, dim)


def shift(values, size):
    return lax.shift_right_logical(values, jnp.int32(size.bit_length() - 1))


def as_column(row):
    size = row.shape[1]
    eye = iota((size, size), 0) == iota((size, size), 1)
    return jnp.sum(jnp.where(eye, row, 0), axis=1, keepdims=True)


def source_row(src_ref):
    return jnp.concatenate([src_ref[t : t + 1, :] for t in range(src_ref.shape[0])], axis=1)


def chip_ranks(row, per_chip):
    size = row.shape[1]
    own_row = shift(row, per_chip)
    col = as_column(row)
    own_col = shift(col, per_chip)
    same = own_col == own_row
    q0, q1 = iota((size, size), 0), iota((size, size), 1)
    rank_col = jnp.sum(jnp.where(same & (q1 < q0), 1, 0), axis=1, keepdims=True)
    rank_row = jnp.sum(jnp.where(same & (q0 < q1), 1, 0), axis=0, keepdims=True)
    return col, own_col, rank_col, own_row, rank_row


def packed(cap, shape, dim):
    lane = iota(shape, dim)
    group = jnp.zeros(shape, I32)
    for j in range(1, PACK // cap + 1):
        group = group + jnp.where(lane >= j * cap, 1, 0)
    return group, lane - group * cap


def frequency_first(rows):
    shape = (FB * WROWS, rows * FB)
    r, c = iota(shape, 0), iota(shape, 1)
    hit = (shift(r, WROWS) == (c & (FB - 1))) & ((r & (WROWS - 1)) == shift(c, FB))
    return jnp.where(hit, 1.0, 0.0).astype(BF)


def pick_kernel(cap, src_ref, spec_ref, keep_ref, send_ref, buf, res, in_sem, out_sem):
    _, _, freqs, chans = spec_ref.shape
    half = freqs // 2
    wg = PACK // (2 * cap)
    groups = in_sem.shape[0]
    me = lax.axis_index("chan")
    core = me & 1
    ins = []
    for b in range(groups):
        for k in range(2):
            at = pl.ds(b * wg, wg)
            ins.append(pltpu.make_async_copy(spec_ref.at[k, at], buf.at[k, at], in_sem.at[b, k]))
    for copy in ins:
        copy.start()

    row = source_row(src_ref)
    col, own_col, rank_col, _, _ = chip_ranks(row, 2 * chans)
    slots = row.shape[1]
    _, lane_r = packed(cap, (slots, PACK), 1)
    match = (own_col == shift(me, 2)) & (rank_col == lane_r)
    local = col - me * chans
    found = jnp.sum(jnp.where(match, local + 1, 0), axis=0, keepdims=True) - 1
    shape = (2 * wg * chans, PACK)
    lane_g, _ = packed(cap, (1, PACK), 1)
    r = iota(shape, 0)
    picker = jnp.where((shift(r, chans) == lane_g) & ((r & (chans - 1)) == found), 1.0, 0.0).astype(BF)

    mine = pl.multiple_of(core * half, half)
    other = pl.multiple_of((1 - core) * half, half)
    outs = []
    turn = 2 if groups % 2 == 0 else 1
    for b0 in range(0, groups, turn):
        lefts = []
        for b in range(b0, b0 + turn):
            for copy in ins[2 * b : 2 * b + 2]:
                copy.wait()
            lefts.append(jnp.concatenate([buf[k, b * wg + i] for i in range(wg) for k in range(2)], axis=1))
        left = jnp.concatenate(lefts, axis=0)
        got = []
        for h in range(PACK // LANES):
            first, last = h * LANES // cap * chans, min(-(-(h + 1) * LANES // cap), 2 * wg) * chans
            part = picker[first:last, h * LANES : (h + 1) * LANES]
            got.append(jnp.dot(left[:, first:last], part, preferred_element_type=F32))
        got = jnp.concatenate(got, axis=1).astype(BF)
        for b in range(b0, b0 + turn):
            res[b] = got[(b - b0) * freqs : (b - b0 + 1) * freqs]
        for n, (start, ref) in enumerate(((other, send_ref), (mine, keep_ref))):
            at = pl.ds(b0, turn)
            outs.append(pltpu.make_async_copy(res.at[at, pl.ds(start, half)], ref.at[at], out_sem.at[b0, n]))
            outs[-1].start()
    for copy in outs:
        copy.wait()


def pick(spectra, src_ids, cap):
    _, windows, freqs, chans = spectra.shape
    half = freqs // 2
    groups = windows // (PACK // (2 * cap))
    shape = (groups, half, PACK)
    out = jax.ShapeDtypeStruct(shape, BF)
    return pl.pallas_call(
        functools.partial(pick_kernel, cap),
        in_specs=[VMEM, ANY],
        out_specs=[ANY, ANY],
        out_shape=[out, out],
        scratch_shapes=[
            pltpu.VMEM(spectra.shape, BF),
            pltpu.VMEM((groups, freqs, PACK), BF),
            pltpu.SemaphoreType.DMA((groups, 2)),
            pltpu.SemaphoreType.DMA((groups, 2)),
        ],
        compiler_params=params((spectra.shape, BF), (shape, BF), (shape, BF)),
        name="pick_sources",
    )(src_ids, spectra)


def placement(cap, names, src_ref, per_chip):
    wg = PACK // (2 * cap)
    me = lax.axis_index("chan")
    row = source_row(src_ref)
    slots = row.shape[1]
    _, _, _, own_row, rank_row = chip_ranks(row, per_chip)
    own_row = jnp.concatenate([own_row] * (2 * wg), axis=1)
    rank_row = jnp.concatenate([rank_row] * (2 * wg), axis=1)
    lane_g, lane_r = packed(cap, (PACK, 1), 0)
    wide = 2 * wg * slots
    aligned = (lane_g == shift(iota((1, wide), 1), slots)) & (lane_r == rank_row)
    place = [jnp.where(aligned & (own_row == (shift(me, 2) ^ d)), 1.0, 0.0).astype(BF) for d in names]
    return jnp.concatenate(place, axis=0)


def place_sources(place, xrefs, xs):
    groups, part, _ = xrefs[0].shape
    chips = place.shape[0] // PACK
    wg = place.shape[1] // LANES
    wp = groups * wg // 2
    for p in range(len(xrefs) // chips):
        got = jnp.concatenate([xrefs[p * chips + n][...] for n in range(chips)], axis=2)
        got = jnp.dot(got.reshape(groups * part, chips * PACK), place, preferred_element_type=F32)
        for w in range(2 * wp):
            b, i = w // wg, w % wg
            at = pl.ds(p * part * XPITCH + (w // wp) * WROWS + w % wp, part, stride=XPITCH)
            xs[at, :] = got[b * part : (b + 1) * part, i * LANES : (i + 1) * LANES]
        for w2 in range(2):
            for w in range(wp, WROWS):
                at = pl.ds(p * part * XPITCH + w2 * WROWS + w, part, stride=XPITCH)
                xs[at, :] = jnp.zeros((part, LANES), F32)


def tables_kernel(
    nchan, spec_ref, got_ref, own_pairs, got_pairs, slot_ref, recv_ref, hot_ref, count_ref, own, got, named, tally, in_sem
):
    _, windows, half, chans = got.shape
    slots = own_pairs.shape[0]
    bins = slot_ref.shape[1]
    per = bins // nchan
    wp = windows // 2
    core = lax.axis_index("chan") & 1
    mine = pl.ds(pl.multiple_of(core * half, half), half)
    ins = []
    for k in range(2):
        ins.append(pltpu.make_async_copy(spec_ref.at[k, :, mine], own.at[k], in_sem.at[k, 0]))
        ins.append(pltpu.make_async_copy(got_ref.at[k, :, mine], got.at[k], in_sem.at[k, 1]))
    for copy in ins:
        copy.start()

    r = iota((bins, 1), 0)
    block, rest = shift(r, per), r & (per - 1)
    side, chip = shift(block, nchan // 2), block & (nchan // 2 - 1)
    order = (chip * 2 + side) * per + rest
    row_bin = jnp.sum(jnp.where(slot_ref[...] == order, iota((1, bins), 1), 0), axis=1, keepdims=True)
    named[...] = jnp.broadcast_to(row_bin, named.shape)
    tally[...] = jnp.zeros_like(tally)

    def one_step(step, carry):
        total = tally[...]
        for u in range(GROUP):
            s = step * GROUP + u
            bin_of = named[...]
            mine_hit = jnp.where(own_pairs[pl.ds(s, 1), :] == bin_of, 1.0, 0.0)
            hot_ref[s, :, pl.ds(0, chans)] = mine_hit.astype(BF)
            hot_ref[s, :, pl.ds(chans, chans)] = jnp.where(got_pairs[pl.ds(s, 1), :] == bin_of, 1.0, 0.0).astype(BF)
            total = total + mine_hit
        tally[...] = total
        return carry

    lax.fori_loop(0, slots // GROUP, one_step, 0)
    count_ref[...] = lax.dot_general(
        jnp.ones((8, chans), BF), tally[...].astype(BF), (((1,), (1,)), ((), ())), preferred_element_type=F32
    )

    turn = frequency_first(wp)
    for copy in ins:
        copy.wait()
    for b in range(half // FB):
        at = pl.ds(b * FB, FB)
        for k in range(2):
            for w2 in range(2):
                ws = pl.ds(w2 * wp, wp)
                both = jnp.concatenate([own[k, ws, at, :], got[k, ws, at, :]], axis=2).reshape(wp * FB, 2 * chans)
                moved = jnp.dot(turn, both, preferred_element_type=F32).astype(BF)
                recv_ref[at, pl.ds((2 * k + w2) * WROWS, WROWS), :] = moved.reshape(FB, WROWS, 2 * chans)


def tables(spectra, got, own_pairs, got_pairs, slot_of_bin, nchan):
    _, windows, freqs, chans = spectra.shape
    half = freqs // 2
    slots = own_pairs.shape[0]
    bins = slot_of_bin.shape[0]
    side = ((2, windows, half, chans), BF)
    square = ((bins, chans), I32)
    return pl.pallas_call(
        functools.partial(tables_kernel, nchan),
        in_specs=[ANY, ANY, VMEM, VMEM, VMEM],
        out_specs=[VMEM, VMEM, VMEM],
        out_shape=[
            jax.ShapeDtypeStruct((half, 4 * WROWS, 2 * chans), BF),
            jax.ShapeDtypeStruct((slots, bins, 2 * chans), BF),
            jax.ShapeDtypeStruct((8, bins), F32),
        ],
        scratch_shapes=[
            pltpu.VMEM(*side),
            pltpu.VMEM(*side),
            pltpu.VMEM(*square),
            pltpu.VMEM((bins, chans), F32),
            pltpu.SemaphoreType.DMA((2, 2)),
        ],
        compiler_params=params(side, side, square, square, ((bins, bins), I32)),
        name="tables",
    )(spectra, got, own_pairs, got_pairs, slot_of_bin[None, :])


def early_kernel(cap, names, late, per_chip, src_ref, *refs):
    *xrefs, xs_ref, late_ref = refs
    place_sources(placement(cap, names, src_ref, per_chip), xrefs, xs_ref)
    late_ref[...] = placement(cap, late, src_ref, per_chip)


def place_early(arrays, names, late, src_ids, cap, per_chip):
    groups, part, _ = arrays[0].shape
    count = len(arrays) // len(names) * part
    shape = ((count + 1) * XPITCH + 7, LANES)
    return pl.pallas_call(
        functools.partial(early_kernel, cap, names, late, per_chip),
        in_specs=[VMEM] * (1 + len(arrays)),
        out_specs=[VMEM, VMEM],
        out_shape=[
            jax.ShapeDtypeStruct(shape, F32),
            jax.ShapeDtypeStruct((len(late) * PACK, PACK // (2 * cap) * LANES), BF),
        ],
        compiler_params=params(*staging(arrays, names)),
        name="place_early",
    )(src_ids, *arrays)


def cross_kernel(inputs, *refs):
    place_ref, recv, hot, cos_ref, sin_ref, count_ref, xs_early = refs[:7]
    xrefs, refs = refs[7 : 7 + inputs], refs[7 + inputs :]
    outs, refs = refs[:2], refs[2:]
    xs, cross, sums, whole = refs
    count, _, chans2 = recv.shape
    slots, bins, _ = hot.shape
    place_sources(place_ref[...], xrefs, xs)
    imag = iota((2 * WROWS, LANES), 1) >= slots
    quarter = shift(iota((1, 4 * 4 * WROWS), 1), 4 * WROWS)
    masks = [jnp.where(quarter == i, 1.0, 0.0).astype(BF) for i in range(4)]

    def one_group(step, carry):
        for sub in range(2 * min(GROUPS, count // 8)):
            g, q = step * min(GROUPS, count // 8) + sub // 2, sub % 2
            lefts = []
            for j in range(4 * q, 4 * q + 4):
                at = pl.ds((g * 8 + j) * XPITCH, 2 * WROWS)
                x = (xs_early[at, :] + xs[at, :]).astype(BF)
                upper = jnp.where(imag, -x, x)
                if j:
                    upper = pltpu.roll(upper, j, 1)
                lefts += [upper, pltpu.roll(x, slots + j, 1)]
            left = jnp.transpose(jnp.concatenate(lefts, axis=0))
            left = jnp.concatenate([left * mask for mask in masks], axis=0)
            right = recv[pl.ds(g * 8 + 4 * q, 4)].reshape(4 * 4 * WROWS, chans2)
            got = jnp.dot(left, right, preferred_element_type=F32)
            for i in range(4):
                j = 4 * q + i
                base = pl.multiple_of(g * (8 * PITCH) + j * (PITCH - 1), 8)
                for h in range(2):
                    side = got[i * LANES : (i + 1) * LANES, h * LANES : (h + 1) * LANES]
                    cross[h, pl.ds(base, LANES), :] = side
                    if j:
                        cross[h, pl.ds(pl.multiple_of(base + LANES, 8), 8), :] = side[:8]
        return carry

    lax.fori_loop(0, count // (8 * min(GROUPS, count // 8)), one_group, 0)

    sums[...] = jnp.zeros_like(sums)

    def one_turn(step, carry):
        lefts = []
        for u in range(TURN):
            s = step * TURN + u
            parts = []
            for turn in range(2):
                at = pl.ds(s + turn * slots, count, stride=PITCH)
                parts.append(jnp.concatenate([cross[0, at, :], cross[1, at, :]], axis=1))
            x = jnp.concatenate(parts, axis=0)
            high = x.astype(BF)
            low = (x - high.astype(F32)).astype(BF)
            lefts.append(jnp.concatenate([high, low], axis=0))
        left = jnp.concatenate(lefts, axis=1)
        right = jnp.concatenate([hot[step * TURN + u] for u in range(TURN)], axis=1)
        sums[...] += lax.dot_general(left, right, (((1,), (1,)), ((), ())), preferred_element_type=F32)
        return carry

    lax.fori_loop(0, slots // TURN, one_turn, 0)
    total = sums[pl.ds(0, 2 * count), :] + sums[pl.ds(2 * count, 2 * count), :]
    table = jnp.concatenate([cos_ref[...], sin_ref[...]], axis=0)
    whole[...] = lax.dot_general(total, table, (((0,), (0,)), ((), ())), precision=lax.Precision.HIGHEST, preferred_element_type=F32)
    core = lax.axis_index("chan") & 1
    blocks = outs[0].shape[0]
    per = bins // (2 * blocks)
    crows = count_ref.shape[0]
    for which, dest in ((core, outs[0]), (1 - core, outs[1])):
        for d in range(blocks):
            start = pl.multiple_of((which * blocks + d) * per, per)
            dest[d, pl.ds(0, per), :] = whole[pl.ds(start, per), :]
            dest[d, pl.ds(per, crows), :] = count_ref[...]


def staging(arrays, names):
    groups, part, _ = arrays[0].shape
    chips = len(names)
    return [((groups * part, 4 * PACK), F32), ((groups * part, chips * PACK), BF), ((chips * PACK, 4 * PACK), F32)]


def cross_and_bin(arrays, names, xs_early, place, recv, hot, counts, cos, sin, nchan):
    _, bins, chans2 = hot.shape
    lags = cos.shape[1]
    count = recv.shape[0]
    per = bins // nchan
    out = jax.ShapeDtypeStruct((nchan // 2, per + 8, lags), F32)
    scratch = [
        (xs_early.shape, F32),
        ((2, (count + 1) * PITCH, chans2 // 2), F32),
        ((4 * count, bins), F32),
        ((bins, lags), F32),
    ]
    buffers = scratch + staging(arrays, names)
    return pl.pallas_call(
        functools.partial(cross_kernel, len(arrays)),
        in_specs=[VMEM] * (7 + len(arrays)),
        out_specs=[VMEM, VMEM],
        out_shape=[out, out],
        scratch_shapes=[pltpu.VMEM(shape, kind) for shape, kind in scratch],
        compiler_params=params(*buffers, *([(hot.shape, BF)] if hot.size > BIG else [])),
        name="cross_and_bin",
    )(place, recv, hot, cos, sin, counts, xs_early, *arrays)


def swap(x, size, bit):
    return lax.ppermute(x, "chan", [(i, i ^ bit) for i in range(size)])


def gathered(nchan, pieces, chip):
    rest = [1 << k for k in range(1, nchan.bit_length() - 1)]
    result = []
    held = [[x] for x in chip]
    names = [[0] for _ in chip]
    for hop in range(len(rest)):
        bits = [rest[hop] if p % 2 == 0 else rest[-1 - hop] for p in range(pieces)]
        early = [swap(chip[p], nchan, bits[p]) for p in range(pieces)]
        for p, bit in enumerate(bits):
            held[p] = held[p] + [early[p]] + [swap(x, nchan, bit) for x in held[p][1:]]
            names[p] = names[p] + [name ^ bit for name in names[p]]
    for p in range(pieces):
        result.append([held[p][names[p].index(2 * d)] for d in range(len(held[p]))])
    return result


def chip_sources(nchan, cap, pieces, spectra, src_ids):
    keep, send = pick(spectra, src_ids, cap)
    got = swap(send, nchan, 1)
    part = keep.shape[1] // pieces
    return [keep[:, p * part : (p + 1) * part] + got[:, p * part : (p + 1) * part] for p in range(pieces)]


def finish(nchan, nfreq, cap, chip, table, spectra, src_ids, pairs_own, got_pairs, slot_of_bin):
    _, windows, freqs, chans = spectra.shape
    half = freqs // 2
    bins = slot_of_bin.shape[0]
    me = lax.axis_index("chan")
    core = me & 1
    rest = [1 << k for k in range(1, nchan.bit_length() - 1)]
    arrays = gathered(nchan, len(chip), chip)
    spectra_sent, chip = lax.optimization_barrier((spectra, chip))
    got_spec = swap(spectra_sent, nchan, 1)
    chips = len(arrays[0])
    early, late = list(range(chips - chips // 4)), list(range(chips - chips // 4, chips))
    first = [held[d] for held in arrays for d in early]
    recv, hot, counts = tables(spectra, got_spec, pairs_own, got_pairs, slot_of_bin, nchan)
    counts, first = lax.optimization_barrier((counts, first))
    xs_early, place = place_early(first, early, late, src_ids, cap, 2 * chans)
    counts = counts[0].reshape(bins // NLAG, NLAG)
    last = [held[d] for held in arrays for d in late]
    out = cross_and_bin(last, late, xs_early, place, recv, hot, counts, *table, nchan)
    mine, other = out

    per = bins // nchan
    mine = mine + swap(other, nchan, 1)
    at = me // 2
    if nchan // 2 <= 4:
        total = lax.dynamic_index_in_dim(mine, at, 0, keepdims=False)
        for move in range(nchan // 2 - 1, 0, -1):
            total = total + swap(lax.dynamic_index_in_dim(mine, at ^ move, 0, keepdims=False), nchan, 2 * move)
    else:
        for bit in rest[::-1]:
            size = mine.shape[0] // 2
            up = (me & bit) != 0
            low, high = mine[:size], mine[size:]
            mine = jnp.where(up, high, low) + swap(jnp.where(up, low, high), nchan, bit)
        total = mine[0]
    owned = total[:per]
    parts = [owned]
    if nfreq <= 4:
        parts += [lax.ppermute(owned, "freq", [(i, i ^ k) for i in range(nfreq)]) for k in range(nfreq - 1, 0, -1)]
    else:
        for k in range(nfreq.bit_length() - 1):
            owned = parts[0]
            parts = [owned + lax.ppermute(owned, "freq", [(i, i ^ (1 << k)) for i in range(nfreq)])]
    counted = total[per : per + bins // NLAG].reshape(bins)
    count = lax.dynamic_slice(counted, ((core * (nchan // 2) + at) * per,), (per,))
    return parts, count


def scaled(parts, count):
    total = parts[0]
    for part in parts[1:]:
        total = total + part
    return total / jnp.sqrt(jnp.maximum(count, 1.0))[:, None]


def body(nchan, nfreq, spectra, src_ids, pair_bin, slot_of_bin):
    chans = spectra.shape[3]
    slots = src_ids.shape[0] * src_ids.shape[1]
    pieces = 2
    pairs_own = pair_bin.reshape(slots, chans)
    got_pairs = swap(pairs_own, nchan, 1)
    windows, half = spectra.shape[1], spectra.shape[2] // 2
    anchor = (lax.axis_index("freq") * 2 + (lax.axis_index("chan") & 1)) * half
    table = lag_basis(anchor, half, F, NLAG, windows)
    chip = chip_sources(nchan, CAP, pieces, spectra, src_ids)
    chip, table, got_pairs = lax.optimization_barrier((chip, table, got_pairs))
    owner = src_ids // (2 * chans)
    loads = jnp.sum((owner[None] == lax.iota(I32, nchan // 2)[:, None, None]).astype(I32), axis=(1, 2))
    fits = jnp.max(loads) <= CAP

    def small(parts, count, *args):
        return scaled(parts, count)

    def large(parts, count, *args):
        chip = chip_sources(nchan, slots, pieces, *args[1:3])
        return scaled(*finish(nchan, nfreq, slots, chip, *args))

    args = (table, spectra, src_ids, pairs_own, got_pairs, slot_of_bin)
    parts, count = finish(nchan, nfreq, CAP, chip, *args)
    return lax.cond(fits, small, large, parts, count, *args)


def solution(mesh):
    return jax.shard_map(
        functools.partial(body, mesh.shape["chan"], mesh.shape["freq"]),
        mesh=mesh,
        in_specs=(P(None, None, "freq", "chan"), P(), P(None, None, "chan"), P()),
        out_specs=P("chan", None),
        check_vma=False,
    )
```

```python
import functools
import math

import jax
import jax.numpy as jnp
from jax import lax
from jax.experimental import pallas as pl
from jax.experimental.pallas import tpu as pltpu
from jax.sharding import PartitionSpec as P

F = 1024
NLAG = 256
BF = jnp.bfloat16
F8 = jnp.float8_e4m3fn
F8_TOP = 224.0
F32 = jnp.float32
I32 = jnp.int32
FB = 16
WROWS = 16
LANES = 128
SLACK = 6 * 1024 * 1024
PITCH = LANES + 9
TURN = 32
BIG = 8 * 1024 * 1024
CAP = 25
PACK = 2 * LANES
XPITCH = 2 * WROWS + 1
GROUPS = 16
GROUP = 8
ANY = pl.BlockSpec(memory_space=pl.ANY)
VMEM = pl.BlockSpec(memory_space=pltpu.VMEM)


def lag_basis(anchor, amount, totals, lag_count, windows):
    frequency = anchor + lax.iota(I32, amount)
    shifts = lax.iota(I32, lag_count) - lag_count // 2
    phases = frequency[:, None] * shifts[None, :] % (2 * totals)
    angles = phases.astype(F32) * (math.pi / totals)
    factor = 1.0 / math.sqrt(windows * totals)
    return jnp.cos(angles) * factor, -jnp.sin(angles) * factor


def params(*buffers):
    used = sum(math.prod(shape) * jnp.dtype(kind).itemsize for shape, kind in buffers)
    return pltpu.CompilerParams(vmem_limit_bytes=used + SLACK)


def iota(shape, dim):
    return lax.broadcasted_iota(I32, shape, dim)


def shift(values, size):
    return lax.shift_right_logical(values, jnp.int32(size.bit_length() - 1))


def as_column(row):
    size = row.shape[1]
    eye = iota((size, size), 0) == iota((size, size), 1)
    return jnp.sum(jnp.where(eye, row, 0), axis=1, keepdims=True)


def source_row(src_ref):
    return jnp.concatenate([src_ref[t : t + 1, :] for t in range(src_ref.shape[0])], axis=1)


def chip_ranks(row, per_chip):
    size = row.shape[1]
    own_row = shift(row, per_chip)
    col = as_column(row)
    own_col = shift(col, per_chip)
    same = own_col == own_row
    q0, q1 = iota((size, size), 0), iota((size, size), 1)
    rank_col = jnp.sum(jnp.where(same & (q1 < q0), 1, 0), axis=1, keepdims=True)
    rank_row = jnp.sum(jnp.where(same & (q0 < q1), 1, 0), axis=0, keepdims=True)
    return col, own_col, rank_col, own_row, rank_row


def packed(cap, shape, dim):
    lane = iota(shape, dim)
    group = jnp.zeros(shape, I32)
    for j in range(1, PACK // cap + 1):
        group = group + jnp.where(lane >= j * cap, 1, 0)
    return group, lane - group * cap


def frequency_first(rows):
    shape = (FB * WROWS, rows * FB)
    r, c = iota(shape, 0), iota(shape, 1)
    hit = (shift(r, WROWS) == (c & (FB - 1))) & ((r & (WROWS - 1)) == shift(c, FB))
    return jnp.where(hit, 1.0, 0.0).astype(BF)


def pick_kernel(cap, src_ref, spec_ref, keep_ref, send_ref, buf, res, in_sem, out_sem):
    _, _, freqs, chans = spec_ref.shape
    half = freqs // 2
    wg = PACK // (2 * cap)
    groups = in_sem.shape[0]
    me = lax.axis_index("chan")
    core = me & 1
    ins = []
    for b in range(groups):
        for k in range(2):
            at = pl.ds(b * wg, wg)
            ins.append(pltpu.make_async_copy(spec_ref.at[k, at], buf.at[k, at], in_sem.at[b, k]))
    for copy in ins:
        copy.start()

    row = source_row(src_ref)
    col, own_col, rank_col, _, _ = chip_ranks(row, 2 * chans)
    slots = row.shape[1]
    _, lane_r = packed(cap, (slots, PACK), 1)
    match = (own_col == shift(me, 2)) & (rank_col == lane_r)
    local = col - me * chans
    found = jnp.sum(jnp.where(match, local + 1, 0), axis=0, keepdims=True) - 1
    shape = (2 * wg * chans, PACK)
    lane_g, _ = packed(cap, (1, PACK), 1)
    r = iota(shape, 0)
    picker = jnp.where((shift(r, chans) == lane_g) & ((r & (chans - 1)) == found), 1.0, 0.0).astype(BF)

    mine = pl.multiple_of(core * half, half)
    other = pl.multiple_of((1 - core) * half, half)
    outs = []
    turn = 2 if groups % 2 == 0 else 1
    for b0 in range(0, groups, turn):
        lefts = []
        for b in range(b0, b0 + turn):
            for copy in ins[2 * b : 2 * b + 2]:
                copy.wait()
            lefts.append(jnp.concatenate([buf[k, b * wg + i] for i in range(wg) for k in range(2)], axis=1))
        left = jnp.concatenate(lefts, axis=0)
        got = []
        for h in range(PACK // LANES):
            first, last = h * LANES // cap * chans, min(-(-(h + 1) * LANES // cap), 2 * wg) * chans
            part = picker[first:last, h * LANES : (h + 1) * LANES]
            got.append(jnp.dot(left[:, first:last], part, preferred_element_type=F32))
        got = jnp.concatenate(got, axis=1).astype(BF)
        for b in range(b0, b0 + turn):
            res[b] = got[(b - b0) * freqs : (b - b0 + 1) * freqs]
        for n, (start, ref) in enumerate(((other, send_ref), (mine, keep_ref))):
            at = pl.ds(b0, turn)
            outs.append(pltpu.make_async_copy(res.at[at, pl.ds(start, half)], ref.at[at], out_sem.at[b0, n]))
            outs[-1].start()
    for copy in outs:
        copy.wait()


def pick(spectra, src_ids, cap):
    _, windows, freqs, chans = spectra.shape
    half = freqs // 2
    groups = windows // (PACK // (2 * cap))
    shape = (groups, half, PACK)
    out = jax.ShapeDtypeStruct(shape, BF)
    return pl.pallas_call(
        functools.partial(pick_kernel, cap),
        in_specs=[VMEM, ANY],
        out_specs=[ANY, ANY],
        out_shape=[out, out],
        scratch_shapes=[
            pltpu.VMEM(spectra.shape, BF),
            pltpu.VMEM((groups, freqs, PACK), BF),
            pltpu.SemaphoreType.DMA((groups, 2)),
            pltpu.SemaphoreType.DMA((groups, 2)),
        ],
        compiler_params=params((spectra.shape, BF), (shape, BF), (shape, BF)),
        name="pick_sources",
    )(src_ids, spectra)


def largest(values, rows=16):
    lanes = values.shape[-1]
    return jnp.max(jnp.abs(values).reshape(-1, rows, lanes), axis=0)


def placement(cap, names, src_ref, per_chip):
    wg = PACK // (2 * cap)
    me = lax.axis_index("chan")
    row = source_row(src_ref)
    slots = row.shape[1]
    _, _, _, own_row, rank_row = chip_ranks(row, per_chip)
    own_row = jnp.concatenate([own_row] * (2 * wg), axis=1)
    rank_row = jnp.concatenate([rank_row] * (2 * wg), axis=1)
    lane_g, lane_r = packed(cap, (PACK, 1), 0)
    wide = 2 * wg * slots
    aligned = (lane_g == shift(iota((1, wide), 1), slots)) & (lane_r == rank_row)
    place = [jnp.where(aligned & (own_row == (shift(me, 2) ^ d)), 1.0, 0.0).astype(BF) for d in names]
    return jnp.concatenate(place, axis=0)


def place_sources(place, xrefs, xs):
    groups, part, _ = xrefs[0].shape
    chips = place.shape[0] // PACK
    wg = place.shape[1] // LANES
    wp = groups * wg // 2
    for p in range(len(xrefs) // chips):
        got = jnp.concatenate([xrefs[p * chips + n][...] for n in range(chips)], axis=2)
        got = jnp.dot(got.reshape(groups * part, chips * PACK), place, preferred_element_type=F32)
        for w in range(2 * wp):
            b, i = w // wg, w % wg
            at = pl.ds(p * part * XPITCH + (w // wp) * WROWS + w % wp, part, stride=XPITCH)
            xs[at, :] = got[b * part : (b + 1) * part, i * LANES : (i + 1) * LANES]
        for w2 in range(2):
            for w in range(wp, WROWS):
                at = pl.ds(p * part * XPITCH + w2 * WROWS + w, part, stride=XPITCH)
                xs[at, :] = jnp.zeros((part, LANES), F32)


def tables_kernel(
    nchan, spec_ref, got_ref, own_pairs, got_pairs, slot_ref, *refs
):
    recv_ref, hot_ref, *narrow, count_ref, top_ref, own, got, named, tally, in_sem = refs
    _, windows, half, chans = got.shape
    slots = own_pairs.shape[0]
    bins = slot_ref.shape[1]
    per = bins // nchan
    wp = windows // 2
    core = lax.axis_index("chan") & 1
    mine = pl.ds(pl.multiple_of(core * half, half), half)
    ins = []
    for k in range(2):
        ins.append(pltpu.make_async_copy(spec_ref.at[k, :, mine], own.at[k], in_sem.at[k, 0]))
        ins.append(pltpu.make_async_copy(got_ref.at[k, :, mine], got.at[k], in_sem.at[k, 1]))
    for copy in ins:
        copy.start()

    r = iota((bins, 1), 0)
    block, rest = shift(r, per), r & (per - 1)
    side, chip = shift(block, nchan // 2), block & (nchan // 2 - 1)
    order = (chip * 2 + side) * per + rest
    row_bin = jnp.sum(jnp.where(slot_ref[...] == order, iota((1, bins), 1), 0), axis=1, keepdims=True)
    named[...] = jnp.broadcast_to(row_bin, named.shape)
    tally[...] = jnp.zeros_like(tally)

    def one_step(step, carry):
        total = tally[...]
        for u in range(GROUP):
            s = step * GROUP + u
            bin_of = named[...]
            mine_hit = jnp.where(own_pairs[pl.ds(s, 1), :] == bin_of, 1.0, 0.0)
            hot_ref[s, :, pl.ds(0, chans)] = mine_hit.astype(BF)
            got_hit = jnp.where(got_pairs[pl.ds(s, 1), :] == bin_of, 1.0, 0.0)
            hot_ref[s, :, pl.ds(chans, chans)] = got_hit.astype(BF)
            for hot8_ref in narrow:
                hot8_ref[s, :, pl.ds(0, chans)] = mine_hit.astype(F8)
                hot8_ref[s, :, pl.ds(chans, chans)] = got_hit.astype(F8)
            total = total + mine_hit
        tally[...] = total
        return carry

    lax.fori_loop(0, slots // GROUP, one_step, 0)
    count_ref[...] = lax.dot_general(
        jnp.ones((8, chans), BF), tally[...].astype(BF), (((1,), (1,)), ((), ())), preferred_element_type=F32
    )

    turn = frequency_first(wp)
    for copy in ins:
        copy.wait()
    top = jnp.zeros(top_ref.shape, BF)
    for b in range(half // FB):
        at = pl.ds(b * FB, FB)
        for k in range(2):
            for w2 in range(2):
                ws = pl.ds(w2 * wp, wp)
                both = jnp.concatenate([own[k, ws, at, :], got[k, ws, at, :]], axis=2).reshape(wp * FB, 2 * chans)
                moved = jnp.dot(turn, both, preferred_element_type=F32).astype(BF)
                recv_ref[at, pl.ds((2 * k + w2) * WROWS, WROWS), :] = moved.reshape(FB, WROWS, 2 * chans)
                top = jnp.maximum(top, largest(moved))
    top_ref[...] = top


def tables(spectra, got, own_pairs, got_pairs, slot_of_bin, nchan):
    _, windows, freqs, chans = spectra.shape
    half = freqs // 2
    slots = own_pairs.shape[0]
    bins = slot_of_bin.shape[0]
    side = ((2, windows, half, chans), BF)
    square = ((bins, chans), I32)
    narrow = [jax.ShapeDtypeStruct((slots, bins, 2 * chans), F8)]
    narrow = narrow if narrow[0].size <= BIG else []
    return pl.pallas_call(
        functools.partial(tables_kernel, nchan),
        in_specs=[ANY, ANY, VMEM, VMEM, VMEM],
        out_specs=[VMEM] * (4 + len(narrow)),
        out_shape=[
            jax.ShapeDtypeStruct((half, 4 * WROWS, 2 * chans), BF),
            jax.ShapeDtypeStruct((slots, bins, 2 * chans), BF),
            *narrow,
            jax.ShapeDtypeStruct((8, bins), F32),
            jax.ShapeDtypeStruct((16, 2 * chans), BF),
        ],
        scratch_shapes=[
            pltpu.VMEM(*side),
            pltpu.VMEM(*side),
            pltpu.VMEM(*square),
            pltpu.VMEM((bins, chans), F32),
            pltpu.SemaphoreType.DMA((2, 2)),
        ],
        compiler_params=params(side, side, square, square, ((bins, bins), I32)),
        name="tables",
    )(spectra, got, own_pairs, got_pairs, slot_of_bin[None, :])


def early_kernel(cap, names, late, per_chip, src_ref, *refs):
    *xrefs, xs_ref, late_ref, top_ref = refs
    top_ref[...] = functools.reduce(jnp.maximum, [largest(x[...]) for x in xrefs])
    place_sources(placement(cap, names, src_ref, per_chip), xrefs, xs_ref)
    late_ref[...] = placement(cap, late, src_ref, per_chip)


def place_early(arrays, names, late, src_ids, cap, per_chip):
    groups, part, _ = arrays[0].shape
    count = len(arrays) // len(names) * part
    shape = ((count + 1) * XPITCH + 7, LANES)
    return pl.pallas_call(
        functools.partial(early_kernel, cap, names, late, per_chip),
        in_specs=[VMEM] * (1 + len(arrays)),
        out_specs=[VMEM] * 3,
        out_shape=[
            jax.ShapeDtypeStruct(shape, F32),
            jax.ShapeDtypeStruct((len(late) * PACK, PACK // (2 * cap) * LANES), BF),
            jax.ShapeDtypeStruct((16, PACK), BF),
        ],
        compiler_params=params(*staging(arrays, names)),
        name="place_early",
    )(src_ids, *arrays)


def cross_kernel(inputs, hots, *refs):
    place_ref, recv, cos_ref, sin_ref, count_ref, xs_early, top_recv, top_early = refs[:8]
    xrefs, refs = refs[8 : 8 + inputs], refs[8 + inputs :]
    (hot, *narrow), refs = refs[:hots], refs[hots:]
    outs, refs = refs[:2], refs[2:]
    xs, cross, sums, whole = refs
    count, _, chans2 = recv.shape
    slots, bins, _ = hot.shape
    place_sources(place_ref[...], xrefs, xs)
    top_src = functools.reduce(jnp.maximum, [top_early[...]] + [largest(x[...]) for x in xrefs]).astype(F32)
    products = 2 * xrefs[0].shape[0] * place_ref.shape[1] // LANES
    bound = jnp.max(top_src, axis=(0, 1), keepdims=True) * jnp.max(top_recv[...].astype(F32), axis=(0, 1), keepdims=True)
    bound = jnp.maximum(bound * products, 1e-30) * (1.0 / 256)
    scale, unscale = F8_TOP / bound, bound * (1.0 / F8_TOP)
    imag = iota((2 * WROWS, LANES), 1) >= slots
    quarter = shift(iota((1, 4 * 4 * WROWS), 1), 4 * WROWS)
    masks = [jnp.where(quarter == i, 1.0, 0.0).astype(BF) for i in range(4)]

    def one_group(step, carry):
        for sub in range(2 * min(GROUPS, count // 8)):
            g, q = step * min(GROUPS, count // 8) + sub // 2, sub % 2
            lefts = []
            for j in range(4 * q, 4 * q + 4):
                at = pl.ds((g * 8 + j) * XPITCH, 2 * WROWS)
                x = (xs_early[at, :] + xs[at, :]).astype(BF)
                upper = jnp.where(imag, -x, x)
                if j:
                    upper = pltpu.roll(upper, j, 1)
                lefts += [upper, pltpu.roll(x, slots + j, 1)]
            left = jnp.transpose(jnp.concatenate(lefts, axis=0))
            left = jnp.concatenate([left * mask for mask in masks], axis=0)
            right = recv[pl.ds(g * 8 + 4 * q, 4)].reshape(4 * 4 * WROWS, chans2)
            got = jnp.dot(left, right, preferred_element_type=F32)
            for i in range(4):
                j = 4 * q + i
                base = pl.multiple_of(g * (8 * PITCH) + j * (PITCH - 1), 8)
                for h in range(2):
                    side = got[i * LANES : (i + 1) * LANES, h * LANES : (h + 1) * LANES]
                    cross[h, pl.ds(base, LANES), :] = side
                    if j:
                        cross[h, pl.ds(pl.multiple_of(base + LANES, 8), 8), :] = side[:8]
        return carry

    lax.fori_loop(0, count // (8 * min(GROUPS, count // 8)), one_group, 0)

    sums[...] = jnp.zeros_like(sums)

    def one_turn(step, carry):
        lefts, lows = [], []
        for u in range(TURN):
            s = step * TURN + u
            parts = []
            for turn in range(2):
                at = pl.ds(s + turn * slots, count, stride=PITCH)
                parts.append(jnp.concatenate([cross[0, at, :], cross[1, at, :]], axis=1))
            x = jnp.concatenate(parts, axis=0)
            high = x.astype(BF)
            low = x - high.astype(F32)
            if narrow:
                lefts.append(high)
                lows.append((low * scale).astype(F8))
            else:
                lefts.append(jnp.concatenate([high, low.astype(BF)], axis=0))
        left = jnp.concatenate(lefts, axis=1)
        right = jnp.concatenate([hot[step * TURN + u] for u in range(TURN)], axis=1)
        at = pl.ds(0, left.shape[0])
        sums[at, :] += lax.dot_general(left, right, (((1,), (1,)), ((), ())), preferred_element_type=F32)
        for hot8 in narrow:
            left = jnp.concatenate(lows, axis=1)
            right = jnp.concatenate([hot8[step * TURN + u] for u in range(TURN)], axis=1)
            at = pl.ds(2 * count, 2 * count)
            sums[at, :] += lax.dot_general(left, right, (((1,), (1,)), ((), ())), preferred_element_type=F32)
        return carry

    lax.fori_loop(0, slots // TURN, one_turn, 0)
    low = sums[pl.ds(2 * count, 2 * count), :]
    total = sums[pl.ds(0, 2 * count), :] + (low * unscale if narrow else low)
    table = jnp.concatenate([cos_ref[...], sin_ref[...]], axis=0)
    whole[...] = lax.dot_general(total, table, (((0,), (0,)), ((), ())), precision=lax.Precision.HIGHEST, preferred_element_type=F32)
    core = lax.axis_index("chan") & 1
    blocks = outs[0].shape[0]
    per = bins // (2 * blocks)
    crows = count_ref.shape[0]
    for which, dest in ((core, outs[0]), (1 - core, outs[1])):
        for d in range(blocks):
            start = pl.multiple_of((which * blocks + d) * per, per)
            dest[d, pl.ds(0, per), :] = whole[pl.ds(start, per), :]
            dest[d, pl.ds(per, crows), :] = count_ref[...]


def staging(arrays, names):
    groups, part, _ = arrays[0].shape
    chips = len(names)
    return [((groups * part, 4 * PACK), F32), ((groups * part, chips * PACK), BF), ((chips * PACK, 4 * PACK), F32)]


def cross_and_bin(arrays, names, xs_early, place, recv, hots, counts, tops, cos, sin, nchan):
    hot = hots[0]
    _, bins, chans2 = hot.shape
    lags = cos.shape[1]
    count = recv.shape[0]
    per = bins // nchan
    out = jax.ShapeDtypeStruct((nchan // 2, per + 8, lags), F32)
    scratch = [
        (xs_early.shape, F32),
        ((2, (count + 1) * PITCH, chans2 // 2), F32),
        ((4 * count, bins), F32),
        ((bins, lags), F32),
    ]
    buffers = scratch + staging(arrays, names)
    return pl.pallas_call(
        functools.partial(cross_kernel, len(arrays), len(hots)),
        in_specs=[VMEM] * (8 + len(arrays) + len(hots)),
        out_specs=[VMEM, VMEM],
        out_shape=[out, out],
        scratch_shapes=[pltpu.VMEM(shape, kind) for shape, kind in scratch],
        compiler_params=params(*buffers, *([(hot.shape, BF)] if hot.size > BIG else [])),
        name="cross_and_bin",
    )(place, recv, cos, sin, counts, xs_early, *tops, *arrays, *hots)


def swap(x, size, bit):
    return lax.ppermute(x, "chan", [(i, i ^ bit) for i in range(size)])


def gathered(nchan, pieces, chip):
    rest = [1 << k for k in range(1, nchan.bit_length() - 1)]
    result = []
    held = [[x] for x in chip]
    names = [[0] for _ in chip]
    for hop in range(len(rest)):
        bits = [rest[hop] if p % 2 == 0 else rest[-1 - hop] for p in range(pieces)]
        early = [swap(chip[p], nchan, bits[p]) for p in range(pieces)]
        for p, bit in enumerate(bits):
            held[p] = held[p] + [early[p]] + [swap(x, nchan, bit) for x in held[p][1:]]
            names[p] = names[p] + [name ^ bit for name in names[p]]
    for p in range(pieces):
        result.append([held[p][names[p].index(2 * d)] for d in range(len(held[p]))])
    return result


def chip_sources(nchan, cap, pieces, spectra, src_ids):
    keep, send = pick(spectra, src_ids, cap)
    got = swap(send, nchan, 1)
    part = keep.shape[1] // pieces
    return [keep[:, p * part : (p + 1) * part] + got[:, p * part : (p + 1) * part] for p in range(pieces)]


def finish(nchan, nfreq, cap, chip, table, spectra, src_ids, pairs_own, got_pairs, slot_of_bin):
    _, windows, freqs, chans = spectra.shape
    half = freqs // 2
    bins = slot_of_bin.shape[0]
    me = lax.axis_index("chan")
    core = me & 1
    rest = [1 << k for k in range(1, nchan.bit_length() - 1)]
    arrays = gathered(nchan, len(chip), chip)
    spectra_sent, chip = lax.optimization_barrier((spectra, chip))
    got_spec = swap(spectra_sent, nchan, 1)
    chips = len(arrays[0])
    early, late = list(range(chips - chips // 4)), list(range(chips - chips // 4, chips))
    first = [held[d] for held in arrays for d in early]
    recv, *hots, counts, top_recv = tables(spectra, got_spec, pairs_own, got_pairs, slot_of_bin, nchan)
    counts, first = lax.optimization_barrier((counts, first))
    xs_early, place, top_early = place_early(first, early, late, src_ids, cap, 2 * chans)
    counts = counts[0].reshape(bins // NLAG, NLAG)
    last = [held[d] for held in arrays for d in late]
    out = cross_and_bin(last, late, xs_early, place, recv, hots, counts, (top_recv, top_early), *table, nchan)
    mine, other = out

    per = bins // nchan
    mine = mine + swap(other, nchan, 1)
    at = me // 2
    if nchan // 2 <= 4:
        total = lax.dynamic_index_in_dim(mine, at, 0, keepdims=False)
        for move in range(nchan // 2 - 1, 0, -1):
            total = total + swap(lax.dynamic_index_in_dim(mine, at ^ move, 0, keepdims=False), nchan, 2 * move)
    else:
        for bit in rest[::-1]:
            size = mine.shape[0] // 2
            up = (me & bit) != 0
            low, high = mine[:size], mine[size:]
            mine = jnp.where(up, high, low) + swap(jnp.where(up, low, high), nchan, bit)
        total = mine[0]
    owned = total[:per]
    parts = [owned]
    if nfreq <= 4:
        parts += [lax.ppermute(owned, "freq", [(i, i ^ k) for i in range(nfreq)]) for k in range(nfreq - 1, 0, -1)]
    else:
        for k in range(nfreq.bit_length() - 1):
            owned = parts[0]
            parts = [owned + lax.ppermute(owned, "freq", [(i, i ^ (1 << k)) for i in range(nfreq)])]
    counted = total[per : per + bins // NLAG].reshape(bins)
    count = lax.dynamic_slice(counted, ((core * (nchan // 2) + at) * per,), (per,))
    return parts, count


def scaled(parts, count):
    total = parts[0]
    for part in parts[1:]:
        total = total + part
    return total / jnp.sqrt(jnp.maximum(count, 1.0))[:, None]


def body(nchan, nfreq, spectra, src_ids, pair_bin, slot_of_bin):
    chans = spectra.shape[3]
    slots = src_ids.shape[0] * src_ids.shape[1]
    pieces = 2
    pairs_own = pair_bin.reshape(slots, chans)
    got_pairs = swap(pairs_own, nchan, 1)
    windows, half = spectra.shape[1], spectra.shape[2] // 2
    anchor = (lax.axis_index("freq") * 2 + (lax.axis_index("chan") & 1)) * half
    table = lag_basis(anchor, half, F, NLAG, windows)
    chip = chip_sources(nchan, CAP, pieces, spectra, src_ids)
    chip, table, got_pairs = lax.optimization_barrier((chip, table, got_pairs))
    owner = src_ids // (2 * chans)
    loads = jnp.sum((owner[None] == lax.iota(I32, nchan // 2)[:, None, None]).astype(I32), axis=(1, 2))
    fits = jnp.max(loads) <= CAP

    def small(parts, count, *args):
        return scaled(parts, count)

    def large(parts, count, *args):
        chip = chip_sources(nchan, slots, pieces, *args[1:3])
        return scaled(*finish(nchan, nfreq, slots, chip, *args))

    args = (table, spectra, src_ids, pairs_own, got_pairs, slot_of_bin)
    parts, count = finish(nchan, nfreq, CAP, chip, *args)
    return lax.cond(fits, small, large, parts, count, *args)


def solution(mesh):
    return jax.shard_map(
        functools.partial(body, mesh.shape["chan"], mesh.shape["freq"]),
        mesh=mesh,
        in_specs=(P(None, None, "freq", "chan"), P(), P(None, None, "chan"), P()),
        out_specs=P("chan", None),
        check_vma=False,
    )
```

```python
import functools
import math

import jax
import jax.numpy as jnp
from jax import lax
from jax.experimental import pallas as pl
from jax.experimental.pallas import tpu as pltpu
from jax.sharding import PartitionSpec as P

F = 1024
NLAG = 256
BF = jnp.bfloat16
F8 = jnp.float8_e4m3fn
F8_TOP = 224.0
F32 = jnp.float32
I32 = jnp.int32
FB = 16
WROWS = 16
LANES = 128
SLACK = 6 * 1024 * 1024
PITCH = LANES + 9
TURN = 32
BIG = 8 * 1024 * 1024
CAP = 25
PACK = 2 * LANES
XPITCH = 2 * WROWS + 1
GROUPS = 16
GROUP = 8
ANY = pl.BlockSpec(memory_space=pl.ANY)
VMEM = pl.BlockSpec(memory_space=pltpu.VMEM)


def lag_basis(anchor, amount, totals, lag_count, windows):
    frequency = anchor + lax.iota(I32, amount)
    shifts = lax.iota(I32, lag_count) - lag_count // 2
    phases = frequency[:, None] * shifts[None, :] % (2 * totals)
    angles = phases.astype(F32) * (math.pi / totals)
    factor = 1.0 / math.sqrt(windows * totals)
    return jnp.cos(angles) * factor, -jnp.sin(angles) * factor


def params(*buffers):
    used = sum(math.prod(shape) * jnp.dtype(kind).itemsize for shape, kind in buffers)
    return pltpu.CompilerParams(vmem_limit_bytes=used + SLACK)


def iota(shape, dim):
    return lax.broadcasted_iota(I32, shape, dim)


def shift(values, size):
    return lax.shift_right_logical(values, jnp.int32(size.bit_length() - 1))


def as_column(row):
    size = row.shape[1]
    eye = iota((size, size), 0) == iota((size, size), 1)
    return jnp.sum(jnp.where(eye, row, 0), axis=1, keepdims=True)


def source_row(src_ref):
    return jnp.concatenate([src_ref[t : t + 1, :] for t in range(src_ref.shape[0])], axis=1)


def chip_ranks(row, per_chip):
    size = row.shape[1]
    own_row = shift(row, per_chip)
    col = as_column(row)
    own_col = shift(col, per_chip)
    same = own_col == own_row
    q0, q1 = iota((size, size), 0), iota((size, size), 1)
    rank_col = jnp.sum(jnp.where(same & (q1 < q0), 1, 0), axis=1, keepdims=True)
    rank_row = jnp.sum(jnp.where(same & (q0 < q1), 1, 0), axis=0, keepdims=True)
    return col, own_col, rank_col, own_row, rank_row


def packed(cap, shape, dim):
    lane = iota(shape, dim)
    group = jnp.zeros(shape, I32)
    for j in range(1, PACK // cap + 1):
        group = group + jnp.where(lane >= j * cap, 1, 0)
    return group, lane - group * cap


def frequency_first(rows):
    shape = (FB * WROWS, rows * FB)
    r, c = iota(shape, 0), iota(shape, 1)
    hit = (shift(r, WROWS) == (c & (FB - 1))) & ((r & (WROWS - 1)) == shift(c, FB))
    return jnp.where(hit, 1.0, 0.0).astype(BF)


def pick_kernel(cap, src_ref, spec_ref, keep_ref, send_ref, buf, res, in_sem, out_sem):
    _, _, freqs, chans = spec_ref.shape
    half = freqs // 2
    wg = PACK // (2 * cap)
    groups = in_sem.shape[0]
    me = lax.axis_index("chan")
    core = me & 1
    ins = []
    for b in range(groups):
        for k in range(2):
            at = pl.ds(b * wg, wg)
            ins.append(pltpu.make_async_copy(spec_ref.at[k, at], buf.at[k, at], in_sem.at[b, k]))
    for copy in ins:
        copy.start()

    row = source_row(src_ref)
    col, own_col, rank_col, _, _ = chip_ranks(row, 2 * chans)
    slots = row.shape[1]
    _, lane_r = packed(cap, (slots, PACK), 1)
    match = (own_col == shift(me, 2)) & (rank_col == lane_r)
    local = col - me * chans
    found = jnp.sum(jnp.where(match, local + 1, 0), axis=0, keepdims=True) - 1
    shape = (2 * wg * chans, PACK)
    lane_g, _ = packed(cap, (1, PACK), 1)
    r = iota(shape, 0)
    picker = jnp.where((shift(r, chans) == lane_g) & ((r & (chans - 1)) == found), 1.0, 0.0).astype(BF)

    mine = pl.multiple_of(core * half, half)
    other = pl.multiple_of((1 - core) * half, half)
    outs = []
    turn = 3 if groups % 3 == 0 else 1
    for b0 in range(0, groups, turn):
        lefts = []
        for b in range(b0, b0 + turn):
            for copy in ins[2 * b : 2 * b + 2]:
                copy.wait()
            lefts.append(jnp.concatenate([buf[k, b * wg + i] for i in range(wg) for k in range(2)], axis=1))
        left = jnp.concatenate(lefts, axis=0)
        got = []
        for h in range(PACK // LANES):
            first, last = h * LANES // cap * chans, min(-(-(h + 1) * LANES // cap), 2 * wg) * chans
            part = picker[first:last, h * LANES : (h + 1) * LANES]
            got.append(jnp.dot(left[:, first:last], part, preferred_element_type=F32))
        got = jnp.concatenate(got, axis=1).astype(BF)
        for b in range(b0, b0 + turn):
            res[b] = got[(b - b0) * freqs : (b - b0 + 1) * freqs]
        for n, (start, ref) in enumerate(((other, send_ref), (mine, keep_ref))):
            at = pl.ds(b0, turn)
            outs.append(pltpu.make_async_copy(res.at[at, pl.ds(start, half)], ref.at[at], out_sem.at[b0, n]))
            outs[-1].start()
    for copy in outs:
        copy.wait()


def pick(spectra, src_ids, cap):
    _, windows, freqs, chans = spectra.shape
    half = freqs // 2
    groups = windows // (PACK // (2 * cap))
    shape = (groups, half, PACK)
    out = jax.ShapeDtypeStruct(shape, BF)
    return pl.pallas_call(
        functools.partial(pick_kernel, cap),
        in_specs=[VMEM, ANY],
        out_specs=[ANY, ANY],
        out_shape=[out, out],
        scratch_shapes=[
            pltpu.VMEM(spectra.shape, BF),
            pltpu.VMEM((groups, freqs, PACK), BF),
            pltpu.SemaphoreType.DMA((groups, 2)),
            pltpu.SemaphoreType.DMA((groups, 2)),
        ],
        compiler_params=params((spectra.shape, BF), (shape, BF), (shape, BF)),
        name="pick_sources",
    )(src_ids, spectra)


def largest(values, rows=16):
    lanes = values.shape[-1]
    return jnp.max(jnp.abs(values).reshape(-1, rows, lanes), axis=0)


def placement(cap, names, src_ref, per_chip):
    wg = PACK // (2 * cap)
    me = lax.axis_index("chan")
    row = source_row(src_ref)
    slots = row.shape[1]
    _, _, _, own_row, rank_row = chip_ranks(row, per_chip)
    own_row = jnp.concatenate([own_row] * (2 * wg), axis=1)
    rank_row = jnp.concatenate([rank_row] * (2 * wg), axis=1)
    lane_g, lane_r = packed(cap, (PACK, 1), 0)
    wide = 2 * wg * slots
    aligned = (lane_g == shift(iota((1, wide), 1), slots)) & (lane_r == rank_row)
    place = [jnp.where(aligned & (own_row == (shift(me, 2) ^ d)), 1.0, 0.0).astype(BF) for d in names]
    return jnp.concatenate(place, axis=0)


def place_sources(place, xrefs, xs):
    groups, part, _ = xrefs[0].shape
    chips = place.shape[0] // PACK
    wg = place.shape[1] // LANES
    wp = groups * wg // 2
    for p in range(len(xrefs) // chips):
        got = jnp.concatenate([xrefs[p * chips + n][...] for n in range(chips)], axis=2)
        got = jnp.dot(got.reshape(groups * part, chips * PACK), place, preferred_element_type=F32)
        for w in range(2 * wp):
            b, i = w // wg, w % wg
            at = pl.ds(p * part * XPITCH + (w // wp) * WROWS + w % wp, part, stride=XPITCH)
            xs[at, :] = got[b * part : (b + 1) * part, i * LANES : (i + 1) * LANES]
        for w2 in range(2):
            for w in range(wp, WROWS):
                at = pl.ds(p * part * XPITCH + w2 * WROWS + w, part, stride=XPITCH)
                xs[at, :] = jnp.zeros((part, LANES), F32)


def tables_kernel(
    nchan, spec_ref, got_ref, own_pairs, got_pairs, slot_ref, *refs
):
    recv_ref, hot_ref, *narrow, count_ref, top_ref, own, got, named, tally, in_sem = refs
    _, windows, half, chans = got.shape
    slots = own_pairs.shape[0]
    bins = slot_ref.shape[1]
    per = bins // nchan
    wp = windows // 2
    core = lax.axis_index("chan") & 1
    mine = pl.ds(pl.multiple_of(core * half, half), half)
    ins = []
    for k in range(2):
        ins.append(pltpu.make_async_copy(spec_ref.at[k, :, mine], own.at[k], in_sem.at[k, 0]))
        ins.append(pltpu.make_async_copy(got_ref.at[k, :, mine], got.at[k], in_sem.at[k, 1]))
    for copy in ins:
        copy.start()

    r = iota((bins, 1), 0)
    block, rest = shift(r, per), r & (per - 1)
    side, chip = shift(block, nchan // 2), block & (nchan // 2 - 1)
    order = (chip * 2 + side) * per + rest
    row_bin = jnp.sum(jnp.where(slot_ref[...] == order, iota((1, bins), 1), 0), axis=1, keepdims=True)
    named[...] = jnp.broadcast_to(row_bin, named.shape)
    tally[...] = jnp.zeros_like(tally)

    def one_step(step, carry):
        total = tally[...]
        for u in range(GROUP):
            s = step * GROUP + u
            bin_of = named[...]
            mine_hit = jnp.where(own_pairs[pl.ds(s, 1), :] == bin_of, 1.0, 0.0)
            hot_ref[s, :, pl.ds(0, chans)] = mine_hit.astype(BF)
            got_hit = jnp.where(got_pairs[pl.ds(s, 1), :] == bin_of, 1.0, 0.0)
            hot_ref[s, :, pl.ds(chans, chans)] = got_hit.astype(BF)
            for hot8_ref in narrow:
                hot8_ref[s, :, pl.ds(0, chans)] = mine_hit.astype(F8)
                hot8_ref[s, :, pl.ds(chans, chans)] = got_hit.astype(F8)
            total = total + mine_hit
        tally[...] = total
        return carry

    lax.fori_loop(0, slots // GROUP, one_step, 0)
    count_ref[...] = lax.dot_general(
        jnp.ones((8, chans), BF), tally[...].astype(BF), (((1,), (1,)), ((), ())), preferred_element_type=F32
    )

    turn = frequency_first(wp)
    for copy in ins:
        copy.wait()
    top = jnp.zeros(top_ref.shape, BF)
    for b in range(half // FB):
        at = pl.ds(b * FB, FB)
        for k in range(2):
            for w2 in range(2):
                ws = pl.ds(w2 * wp, wp)
                both = jnp.concatenate([own[k, ws, at, :], got[k, ws, at, :]], axis=2).reshape(wp * FB, 2 * chans)
                moved = jnp.dot(turn, both, preferred_element_type=F32).astype(BF)
                recv_ref[at, pl.ds((2 * k + w2) * WROWS, WROWS), :] = moved.reshape(FB, WROWS, 2 * chans)
                top = jnp.maximum(top, largest(moved))
    top_ref[...] = top


def tables(spectra, got, own_pairs, got_pairs, slot_of_bin, nchan):
    _, windows, freqs, chans = spectra.shape
    half = freqs // 2
    slots = own_pairs.shape[0]
    bins = slot_of_bin.shape[0]
    side = ((2, windows, half, chans), BF)
    square = ((bins, chans), I32)
    narrow = [jax.ShapeDtypeStruct((slots, bins, 2 * chans), F8)]
    narrow = narrow if narrow[0].size <= BIG else []
    return pl.pallas_call(
        functools.partial(tables_kernel, nchan),
        in_specs=[ANY, ANY, VMEM, VMEM, VMEM],
        out_specs=[VMEM] * (4 + len(narrow)),
        out_shape=[
            jax.ShapeDtypeStruct((half, 4 * WROWS, 2 * chans), BF),
            jax.ShapeDtypeStruct((slots, bins, 2 * chans), BF),
            *narrow,
            jax.ShapeDtypeStruct((8, bins), F32),
            jax.ShapeDtypeStruct((16, 2 * chans), BF),
        ],
        scratch_shapes=[
            pltpu.VMEM(*side),
            pltpu.VMEM(*side),
            pltpu.VMEM(*square),
            pltpu.VMEM((bins, chans), F32),
            pltpu.SemaphoreType.DMA((2, 2)),
        ],
        compiler_params=params(side, side, square, square, ((bins, bins), I32)),
        name="tables",
    )(spectra, got, own_pairs, got_pairs, slot_of_bin[None, :])


def early_kernel(cap, names, late, per_chip, src_ref, *refs):
    *xrefs, xs_ref, late_ref, top_ref = refs
    top_ref[...] = functools.reduce(jnp.maximum, [largest(x[...]) for x in xrefs])
    place_sources(placement(cap, names, src_ref, per_chip), xrefs, xs_ref)
    late_ref[...] = placement(cap, late, src_ref, per_chip)


def place_early(arrays, names, late, src_ids, cap, per_chip):
    groups, part, _ = arrays[0].shape
    count = len(arrays) // len(names) * part
    shape = ((count + 1) * XPITCH + 7, LANES)
    return pl.pallas_call(
        functools.partial(early_kernel, cap, names, late, per_chip),
        in_specs=[VMEM] * (1 + len(arrays)),
        out_specs=[VMEM] * 3,
        out_shape=[
            jax.ShapeDtypeStruct(shape, F32),
            jax.ShapeDtypeStruct((len(late) * PACK, PACK // (2 * cap) * LANES), BF),
            jax.ShapeDtypeStruct((16, PACK), BF),
        ],
        compiler_params=params(*staging(arrays, names)),
        name="place_early",
    )(src_ids, *arrays)


def cross_kernel(inputs, hots, *refs):
    place_ref, recv, cos_ref, sin_ref, count_ref, xs_early, top_recv, top_early = refs[:8]
    xrefs, refs = refs[8 : 8 + inputs], refs[8 + inputs :]
    (hot, *narrow), refs = refs[:hots], refs[hots:]
    outs, refs = refs[:2], refs[2:]
    xs, cross, sums, whole = refs
    count, _, chans2 = recv.shape
    slots, bins, _ = hot.shape
    place_sources(place_ref[...], xrefs, xs)
    top_src = functools.reduce(jnp.maximum, [top_early[...]] + [largest(x[...]) for x in xrefs]).astype(F32)
    products = 2 * xrefs[0].shape[0] * place_ref.shape[1] // LANES
    bound = jnp.max(top_src, axis=(0, 1), keepdims=True) * jnp.max(top_recv[...].astype(F32), axis=(0, 1), keepdims=True)
    bound = jnp.maximum(bound * products, 1e-30) * (1.0 / 256)
    scale, unscale = F8_TOP / bound, bound * (1.0 / F8_TOP)
    imag = iota((2 * WROWS, LANES), 1) >= slots
    quarter = shift(iota((1, 4 * 4 * WROWS), 1), 4 * WROWS)
    masks = [jnp.where(quarter == i, 1.0, 0.0).astype(BF) for i in range(4)]

    def one_group(step, carry):
        for sub in range(2 * min(GROUPS, count // 8)):
            g, q = step * min(GROUPS, count // 8) + sub // 2, sub % 2
            lefts = []
            for j in range(4 * q, 4 * q + 4):
                at = pl.ds((g * 8 + j) * XPITCH, 2 * WROWS)
                x = (xs_early[at, :] + xs[at, :]).astype(BF)
                upper = jnp.where(imag, -x, x)
                if j:
                    upper = pltpu.roll(upper, j, 1)
                lefts += [upper, pltpu.roll(x, slots + j, 1)]
            left = jnp.transpose(jnp.concatenate(lefts, axis=0))
            left = jnp.concatenate([left * mask for mask in masks], axis=0)
            right = recv[pl.ds(g * 8 + 4 * q, 4)].reshape(4 * 4 * WROWS, chans2)
            got = jnp.dot(left, right, preferred_element_type=F32)
            for i in range(4):
                j = 4 * q + i
                base = pl.multiple_of(g * (8 * PITCH) + j * (PITCH - 1), 8)
                for h in range(2):
                    side = got[i * LANES : (i + 1) * LANES, h * LANES : (h + 1) * LANES]
                    cross[h, pl.ds(base, LANES), :] = side
                    if j:
                        cross[h, pl.ds(pl.multiple_of(base + LANES, 8), 8), :] = side[:8]
        return carry

    lax.fori_loop(0, count // (8 * min(GROUPS, count // 8)), one_group, 0)

    sums[...] = jnp.zeros_like(sums)

    def one_turn(step, carry):
        lefts, lows = [], []
        for u in range(TURN):
            s = step * TURN + u
            parts = []
            for turn in range(2):
                at = pl.ds(s + turn * slots, count, stride=PITCH)
                parts.append(jnp.concatenate([cross[0, at, :], cross[1, at, :]], axis=1))
            x = jnp.concatenate(parts, axis=0)
            high = x.astype(BF)
            low = x - high.astype(F32)
            if narrow:
                lefts.append(high)
                lows.append((low * scale).astype(F8))
            else:
                lefts.append(jnp.concatenate([high, low.astype(BF)], axis=0))
        left = jnp.concatenate(lefts, axis=1)
        right = jnp.concatenate([hot[step * TURN + u] for u in range(TURN)], axis=1)
        at = pl.ds(0, left.shape[0])
        sums[at, :] += lax.dot_general(left, right, (((1,), (1,)), ((), ())), preferred_element_type=F32)
        for hot8 in narrow:
            left = jnp.concatenate(lows, axis=1)
            right = jnp.concatenate([hot8[step * TURN + u] for u in range(TURN)], axis=1)
            at = pl.ds(2 * count, 2 * count)
            sums[at, :] += lax.dot_general(left, right, (((1,), (1,)), ((), ())), preferred_element_type=F32)
        return carry

    lax.fori_loop(0, slots // TURN, one_turn, 0)
    low = sums[pl.ds(2 * count, 2 * count), :]
    total = sums[pl.ds(0, 2 * count), :] + (low * unscale if narrow else low)
    table = jnp.concatenate([cos_ref[...], sin_ref[...]], axis=0)
    whole[...] = lax.dot_general(total, table, (((0,), (0,)), ((), ())), precision=lax.Precision.HIGHEST, preferred_element_type=F32)
    core = lax.axis_index("chan") & 1
    blocks = outs[0].shape[0]
    per = bins // (2 * blocks)
    crows = count_ref.shape[0]
    for which, dest in ((core, outs[0]), (1 - core, outs[1])):
        for d in range(blocks):
            start = pl.multiple_of((which * blocks + d) * per, per)
            dest[d, pl.ds(0, per), :] = whole[pl.ds(start, per), :]
            dest[d, pl.ds(per, crows), :] = count_ref[...]


def staging(arrays, names):
    groups, part, _ = arrays[0].shape
    chips = len(names)
    return [((groups * part, 4 * PACK), F32), ((groups * part, chips * PACK), BF), ((chips * PACK, 4 * PACK), F32)]


def cross_and_bin(arrays, names, xs_early, place, recv, hots, counts, tops, cos, sin, nchan):
    hot = hots[0]
    _, bins, chans2 = hot.shape
    lags = cos.shape[1]
    count = recv.shape[0]
    per = bins // nchan
    out = jax.ShapeDtypeStruct((nchan // 2, per + 8, lags), F32)
    scratch = [
        (xs_early.shape, F32),
        ((2, (count + 1) * PITCH, chans2 // 2), F32),
        ((4 * count, bins), F32),
        ((bins, lags), F32),
    ]
    buffers = scratch + staging(arrays, names)
    return pl.pallas_call(
        functools.partial(cross_kernel, len(arrays), len(hots)),
        in_specs=[VMEM] * (8 + len(arrays) + len(hots)),
        out_specs=[VMEM, VMEM],
        out_shape=[out, out],
        scratch_shapes=[pltpu.VMEM(shape, kind) for shape, kind in scratch],
        compiler_params=params(*buffers, *([(hot.shape, BF)] if hot.size > BIG else [])),
        name="cross_and_bin",
    )(place, recv, cos, sin, counts, xs_early, *tops, *arrays, *hots)


def swap(x, size, bit):
    return lax.ppermute(x, "chan", [(i, i ^ bit) for i in range(size)])


def gathered(nchan, pieces, chip):
    rest = [1 << k for k in range(1, nchan.bit_length() - 1)]
    result = []
    held = [[x] for x in chip]
    names = [[0] for _ in chip]
    for hop in range(len(rest)):
        bits = [rest[hop] if p % 2 == 0 else rest[-1 - hop] for p in range(pieces)]
        early = [swap(chip[p], nchan, bits[p]) for p in range(pieces)]
        for p, bit in enumerate(bits):
            held[p] = held[p] + [early[p]] + [swap(x, nchan, bit) for x in held[p][1:]]
            names[p] = names[p] + [name ^ bit for name in names[p]]
    for p in range(pieces):
        result.append([held[p][names[p].index(2 * d)] for d in range(len(held[p]))])
    return result


def chip_sources(nchan, cap, pieces, spectra, src_ids):
    keep, send = pick(spectra, src_ids, cap)
    got = swap(send, nchan, 1)
    part = keep.shape[1] // pieces
    return [keep[:, p * part : (p + 1) * part] + got[:, p * part : (p + 1) * part] for p in range(pieces)]


def finish(nchan, nfreq, cap, chip, table, spectra, src_ids, pairs_own, got_pairs, slot_of_bin):
    _, windows, freqs, chans = spectra.shape
    half = freqs // 2
    bins = slot_of_bin.shape[0]
    me = lax.axis_index("chan")
    core = me & 1
    rest = [1 << k for k in range(1, nchan.bit_length() - 1)]
    arrays = gathered(nchan, len(chip), chip)
    spectra_sent, chip = lax.optimization_barrier((spectra, chip))
    got_spec = swap(spectra_sent, nchan, 1)
    chips = len(arrays[0])
    early, late = list(range(chips - chips // 4)), list(range(chips - chips // 4, chips))
    first = [held[d] for held in arrays for d in early]
    recv, *hots, counts, top_recv = tables(spectra, got_spec, pairs_own, got_pairs, slot_of_bin, nchan)
    counts, first = lax.optimization_barrier((counts, first))
    xs_early, place, top_early = place_early(first, early, late, src_ids, cap, 2 * chans)
    counts = counts[0].reshape(bins // NLAG, NLAG)
    last = [held[d] for held in arrays for d in late]
    out = cross_and_bin(last, late, xs_early, place, recv, hots, counts, (top_recv, top_early), *table, nchan)
    mine, other = out

    per = bins // nchan
    mine = mine + swap(other, nchan, 1)
    at = me // 2
    if nchan // 2 <= 4:
        total = lax.dynamic_index_in_dim(mine, at, 0, keepdims=False)
        for move in range(nchan // 2 - 1, 0, -1):
            total = total + swap(lax.dynamic_index_in_dim(mine, at ^ move, 0, keepdims=False), nchan, 2 * move)
    else:
        for bit in rest[::-1]:
            size = mine.shape[0] // 2
            up = (me & bit) != 0
            low, high = mine[:size], mine[size:]
            mine = jnp.where(up, high, low) + swap(jnp.where(up, low, high), nchan, bit)
        total = mine[0]
    owned = total[:per]
    parts = [owned]
    if nfreq <= 4:
        parts += [lax.ppermute(owned, "freq", [(i, i ^ k) for i in range(nfreq)]) for k in range(nfreq - 1, 0, -1)]
    else:
        for k in range(nfreq.bit_length() - 1):
            owned = parts[0]
            parts = [owned + lax.ppermute(owned, "freq", [(i, i ^ (1 << k)) for i in range(nfreq)])]
    counted = total[per : per + bins // NLAG].reshape(bins)
    count = lax.dynamic_slice(counted, ((core * (nchan // 2) + at) * per,), (per,))
    return parts, count


def scaled(parts, count):
    total = parts[0]
    for part in parts[1:]:
        total = total + part
    return total / jnp.sqrt(jnp.maximum(count, 1.0))[:, None]


def body(nchan, nfreq, spectra, src_ids, pair_bin, slot_of_bin):
    chans = spectra.shape[3]
    slots = src_ids.shape[0] * src_ids.shape[1]
    pieces = 2
    pairs_own = pair_bin.reshape(slots, chans)
    got_pairs = swap(pairs_own, nchan, 1)
    windows, half = spectra.shape[1], spectra.shape[2] // 2
    anchor = (lax.axis_index("freq") * 2 + (lax.axis_index("chan") & 1)) * half
    table = lag_basis(anchor, half, F, NLAG, windows)
    chip = chip_sources(nchan, CAP, pieces, spectra, src_ids)
    chip, table, got_pairs = lax.optimization_barrier((chip, table, got_pairs))
    owner = src_ids // (2 * chans)
    loads = jnp.sum((owner[None] == lax.iota(I32, nchan // 2)[:, None, None]).astype(I32), axis=(1, 2))
    fits = jnp.max(loads) <= CAP

    def small(parts, count, *args):
        return scaled(parts, count)

    def large(parts, count, *args):
        chip = chip_sources(nchan, slots, pieces, *args[1:3])
        return scaled(*finish(nchan, nfreq, slots, chip, *args))

    args = (table, spectra, src_ids, pairs_own, got_pairs, slot_of_bin)
    parts, count = finish(nchan, nfreq, CAP, chip, *args)
    return lax.cond(fits, small, large, parts, count, *args)


def solution(mesh):
    return jax.shard_map(
        functools.partial(body, mesh.shape["chan"], mesh.shape["freq"]),
        mesh=mesh,
        in_specs=(P(None, None, "freq", "chan"), P(), P(None, None, "chan"), P()),
        out_specs=P("chan", None),
        check_vma=False,
    )
```
